256 devices in a mesh: dp: 4 (over x), seq: 64 (over z, y, core).
Axes of the slice: x: 4, y: 4, z: 8, core: 2. Of those that a mesh axis runs over, the one named last changes fastest.
Arguments:
- queries: bfloat16 [32768, 4096], P('seq', 'dp'), may hold values from -6 to 6
- keys: bfloat16 [32768, 4096], P('seq', 'dp'), may hold values from -6 to 6
- values: bfloat16 [32768, 4096], P('seq', 'dp'), may hold values from -6 to 6
- out_grad: bfloat16 [32768, 4096], P('seq', 'dp'), may hold values from -16 to 16
- gain: float32 [4096], P('dp'), may hold values from 0.5 to 1.5
- decay_index: int32 [32], P('dp'), may hold values from 0 to 15
- bounds: int32 [3], replicated, may hold values from 7168 to 25600, as said below
Outputs:
- query_grad: bfloat16 [32768, 4096], P('seq', 'dp')
- key_grad: bfloat16 [32768, 4096], P('seq', 'dp')
- value_grad: bfloat16 [32768, 4096], P('seq', 'dp')
- gain_grad: float32 [4096], P(('dp', 'seq'))
The draws below stay inside these ranges and needn't reach their ends.
Inputs may be any that keep to these rules, and one draw needn't show every extreme that they name: `bounds`: the 3 positions rise strictly and lie inside the stream; token p starts a new episode when p is one of them.
All inputs are finite; a program needn't handle non-finite values.
Results may differ from the reference program's by a relative error of at most 0.0063.
Values sent between devices are 32-bit elements; how exact they have to be, the bound alone decides.
No kernel may reach another device: no remote copies, remote signals or barrier semaphores. Data moves between devices by JAX's collectives and lax.ppermute only.
A program may use at most 128 MiB of HBM per device.

```python
import jax
import jax.numpy as jnp
from jax import lax

HEADS = 32
HEAD = 128
TOK_DEV = 512
BOUNDS = 3
HD = 4096
SEQ = 32768
N_SEQ = 64


def draw_bounds(key, part):
    spacing = SEQ // (BOUNDS + 1)
    jitter = spacing // 8
    offsets = jax.random.randint(key, (BOUNDS,), -jitter, jitter + 1)
    anchors = (jnp.arange(BOUNDS, dtype=jnp.int32) + 1) * spacing
    return (anchors + offsets).astype(jnp.int32)


def plant(result, rng, least, largest):
    longest = result.shape.index(max(result.shape))
    spots = []
    for shift in (0, 1):
        where = [jax.random.randint(jax.random.fold_in(rng, axis), (), 0, length) for axis, length in enumerate(result.shape)]
        where[longest] = (where[longest] + shift) % result.shape[longest]
        spots.append(tuple(where))
    return result.at[spots[0]].set(least).at[spots[1]].set(largest)


def strengthened(array, rng, source, target, parts, factor):
    owner, partner = [(jnp.arange(array.shape[dim]) // (array.shape[dim] // parts)).reshape([-1 if axis == dim else 1 for axis in range(array.ndim)]) for dim in (source, target)]
    chosen = jax.random.permutation(rng, parts)[partner]
    strong = (owner == chosen) | (owner == (partner + parts // 2) % parts)
    return jnp.where(strong, factor * array, array)


def level_of(own_key, dims, pieces, smallest, top_value):
    factor_of, own = 1.0, jax.random.fold_in(own_key, 6)
    for position, shards_of in pieces:
        heights = jnp.exp(jax.random.uniform(jax.random.fold_in(own, position), (shards_of,), jnp.float32, smallest / len(pieces), top_value / len(pieces)))
        factor_of = factor_of * jnp.repeat(heights, dims[position] // shards_of).reshape([-1 if axis == position else 1 for axis in range(len(dims))])
    return factor_of


def bell_draw(key, dims, deviation, limit, cuts=(), kind=jnp.bfloat16):
    drawn = jax.random.normal(key, dims, jnp.float32) * deviation
    if len(cuts) > 0:
        drawn = level_of(key, dims, cuts, -0.22, 0.18) * drawn
    return jnp.clip(drawn, min=-limit, max=limit).astype(kind)


def gaussian_with(rng, dims, scale, most, pieces, heavy, kind=jnp.bfloat16):
    entries = scale * jax.random.normal(rng, dims, jnp.float32)
    if pieces:
        entries = entries * level_of(rng, dims, pieces, -0.22, 0.18)
    return jnp.clip(strengthened(entries, jax.random.fold_in(rng, 3), *heavy), -most, most).astype(kind)


def setup_inputs(seed: int = 0) -> dict:
    streams_of = jax.random.split(jax.random.key(seed), 8)
    queries = bell_draw(streams_of[0], (SEQ, HD), 1.0, 6.0, ((0, 64), (1, 4)))
    keys = bell_draw(streams_of[1], (SEQ, HD), 1.0, 6.0, ((0, 64), (1, 4)))
    values = bell_draw(streams_of[2], (SEQ, HD), 1.0, 6.0, ((0, 64), (1, 4)))
    out_grad = gaussian_with(streams_of[3], (SEQ, HD), 1.0, 16.0, ((0, 64), (1, 4)), (0, 1, 64, 4.0))
    gain = jnp.clip(1.0 + 0.1 * jax.random.normal(streams_of[4], (HD,), jnp.float32), 0.5, 1.5)
    decay_index = plant(jax.random.randint(streams_of[5], (HEADS,), 0, 16), jax.random.fold_in(streams_of[5], 1), 0, 15).astype(jnp.int32)
    bounds = draw_bounds(jax.random.fold_in(streams_of[7], 71), 0)
    return dict(queries=queries, keys=keys, values=values, out_grad=out_grad, gain=gain, decay_index=decay_index, bounds=bounds)


HIGHEST_PRECISION = lax.Precision.HIGHEST

def decay_rates(decay_index, stream_length):
    level = decay_index.astype(jnp.float32)
    slow_rate = -0.25 * jnp.exp(level / 7.0 * jnp.log(8.0)) / stream_length
    lowest = jnp.log(4.0 / stream_length)
    fast_rate = -jnp.exp(lowest + (level - 8.0) / 7.0 * (jnp.log(1.0 / 32.0) - lowest))
    return jnp.where(decay_index < 8, slow_rate, fast_rate)

def lowered(values_in):
    return lax.optimization_barrier(values_in.astype(jnp.bfloat16)).astype(jnp.float32)

def shard_masks(rates, bound_row, first_row, tok_rows):
    places = first_row + jnp.arange(tok_rows, dtype=jnp.int32)
    episode = lax.optimization_barrier(jnp.sum((bound_row[None, :] <= places[:, None]).astype(jnp.int32), axis=1))
    before = jnp.sum((bound_row <= first_row - 1).astype(jnp.int32))
    enter_mask = (episode == before).astype(jnp.float32)
    leave_mask = (episode == episode[tok_rows - 1]).astype(jnp.float32)
    whole_mask = (episode[tok_rows - 1] == before).astype(jnp.float32)
    local_pos = jnp.arange(tok_rows, dtype=jnp.float32)
    enter_decay = jnp.exp(rates[None, :] * (local_pos[:, None] + 1.0)) * enter_mask[:, None]
    leave_decay = jnp.exp(rates[None, :] * (tok_rows - 1.0 - local_pos[:, None])) * leave_mask[:, None]
    passing_decay = jnp.exp(rates * tok_rows) * whole_mask
    spacing = local_pos[:, None] - local_pos[None, :]
    allowed = (spacing >= 0.0) & (episode[:, None] == episode[None, :])
    weights = jnp.where(allowed[None], jnp.exp(rates[:, None, None] * jnp.maximum(spacing, 0.0)[None]), 0.0)
    return (enter_decay, leave_decay, passing_decay, weights)

def block_grads(query_rows, key_rows, value_rows, grad_rows, gain, masks, state_in, state_grad_end):
    enter_decay, leave_decay, passing_decay, weights = masks
    tok_rows = query_rows.shape[0]
    query_wide = query_rows.astype(jnp.float32)
    key_wide = key_rows.astype(jnp.float32)
    value_wide = value_rows.astype(jnp.float32)
    state_low = lowered(state_in)
    state_grad_low = lowered(state_grad_end)
    scores = jnp.einsum('the,she->hts', query_wide, key_wide, precision=HIGHEST_PRECISION)
    mixing = (scores * weights).astype(jnp.bfloat16)
    attended = jnp.einsum('hts,shf->thf', mixing.astype(jnp.float32), value_wide, precision=HIGHEST_PRECISION)
    attended = attended + enter_decay[:, :, None] * jnp.einsum('the,hef->thf', query_wide, state_low, precision=HIGHEST_PRECISION)
    flat = attended.reshape(tok_rows, -1)
    inverse_rms = lax.rsqrt(lax.optimization_barrier(jnp.mean(flat * flat, axis=1, keepdims=True)) + 1e-06)
    normed = flat * inverse_rms
    grad_wide_in = grad_rows.astype(jnp.float32)
    gained = grad_wide_in * gain[None, :]
    grad_flat = inverse_rms * (gained - normed * lax.optimization_barrier(jnp.mean(gained * normed, axis=1, keepdims=True)))
    grad_mixed = grad_flat.astype(jnp.bfloat16).reshape(query_rows.shape)
    grad_wide = grad_mixed.astype(jnp.float32)
    gain_term = lax.optimization_barrier(jnp.sum(grad_wide_in * normed, axis=0))
    decayed_queries = lowered(enter_decay[:, :, None] * query_wide)
    state_grad_local = jnp.einsum('the,thf->hef', decayed_queries, grad_wide, precision=HIGHEST_PRECISION)
    grad_scores = jnp.einsum('thf,shf->hts', grad_wide, value_wide, precision=HIGHEST_PRECISION)
    grad_mixing = lowered(grad_scores * weights)
    query_grad = jnp.einsum('hts,she->the', grad_mixing, key_wide, precision=HIGHEST_PRECISION)
    query_grad = query_grad + enter_decay[:, :, None] * jnp.einsum('thf,hef->the', grad_wide, state_low, precision=HIGHEST_PRECISION)
    key_grad = jnp.einsum('hts,the->she', grad_mixing, query_wide, precision=HIGHEST_PRECISION)
    key_grad = key_grad + leave_decay[:, :, None] * jnp.einsum('thf,hef->the', value_wide, state_grad_low, precision=HIGHEST_PRECISION)
    value_grad = jnp.einsum('hts,thf->shf', mixing.astype(jnp.float32), grad_wide, precision=HIGHEST_PRECISION)
    value_grad = value_grad + leave_decay[:, :, None] * jnp.einsum('the,hef->thf', key_wide, state_grad_low, precision=HIGHEST_PRECISION)
    return (query_grad, key_grad, value_grad, gain_term, state_grad_local)

def reference(queries, keys, values, out_grad, gain, decay_index, bounds):
    rates = decay_rates(decay_index, float(SEQ))
    starts = jnp.arange(N_SEQ, dtype=jnp.int32) * TOK_DEV
    shape_four = (N_SEQ, TOK_DEV, HEADS, HEAD)
    query_all = queries.reshape(shape_four)
    key_all = keys.reshape(shape_four)
    value_all = values.reshape(shape_four)
    grad_all = out_grad.reshape(N_SEQ, TOK_DEV, HD)
    zero_state = jnp.zeros((HEADS, HEAD, HEAD), jnp.float32)

    def forward(state_in, block):
        key_rows, value_rows, first_row = block
        masks = shard_masks(rates, bounds, first_row, TOK_DEV)
        decayed_keys = lowered(masks[1][:, :, None] * key_rows.astype(jnp.float32))
        state_local = jnp.einsum('the,thf->hef', decayed_keys, value_rows.astype(jnp.float32), precision=HIGHEST_PRECISION)
        return (masks[2][:, None, None] * state_in + state_local, state_in)
    unused, states_in = lax.scan(forward, zero_state, (key_all, value_all, starts))

    def backward(state_grad_end, block):
        query_rows, key_rows, value_rows, grad_rows, first_row, state_in = block
        masks = shard_masks(rates, bounds, first_row, TOK_DEV)
        query_grad, key_grad, value_grad, gain_term, state_grad_local = block_grads(query_rows, key_rows, value_rows, grad_rows, gain, masks, state_in, state_grad_end)
        carried = state_grad_local + masks[2][:, None, None] * state_grad_end
        return (carried, (query_grad.astype(jnp.bfloat16), key_grad.astype(jnp.bfloat16), value_grad.astype(jnp.bfloat16), gain_term))
    unused_end, outputs = lax.scan(backward, zero_state, (query_all, key_all, value_all, grad_all, starts, states_in), reverse=True)
    query_grad, key_grad, value_grad, gain_terms = outputs
    return (query_grad.reshape(SEQ, HD), key_grad.reshape(SEQ, HD), value_grad.reshape(SEQ, HD), lax.optimization_barrier(jnp.sum(gain_terms, axis=0)))
```

```python
import functools
import math

import jax
import jax.numpy as jnp
from jax import lax
from jax.experimental import pallas as pl
from jax.experimental.pallas import tpu as pltpu
from jax.sharding import PartitionSpec as P

F32, BF16 = jnp.float32, jnp.bfloat16
HEAD, TOK, HEADS_DEV, STREAM, FEATURES = 128, 512, 8, 32768, 4096
BLOCK_Z, BLOCK_Y = 8 * TOK, 2 * TOK
SMEM = pl.BlockSpec(memory_space=pltpu.SMEM)
VMEM = pl.BlockSpec(memory_space=pltpu.VMEM)


def rate_of(level):
    row = jnp.full((1, HEAD), level.astype(F32), F32)
    slow = jnp.exp(row * (math.log(8.0) / 7.0)) * (-0.25 / STREAM)
    lowest = math.log(4.0 / STREAM)
    fast = -jnp.exp(lowest + (row - 8.0) * ((math.log(1.0 / 32.0) - lowest) / 7.0))
    return jnp.where(row < 8.0, slow, fast)


def starts_before(bounds, place):
    return sum((bounds[i] < place).astype(jnp.int32) for i in range(3))


def carry(rate, bounds, left, right):
    same = (starts_before(bounds, left) == starts_before(bounds, right)) & (left <= right)
    span = jnp.maximum(right - left, 0).astype(F32)
    return jnp.exp(rate * span) * jnp.where(same, 1.0, 0.0).astype(F32)


def place():
    at = lax.axis_index("seq")
    return at, at // 8, (at // 2) % 4, at % 2


def tokens_in(bounds, at):
    first = at * TOK
    entering, leaving = TOK, 0
    for i in range(3):
        local = bounds[i] - first
        entering = jnp.where((local >= 0) & (local < entering), local, entering)
        leaving = jnp.where((local < TOK) & (local > leaving), local, leaving)
    return entering, leaving


def enter_decay(rate, entering):
    t = lax.broadcasted_iota(jnp.int32, (TOK, HEAD), 0)
    return jnp.where(t < entering, jnp.exp(rate * (t + 1).astype(F32)), 0.0)


def leave_decay(rate, leaving):
    t = lax.broadcasted_iota(jnp.int32, (TOK, HEAD), 0)
    return jnp.where(t >= leaving, jnp.exp(rate * (TOK - 1 - t).astype(F32)), 0.0)


def pair_weights(rate, bounds, at, rows, columns, flip):
    shape = (rows[1] - rows[0], columns[1] - columns[0])
    r = lax.broadcasted_iota(jnp.int32, shape, 0) + rows[0]
    c = lax.broadcasted_iota(jnp.int32, shape, 1) + columns[0]
    gap = c - r if flip else r - c
    rcol = lax.broadcasted_iota(jnp.int32, (shape[0], 1), 0) + rows[0]
    crow = lax.broadcasted_iota(jnp.int32, (1, shape[1]), 1) + columns[0]
    first = at * TOK
    er = sum((bounds[i] - first <= rcol).astype(jnp.int32) for i in range(3))
    ec = sum((bounds[i] - first <= crow).astype(jnp.int32) for i in range(3))
    weights = jnp.exp(rate[0, 0] * jnp.maximum(gap, 0).astype(F32))
    return jnp.where((gap >= 0) & (er == ec), weights, 0.0)


def mm(a, b):
    return lax.dot_general(a, b, (((1,), (0,)), ((), ())), preferred_element_type=F32)


def mm_bt(a, b):
    return lax.dot_general(a, b, (((1,), (1,)), ((), ())), preferred_element_type=F32)


def mm_at(a, b):
    return lax.dot_general(a, b, (((0,), (0,)), ((), ())), preferred_element_type=F32)


def call(kernel, outs, grid=None, in_specs=None, out_specs=None, scratch=(), flops=0, moved=0, limit=24):
    extra = {} if grid is None else {"grid": grid}
    return pl.pallas_call(
        kernel,
        out_shape=outs,
        in_specs=in_specs,
        out_specs=out_specs,
        scratch_shapes=list(scratch),
        compiler_params=pltpu.CompilerParams(vmem_limit_bytes=limit << 20),
        cost_estimate=pl.CostEstimate(flops=flops, bytes_accessed=moved, transcendentals=0),
        **extra,
    )


def shape(*dims, dtype=F32):
    return jax.ShapeDtypeStruct(dims, dtype)


def store_states(keep_ref, send_ref, low, high, i):
    _, _, y, c = place()
    spot = pl.ds(pl.multiple_of((i ^ y) * HEAD, HEAD), HEAD)
    keep_ref[spot, :] = jnp.where(c == 0, low, high)
    send_ref[spot, :] = jnp.where(c == 0, high, low)


def local_states_kernel(decay, bounds, k0, k1, v0, v1, keep_ref, send_ref):
    i = pl.program_id(0)
    at = place()[0]
    _, leaving = tokens_in(bounds, at)

    def state(head, k, v):
        weights = leave_decay(rate_of(decay[head]), leaving)
        return mm_at((weights * k[...].astype(F32)).astype(BF16), v[...])

    store_states(keep_ref, send_ref, state(i, k0, v0), state(i + 4, k1, v1), i)


def intra_kernel(decay, bounds, q, k, v, out_ref):
    i = pl.program_id(0)
    at = place()[0]
    rate = rate_of(decay[i])
    half = TOK // 2
    for lo in (0, half):
        rows, columns = (lo, lo + half), (0, lo + half)
        scores = mm_bt(q[lo : lo + half, :], k[0 : lo + half, :])
        mixing = (scores * pair_weights(rate, bounds, at, rows, columns, False)).astype(BF16)
        out_ref[lo : lo + half, :] = mm(mixing, v[0 : lo + half, :])


def chip_kernel(decay, bounds, keep, got, *outs, reverse, gains):
    at, z, y, c = place()
    middle = (at - c + 1) * TOK
    for k in range(4):
        rate = rate_of(decay[4 * c + (y ^ k)])
        if reverse:
            far = carry(rate, bounds, middle - TOK, middle)
            own, other = jnp.where(c == 1, far, 1.0), jnp.where(c == 1, 1.0, far)
        else:
            far = carry(rate, bounds, middle, middle + TOK)
            own, other = jnp.where(c == 0, far, 1.0), jnp.where(c == 0, 1.0, far)
        rows = slice(k * HEAD, (k + 1) * HEAD)
        outs[k][0:HEAD, :] = own * keep[rows, :] + other * got[rows, :]
        if gains:
            tail = slice(4 * HEAD, 4 * HEAD + 8)
            outs[k][HEAD : HEAD + 8, :] = keep[tail, :] + got[tail, :]


def row_kernel(decay, bounds, t0, t1, t2, t3, out, *, reverse, gains):
    at, z, y, c = place()
    rate = rate_of(decay[4 * c + y])
    total = 0.0
    for k, t in enumerate((t0, t1, t2, t3)):
        edge = z * BLOCK_Z + (y ^ k) * BLOCK_Y
        if reverse:
            weight = carry(rate, bounds, z * BLOCK_Z, edge)
        else:
            weight = carry(rate, bounds, edge + BLOCK_Y, (z + 1) * BLOCK_Z)
        total += weight * t[0:HEAD, :]
    out[0:HEAD, :] = total
    if gains:
        tail = slice(HEAD, HEAD + 8)
        out[tail, :] = t0[tail, :] + t1[tail, :] + t2[tail, :] + t3[tail, :]


def half_kernel(decay, bounds, r0, r1, r2, r3, out, *, reverse, gains):
    at, z, y, c = place()
    rate = rate_of(decay[4 * c + y])
    total = 0.0
    for k, r in enumerate((r0, r1, r2, r3)):
        edge = (z ^ k) * BLOCK_Z
        if reverse:
            weight = carry(rate, bounds, 4 * BLOCK_Z, edge)
        else:
            weight = carry(rate, bounds, edge + BLOCK_Z, 4 * BLOCK_Z)
        total += weight * r[0:HEAD, :]
    out[0:HEAD, :] = total
    if gains:
        tail = slice(HEAD, HEAD + 8)
        out[tail, :] = r0[tail, :] + r1[tail, :] + r2[tail, :] + r3[tail, :]


def chips_in_kernel(decay, bounds, r0, r1, r2, r3, far, sent, t0, t1, t2, t3, *outs, reverse, gains):
    at, z, y, c = place()
    rate = rate_of(decay[4 * c + y])
    edge = (z + 1) * BLOCK_Z if reverse else z * BLOCK_Z
    if reverse:
        total = carry(rate, bounds, edge, 4 * BLOCK_Z) * far[0:HEAD, :]
    else:
        total = carry(rate, bounds, 4 * BLOCK_Z, edge) * far[0:HEAD, :]
    for k, r in enumerate((r0, r1, r2, r3)):
        if k == 0:
            continue
        other = (z ^ k) * BLOCK_Z
        if reverse:
            weight = carry(rate, bounds, edge, other)
        else:
            weight = carry(rate, bounds, other + BLOCK_Z, edge)
        total += weight * r[0:HEAD, :]
    for k in range(4):
        here = z * BLOCK_Z + (y ^ k) * BLOCK_Y
        if reverse:
            state = carry(rate, bounds, here + BLOCK_Y, edge) * total
        else:
            state = carry(rate, bounds, edge, here) * total
        for m, t in enumerate((t0, t1, t2, t3)):
            if m == k:
                continue
            there = z * BLOCK_Z + (y ^ m) * BLOCK_Y
            if reverse:
                weight = carry(rate, bounds, here + BLOCK_Y, there)
            else:
                weight = carry(rate, bounds, there + BLOCK_Y, here)
            state += weight * t[0:HEAD, :]
        outs[k][...] = state
    if gains:
        tail = slice(HEAD, HEAD + 8)
        outs[4][...] = sent[tail, :] + far[tail, :]


def cores_in_kernel(decay, bounds, v0, v1, v2, v3, keep, got, mine, other, *, reverse):
    at, z, y, c = place()
    middle = (at - c + 1) * TOK
    for k, v in enumerate((v0, v1, v2, v3)):
        rate = rate_of(decay[4 * c + (y ^ k)])
        if reverse:
            step, deep = carry(rate, bounds, middle, middle + TOK), c == 0
        else:
            step, deep = carry(rate, bounds, middle - TOK, middle), c == 1
        rows = slice(k * HEAD, (k + 1) * HEAD)
        state = v[...]
        mine[rows, :] = jnp.where(deep, step * state + got[rows, :], state)
        other[rows, :] = jnp.where(deep, state, step * state + keep[rows, :])


def state_of(mine, other, head):
    _, _, y, c = place()
    spot = pl.ds(pl.multiple_of(((head % 4) ^ y) * HEAD, HEAD), HEAD)
    return jnp.where(head // 4 == c, mine[spot, :], other[spot, :]).astype(BF16)


def attended_kernel(decay, bounds, q, intra, grad, gain, mine, other, out_ref, sums_ref, squares, crosses):
    i = pl.program_id(0)
    at = place()[0]
    entering, _ = tokens_in(bounds, at)
    weights = enter_decay(rate_of(decay[i]), entering)
    out = intra[...] + weights * mm(q[...], state_of(mine, other, i))
    out_ref[...] = out
    gained = grad[...].astype(F32) * gain[pl.ds(i, 1), :]

    @pl.when(i == 0)
    def _():
        squares[...] = out * out
        crosses[...] = out * gained

    @pl.when(i > 0)
    def _():
        squares[...] += out * out
        crosses[...] += out * gained

    @pl.when(i == HEADS_DEV - 1)
    def _():
        sums_ref[0:4, :] = jnp.broadcast_to(jnp.sum(squares[...].T, axis=0, keepdims=True), (4, TOK))
        sums_ref[4:8, :] = jnp.broadcast_to(jnp.sum(crosses[...].T, axis=0, keepdims=True), (4, TOK))


def mixed_kernel(decay, bounds, s0, s1, s2, s3, o0, o1, g0, g1, q0, q1, gain, d0, d1, keep, send, inverse, mean):
    i = pl.program_id(0)
    at = place()[0]
    entering, _ = tokens_in(bounds, at)

    @pl.when(i == 0)
    def _():
        sums = s0[...] + s1[...] + s2[...] + s3[...]
        r = lax.rsqrt(sums[0:1, :] * (1.0 / FEATURES) + 1e-06)
        inverse[...] = jnp.broadcast_to(r, (HEAD, TOK)).T
        mean[...] = jnp.broadcast_to(sums[4:5, :] * r * (1.0 / FEATURES), (HEAD, TOK)).T

    tail = 4 * HEAD

    def state(head, o, g, q, d):
        normed = inverse[...] * o[...]
        wide = g[...].astype(F32)
        low = (inverse[...] * (wide * gain[pl.ds(head, 1), :] - normed * mean[...])).astype(BF16)
        d[...] = low
        term = jnp.sum(wide * normed, axis=0, keepdims=True)
        keep[pl.ds(tail + head, 1), :] = term
        send[pl.ds(tail + head, 1), :] = term
        weights = enter_decay(rate_of(decay[head]), entering)
        return mm_at((weights * q[...].astype(F32)).astype(BF16), low)

    store_states(keep, send, state(i, o0, g0, q0, d0), state(i + 4, o1, g1, q1, d1), i)


def grads_kernel(decay, bounds, q, k, v, d0, d1, mine, other, dq, dk, dv):
    i = pl.program_id(0)
    at = place()[0]
    rate = rate_of(decay[i])
    entering, _ = tokens_in(bounds, at)
    half = TOK // 2
    d = jnp.where(i < 4, d0[...], d1[...])
    state = state_of(mine, other, i)
    weights = enter_decay(rate, entering)
    for lo in (0, half):
        hi = lo + half
        w = pair_weights(rate, bounds, at, (lo, hi), (0, hi), False)
        mixing = (mm_bt(d[lo:hi, :], v[0:hi, :]) * w).astype(BF16)
        grad = mm(mixing, k[0:hi, :]) + weights[lo:hi, :] * mm_bt(d[lo:hi, :], state)
        dq[lo:hi, :] = grad.astype(BF16)
        w = pair_weights(rate, bounds, at, (lo, hi), (lo, TOK), True)
        mixing = (mm_bt(v[lo:hi, :], d[lo:TOK, :]) * w).astype(BF16)
        dk[lo:hi, :] = mm(mixing, q[lo:TOK, :])
        mixing = (mm_bt(k[lo:hi, :], q[lo:TOK, :]) * w).astype(BF16)
        dv[lo:hi, :] = mm(mixing, d[lo:TOK, :])


def last_kernel(decay, bounds, k, v, dk_in, dv_in, mine, other, dk, dv):
    i = pl.program_id(0)
    at = place()[0]
    _, leaving = tokens_in(bounds, at)
    weights = leave_decay(rate_of(decay[i]), leaving)
    state = state_of(mine, other, i)
    dk[...] = (dk_in[...] + weights * mm_bt(v[...], state)).astype(BF16)
    dv[...] = (dv_in[...] + weights * mm(k[...], state)).astype(BF16)


def index(z, y, c):
    return (z * 4 + y) * 2 + c


def exchange(array, dz=0, dy=0, dc=0):
    pairs = [
        (index(z, y, c), index(z ^ dz, y ^ dy, c ^ dc))
        for z in range(8)
        for y in range(4)
        for c in range(2)
    ]
    return lax.ppermute(array, "seq", pairs)


def carried(keep, send, decay, bounds, reverse, gains):
    extra = 8 if gains else 0
    small = shape(HEAD + extra, HEAD)

    def step(kernel, outs, *args, **more):
        return call(
            functools.partial(kernel, reverse=reverse, **more),
            outs,
            in_specs=[SMEM, SMEM] + [VMEM] * len(args),
            out_specs=jax.tree.map(lambda _: VMEM, outs),
            limit=8,
        )(decay, bounds, *args)

    got = exchange(send, dc=1)
    chips = step(chip_kernel, [small] * 4, keep, got, gains=gains)
    chips = [chips[0]] + [exchange(chips[k], dy=k) for k in (1, 2, 3)]
    row = step(row_kernel, small, *chips, gains=gains)
    rows = [row] + [exchange(row, dz=k) for k in (1, 2, 3)]
    sent = step(half_kernel, small, *rows, gains=gains)
    far = exchange(sent, dz=7)
    outs = [shape(HEAD, HEAD)] * 4 + ([shape(8, HEAD)] if gains else [])
    outs = step(chips_in_kernel, outs, *rows, far, sent, *chips, gains=gains)
    states = [outs[0]] + [exchange(outs[k], dy=k) for k in (1, 2, 3)]
    mine, other = step(cores_in_kernel, [shape(4 * HEAD, HEAD)] * 2, *states, keep, got)
    other = exchange(other, dc=1)
    return mine, other, (outs[4] if gains else None)


def shards(queries, keys, values, out_grad, gain, decay, bounds):
    gain = gain.reshape(HEADS_DEV, HEAD)
    low = pl.BlockSpec((TOK, HEAD), lambda i: (0, i))
    high = pl.BlockSpec((TOK, HEAD), lambda i: (0, i + 4))
    either0 = pl.BlockSpec((TOK, HEAD), lambda i: (0, jnp.minimum(i, 3)))
    either1 = pl.BlockSpec((TOK, HEAD), lambda i: (0, jnp.maximum(i - 4, 0)))

    def whole(*dims):
        return pl.BlockSpec(dims, lambda i: (0,) * len(dims))

    states = whole(4 * HEAD, HEAD)
    width = HEADS_DEV * HEAD
    small_mm = 2 * TOK * HEAD * HEAD * HEADS_DEV
    big_mm = 2 * TOK * TOK * HEAD * HEADS_DEV * 3 // 4

    keep, send = call(
        local_states_kernel,
        [shape(4 * HEAD, HEAD)] * 2,
        grid=(4,),
        in_specs=[SMEM, SMEM, low, high, low, high],
        out_specs=[states] * 2,
        flops=small_mm,
        moved=3 << 20,
    )(decay, bounds, keys, keys, values, values)
    intra = call(
        intra_kernel,
        shape(TOK, width),
        grid=(HEADS_DEV,),
        in_specs=[SMEM, SMEM, low, low, low],
        out_specs=low,
        flops=2 * big_mm,
        moved=5 << 20,
    )(decay, bounds, queries, keys, values)
    mine, other, _ = carried(keep, send, decay, bounds, False, False)
    attended, sums = call(
        attended_kernel,
        [shape(TOK, width), shape(8, TOK)],
        grid=(HEADS_DEV,),
        in_specs=[SMEM, SMEM, low, low, low, whole(HEADS_DEV, HEAD), states, states],
        out_specs=[low, whole(8, TOK)],
        scratch=[pltpu.VMEM((TOK, HEAD), F32)] * 2,
        flops=small_mm,
        moved=7 << 20,
    )(decay, bounds, queries, intra, out_grad, gain, mine, other)
    others = [lax.ppermute(sums, "dp", [(i, i ^ k) for i in range(4)]) for k in (1, 2, 3)]
    sums_spec = whole(8, TOK)
    grown = whole(4 * HEAD + 8, HEAD)
    d0, d1, keep, send = call(
        mixed_kernel,
        [shape(TOK, width // 2, dtype=BF16)] * 2 + [shape(4 * HEAD + 8, HEAD)] * 2,
        grid=(4,),
        in_specs=[SMEM, SMEM] + [sums_spec] * 4 + [low, high] * 3 + [whole(HEADS_DEV, HEAD)],
        out_specs=[low, low, grown, grown],
        scratch=[pltpu.VMEM((TOK, HEAD), F32)] * 2,
        flops=small_mm,
        moved=7 << 20,
    )(decay, bounds, sums, *others, attended, attended, out_grad, out_grad, queries, queries, gain)
    dq, dk, dv = call(
        grads_kernel,
        [shape(TOK, width, dtype=BF16), shape(TOK, width), shape(TOK, width)],
        grid=(HEADS_DEV,),
        in_specs=[SMEM, SMEM, low, low, low, either0, either1, states, states],
        out_specs=[low, low, low],
        flops=6 * big_mm,
        moved=9 << 20,
    )(decay, bounds, queries, keys, values, d0, d1, mine, other)
    mine, other, gains = carried(keep, send, decay, bounds, True, True)
    dk, dv = call(
        last_kernel,
        [shape(TOK, width, dtype=BF16)] * 2,
        grid=(HEADS_DEV,),
        in_specs=[SMEM, SMEM, low, low, low, low, states, states],
        out_specs=[low, low],
        flops=2 * small_mm,
        moved=8 << 20,
    )(decay, bounds, keys, values, dk, dv, mine, other)
    part = lax.dynamic_slice(gains.reshape(width), (lax.axis_index("seq") * 16,), (16,))
    return dq, dk, dv, part


def solution(mesh):
    return jax.shard_map(
        shards,
        mesh=mesh,
        in_specs=(
            P("seq", "dp"),
            P("seq", "dp"),
            P("seq", "dp"),
            P("seq", "dp"),
            P("dp"),
            P("dp"),
            P(),
        ),
        out_specs=(P("seq", "dp"), P("seq", "dp"), P("seq", "dp"), P(("dp", "seq"))),
        check_vma=False,
    )
```

```python
import functools
import math

import jax
import jax.numpy as jnp
from jax import lax
from jax.experimental import pallas as pl
from jax.experimental.pallas import tpu as pltpu
from jax.sharding import PartitionSpec as P

F32, BF16 = jnp.float32, jnp.bfloat16
HEAD, TOK, HEADS_DEV, STREAM, FEATURES = 128, 512, 8, 32768, 4096
BLOCK_Z, BLOCK_Y = 8 * TOK, 2 * TOK
SMEM = pl.BlockSpec(memory_space=pltpu.SMEM)
VMEM = pl.BlockSpec(memory_space=pltpu.VMEM)
ANY = pl.BlockSpec(memory_space=pl.ANY)


def rate_of(level):
    row = jnp.full((1, HEAD), level.astype(F32), F32)
    slow = jnp.exp(row * (math.log(8.0) / 7.0)) * (-0.25 / STREAM)
    lowest = math.log(4.0 / STREAM)
    fast = -jnp.exp(lowest + (row - 8.0) * ((math.log(1.0 / 32.0) - lowest) / 7.0))
    return jnp.where(row < 8.0, slow, fast)


def starts_before(bounds, place):
    return sum((bounds[i] < place).astype(jnp.int32) for i in range(3))


def carry(rate, bounds, left, right):
    same = (starts_before(bounds, left) == starts_before(bounds, right)) & (left <= right)
    span = jnp.maximum(right - left, 0).astype(F32)
    return jnp.exp(rate * span) * jnp.where(same, 1.0, 0.0).astype(F32)


def place():
    at = lax.axis_index("seq")
    return at, at // 8, (at // 2) % 4, at % 2


def tokens_in(bounds, at):
    first = at * TOK
    entering, leaving = TOK, 0
    for i in range(3):
        local = bounds[i] - first
        entering = jnp.where((local >= 0) & (local < entering), local, entering)
        leaving = jnp.where((local < TOK) & (local > leaving), local, leaving)
    return entering, leaving


def powers(rate, first, up):
    t = lax.broadcasted_iota(jnp.int32, (8, HEAD), 0)
    t = (t if up else 7 - t).astype(F32)
    rows, size = jnp.exp(rate * (t + first)), 8
    while size < TOK:
        more = rows * jnp.exp(rate * float(size))
        rows = jnp.concatenate([rows, more] if up else [more, rows], axis=0)
        size *= 2
    return rows


def token_rows():
    return lax.broadcasted_iota(jnp.int32, (TOK, HEAD), 0)


def enter_decay(rate, entering):
    return jnp.where(token_rows() < entering, powers(rate, 1.0, True), 0.0)


def leave_decay(rate, leaving):
    return jnp.where(token_rows() >= leaving, powers(rate, 0.0, False), 0.0)


def masks_kernel(decay, bounds, mask, flipped):
    first = place()[0] * TOK
    for lo in range(0, TOK, HEAD):
        row = lax.broadcasted_iota(jnp.int32, (HEAD, TOK), 0) + lo
        column = lax.broadcasted_iota(jnp.int32, (HEAD, TOK), 1)
        since = jnp.zeros((HEAD, TOK), jnp.int32)
        until = jnp.full((HEAD, TOK), TOK, jnp.int32)
        for i in range(3):
            local = bounds[i] - first
            since = jnp.where(row >= local, jnp.maximum(since, local), since)
            until = jnp.where(row < local, jnp.minimum(until, local), until)
        rows = slice(lo, lo + HEAD)
        mask[rows, :] = jnp.where((column <= row) & (column >= since), 1.0, 0.0).astype(BF16)
        flipped[rows, :] = jnp.where((column >= row) & (column < until), 1.0, 0.0).astype(BF16)


def mm(a, b):
    return lax.dot_general(a, b, (((1,), (0,)), ((), ())), preferred_element_type=F32)


def mm_bt(a, b):
    return lax.dot_general(a, b, (((1,), (1,)), ((), ())), preferred_element_type=F32)


def mm_at(a, b):
    return lax.dot_general(a, b, (((0,), (0,)), ((), ())), preferred_element_type=F32)


def call(kernel, outs, grid=None, in_specs=None, out_specs=None, scratch=(), flops=0, moved=0, limit=24, aliases={}):
    extra = {} if grid is None else {"grid": grid}
    return pl.pallas_call(
        kernel,
        out_shape=outs,
        in_specs=in_specs,
        out_specs=out_specs,
        scratch_shapes=list(scratch),
        input_output_aliases=aliases,
        compiler_params=pltpu.CompilerParams(vmem_limit_bytes=limit << 20),
        cost_estimate=pl.CostEstimate(flops=flops, bytes_accessed=moved, transcendentals=0),
        **extra,
    )


def shape(*dims, dtype=F32):
    return jax.ShapeDtypeStruct(dims, dtype)


def store_states(keep_ref, send_ref, low, high, i):
    _, _, y, c = place()
    spot = pl.ds(pl.multiple_of((i ^ y) * HEAD, HEAD), HEAD)
    keep_ref[spot, :] = jnp.where(c == 0, low, high)
    send_ref[spot, :] = jnp.where(c == 0, high, low)


def local_states_kernel(decay, bounds, k0, k1, v0, v1, keep_ref, send_ref):
    i = pl.program_id(0)
    at = place()[0]
    _, leaving = tokens_in(bounds, at)

    def state(head, k, v):
        weights = leave_decay(rate_of(decay[head]), leaving)
        return mm_at((weights * k[...].astype(F32)).astype(BF16), v[...])

    store_states(keep_ref, send_ref, state(i, k0, v0), state(i + 4, k1, v1), i)


def intra_kernel(decay, bounds, q, k, v, mask, after, out_ref, *, start):
    rate = rate_of(decay[pl.program_id(0) + start])
    scaled = (powers(-rate, 0.0, True) * k[...].astype(F32)).astype(BF16)
    down = powers(rate, 0.0, True)
    half = TOK // 2
    for lo in (0, half):
        hi = lo + half
        mixing = mm_bt(q[lo:hi, :], scaled[0:hi, :]).astype(BF16) * mask[lo:hi, 0:hi]
        out_ref[lo:hi, :] = down[lo:hi, :] * mm(mixing, v[0:hi, :])


def chip_kernel(decay, bounds, keep, got, after, *outs, reverse, gains):
    at, z, y, c = place()
    middle = (at - c + 1) * TOK
    for k in range(4):
        rate = rate_of(decay[4 * c + (y ^ k)])
        if reverse:
            far = carry(rate, bounds, middle - TOK, middle)
            own, other = jnp.where(c == 1, far, 1.0), jnp.where(c == 1, 1.0, far)
        else:
            far = carry(rate, bounds, middle, middle + TOK)
            own, other = jnp.where(c == 0, far, 1.0), jnp.where(c == 0, 1.0, far)
        rows = slice(k * HEAD, (k + 1) * HEAD)
        outs[k][0:HEAD, :] = own * keep[rows, :] + other * got[rows, :]
        if gains:
            tail = slice(4 * HEAD, 4 * HEAD + 8)
            outs[k][HEAD : HEAD + 8, :] = keep[tail, :] + got[tail, :]


def row_kernel(decay, bounds, t0, t1, t2, t3, after, out, *, reverse, gains):
    at, z, y, c = place()
    rate = rate_of(decay[4 * c + y])
    total = 0.0
    for k, t in enumerate((t0, t1, t2, t3)):
        edge = z * BLOCK_Z + (y ^ k) * BLOCK_Y
        if reverse:
            weight = carry(rate, bounds, z * BLOCK_Z, edge)
        else:
            weight = carry(rate, bounds, edge + BLOCK_Y, (z + 1) * BLOCK_Z)
        total += weight * t[0:HEAD, :]
    out[0:HEAD, :] = total
    if gains:
        tail = slice(HEAD, HEAD + 8)
        out[tail, :] = t0[tail, :] + t1[tail, :] + t2[tail, :] + t3[tail, :]


def half_kernel(decay, bounds, r0, r1, r2, r3, after, out, *, reverse, gains):
    at, z, y, c = place()
    rate = rate_of(decay[4 * c + y])
    total = 0.0
    for k, r in enumerate((r0, r1, r2, r3)):
        edge = (z ^ k) * BLOCK_Z
        if reverse:
            weight = carry(rate, bounds, 4 * BLOCK_Z, edge)
        else:
            weight = carry(rate, bounds, edge + BLOCK_Z, 4 * BLOCK_Z)
        total += weight * r[0:HEAD, :]
    out[0:HEAD, :] = total
    if gains:
        tail = slice(HEAD, HEAD + 8)
        out[tail, :] = r0[tail, :] + r1[tail, :] + r2[tail, :] + r3[tail, :]


def chips_in_kernel(decay, bounds, r0, r1, r2, r3, far, sent, t0, t1, t2, t3, after, *outs, reverse, gains):
    at, z, y, c = place()
    rate = rate_of(decay[4 * c + y])
    edge = (z + 1) * BLOCK_Z if reverse else z * BLOCK_Z
    if reverse:
        total = carry(rate, bounds, edge, 4 * BLOCK_Z) * far[0:HEAD, :]
    else:
        total = carry(rate, bounds, 4 * BLOCK_Z, edge) * far[0:HEAD, :]
    for k, r in enumerate((r0, r1, r2, r3)):
        if k == 0:
            continue
        other = (z ^ k) * BLOCK_Z
        if reverse:
            weight = carry(rate, bounds, edge, other)
        else:
            weight = carry(rate, bounds, other + BLOCK_Z, edge)
        total += weight * r[0:HEAD, :]
    for k in range(4):
        here = z * BLOCK_Z + (y ^ k) * BLOCK_Y
        if reverse:
            state = carry(rate, bounds, here + BLOCK_Y, edge) * total
        else:
            state = carry(rate, bounds, edge, here) * total
        for m, t in enumerate((t0, t1, t2, t3)):
            if m == k:
                continue
            there = z * BLOCK_Z + (y ^ m) * BLOCK_Y
            if reverse:
                weight = carry(rate, bounds, here + BLOCK_Y, there)
            else:
                weight = carry(rate, bounds, there + BLOCK_Y, here)
            state += weight * t[0:HEAD, :]
        outs[k][...] = state
    if gains:
        tail = slice(HEAD, HEAD + 8)
        outs[4][...] = sent[tail, :] + far[tail, :]
        row = outs[4][pl.ds(z, 1), :]
        turned = pltpu.roll(row, (HEAD - 32 * y - 16 * c) % HEAD, axis=1)
        outs[5][...] = turned[0, 0:16]


def cores_in_kernel(decay, bounds, v0, v1, v2, v3, keep, got, after, mine, other, *, reverse):
    at, z, y, c = place()
    middle = (at - c + 1) * TOK
    for k, v in enumerate((v0, v1, v2, v3)):
        rate = rate_of(decay[4 * c + (y ^ k)])
        if reverse:
            step, deep = carry(rate, bounds, middle, middle + TOK), c == 0
        else:
            step, deep = carry(rate, bounds, middle - TOK, middle), c == 1
        rows = slice(k * HEAD, (k + 1) * HEAD)
        state = v[...]
        mine[rows, :] = jnp.where(deep, step * state + got[rows, :], state)
        other[rows, :] = jnp.where(deep, state, step * state + keep[rows, :])


def state_of(mine, other, head):
    _, _, y, c = place()
    spot = pl.ds(pl.multiple_of(((head % 4) ^ y) * HEAD, HEAD), HEAD)
    return jnp.where(head // 4 == c, mine[spot, :], other[spot, :]).astype(BF16)


def attended_kernel(decay, bounds, q0, q1, i0, i1, g0, g1, gain, mine, other, o0, o1, sums_ref, squares, crosses):
    i = pl.program_id(0)
    entering, _ = tokens_in(bounds, place()[0])

    def out_of(head, q, intra, grad, out_ref):
        weights = enter_decay(rate_of(decay[head]), entering)
        out = intra[...] + weights * mm(q[...], state_of(mine, other, head))
        out_ref[...] = out
        return out * out, out * (grad[...].astype(F32) * gain[pl.ds(head, 1), :])

    square, cross = out_of(i, q0, i0, g0, o0)
    more, also = out_of(i + 4, q1, i1, g1, o1)

    @pl.when(i == 0)
    def _():
        squares[...] = square + more
        crosses[...] = cross + also

    @pl.when(i > 0)
    def _():
        squares[...] += square + more
        crosses[...] += cross + also

    @pl.when(i == 3)
    def _():
        sums_ref[0:4, :] = jnp.broadcast_to(jnp.sum(squares[...].T, axis=0, keepdims=True), (4, TOK))
        sums_ref[4:8, :] = jnp.broadcast_to(jnp.sum(crosses[...].T, axis=0, keepdims=True), (4, TOK))


def mixed_kernel(decay, bounds, s0, s1, s2, s3, o0, o1, g0, g1, q0, q1, gain, d0, d1, keep, send, inverse, mean):
    i = pl.program_id(0)
    at = place()[0]
    entering, _ = tokens_in(bounds, at)

    @pl.when(i == 0)
    def _():
        sums = s0[...] + s1[...] + s2[...] + s3[...]
        r = lax.rsqrt(sums[0:1, :] * (1.0 / FEATURES) + 1e-06)
        inverse[...] = jnp.broadcast_to(r, (HEAD, TOK)).T
        mean[...] = jnp.broadcast_to(sums[4:5, :] * r * (1.0 / FEATURES), (HEAD, TOK)).T

    tail = 4 * HEAD

    def state(head, o, g, q, d):
        normed = inverse[...] * o[...]
        wide = g[...].astype(F32)
        low = (inverse[...] * (wide * gain[pl.ds(head, 1), :] - normed * mean[...])).astype(BF16)
        d[...] = low
        term = jnp.sum(wide * normed, axis=0, keepdims=True)
        keep[pl.ds(tail + head, 1), :] = term
        send[pl.ds(tail + head, 1), :] = term
        weights = enter_decay(rate_of(decay[head]), entering)
        return mm_at((weights * q[...].astype(F32)).astype(BF16), low)

    store_states(keep, send, state(i, o0, g0, q0, d0), state(i + 4, o1, g1, q1, d1), i)


def grads_kernel(decay, bounds, q, k, v, d, mask, flipped, mine, other, after, *refs, start):
    dq, dk, dv = refs[-3:]
    head = pl.program_id(0) + start
    rate = rate_of(decay[head])
    entering, _ = tokens_in(bounds, place()[0])
    half = TOK // 2
    state = state_of(mine, other, head)
    up, down = powers(-rate, 0.0, True), powers(rate, 0.0, True)
    inside = jnp.where(token_rows() < entering, jnp.exp(rate), 0.0)
    v_up = (up * v[...].astype(F32)).astype(BF16)
    d_down = (down * d[...].astype(F32)).astype(BF16)
    q_down = (down * q[...].astype(F32)).astype(BF16)
    for lo in (0, half):
        hi = lo + half
        mixing = mm_bt(d[lo:hi, :], v_up[0:hi, :]).astype(BF16) * mask[lo:hi, 0:hi]
        grad = mm(mixing, k[0:hi, :]) + inside[lo:hi, :] * mm_bt(d[lo:hi, :], state)
        dq[lo:hi, :] = (down[lo:hi, :] * grad).astype(BF16)
        mixing = mm_bt(v[lo:hi, :], d_down[lo:TOK, :]).astype(BF16) * flipped[lo:hi, lo:TOK]
        dk[lo:hi, :] = up[lo:hi, :] * mm(mixing, q[lo:TOK, :])
        mixing = mm_bt(k[lo:hi, :], q_down[lo:TOK, :]).astype(BF16) * flipped[lo:hi, lo:TOK]
        dv[lo:hi, :] = up[lo:hi, :] * mm(mixing, d[lo:TOK, :])


def last_kernel(decay, bounds, k, v, dk_in, dv_in, mine, other, dk, dv):
    i = pl.program_id(0)
    at = place()[0]
    _, leaving = tokens_in(bounds, at)
    weights = leave_decay(rate_of(decay[i]), leaving)
    state = state_of(mine, other, i)
    dk[...] = (dk_in[...] + weights * mm_bt(v[...], state)).astype(BF16)
    dv[...] = (dv_in[...] + weights * mm(k[...], state)).astype(BF16)


def index(z, y, c):
    return (z * 4 + y) * 2 + c


def exchange(array, dz=0, dy=0, dc=0):
    pairs = [
        (index(z, y, c), index(z ^ dz, y ^ dy, c ^ dc))
        for z in range(8)
        for y in range(4)
        for c in range(2)
    ]
    return lax.ppermute(array, "seq", pairs)


def carried(keep, send, decay, bounds, reverse, gains, work):
    extra = 8 if gains else 0
    small = shape(HEAD + extra, HEAD)

    def step(kernel, outs, *args, after, **more):
        return call(
            functools.partial(kernel, reverse=reverse, **more),
            outs,
            in_specs=[SMEM, SMEM] + [VMEM] * len(args) + [ANY],
            out_specs=jax.tree.map(lambda _: VMEM, outs),
            limit=8,
        )(decay, bounds, *args, after)

    got = exchange(send, dc=1)
    done = work[0](keep)
    chips = step(chip_kernel, [small] * 4, keep, got, gains=gains, after=done)
    done = work[1](chips[0])
    chips = [chips[0]] + [exchange(chips[k], dy=k) for k in (1, 2, 3)]
    row = step(row_kernel, small, *chips, gains=gains, after=done)
    done = work[2](row)
    rows = [row] + [exchange(row, dz=k) for k in (1, 2, 3)]
    sent = step(half_kernel, small, *rows, gains=gains, after=done)
    done = work[3](sent)
    far = exchange(sent, dz=7)
    outs = [shape(HEAD, HEAD)] * 4 + ([shape(8, HEAD), shape(16)] if gains else [])
    outs = step(chips_in_kernel, outs, *rows, far, sent, *chips, gains=gains, after=done)
    done = work[4](outs[0])
    states = [outs[0]] + [exchange(outs[k], dy=k) for k in (1, 2, 3)]
    mine, other = step(cores_in_kernel, [shape(4 * HEAD, HEAD)] * 2, *states, keep, got, after=done)
    other = exchange(other, dc=1)
    return mine, other, (outs[5] if gains else None)


def shards(queries, keys, values, out_grad, gain, decay, bounds):
    gain = gain.reshape(HEADS_DEV, HEAD)

    def part(start):
        return pl.BlockSpec((TOK, HEAD), lambda i: (0, i + start))

    low, high = part(0), part(4)

    def whole(*dims):
        return pl.BlockSpec(dims, lambda i: (0,) * len(dims))

    states = whole(4 * HEAD, HEAD)
    width = HEADS_DEV * HEAD
    small_mm = 2 * TOK * HEAD * HEAD * HEADS_DEV
    big_mm = 2 * TOK * TOK * HEAD * HEADS_DEV * 3 // 4

    keep, send = call(
        local_states_kernel,
        [shape(4 * HEAD, HEAD)] * 2,
        grid=(4,),
        in_specs=[SMEM, SMEM, low, high, low, high],
        out_specs=[states] * 2,
        flops=small_mm,
        moved=3 << 20,
    )(*[pltpu.with_memory_space_constraint(x, pltpu.HBM) for x in (decay, bounds, keys, keys, values, values)])

    made = {}
    pairs = shape(TOK, TOK, dtype=BF16)

    def make_masks(after):
        made["masks"] = call(masks_kernel, [pairs] * 2, in_specs=[SMEM, SMEM], out_specs=[VMEM] * 2, moved=1 << 20)(
            decay, bounds
        )
        return made["masks"][0]

    def make_intra(start):
        def run(after):
            made["intra", start] = call(
                functools.partial(intra_kernel, start=start),
                shape(TOK, width // 2),
                grid=(4,),
                in_specs=[SMEM, SMEM] + [part(start)] * 3 + [whole(TOK, TOK), ANY],
                out_specs=low,
                flops=big_mm,
                moved=3 << 20,
            )(decay, bounds, queries, keys, values, made["masks"][0], after)
            return made["intra", start]

        return run

    def same(after):
        return after

    mine, other, _ = carried(
        keep, send, decay, bounds, False, False, [make_masks, make_intra(0), make_intra(4), same, same]
    )
    o0, o1, sums = call(
        attended_kernel,
        [shape(TOK, width // 2)] * 2 + [shape(8, TOK)],
        grid=(4,),
        in_specs=[SMEM, SMEM, low, high, low, low, low, high, whole(HEADS_DEV, HEAD), states, states],
        out_specs=[low, low, whole(8, TOK)],
        scratch=[pltpu.VMEM((TOK, HEAD), F32)] * 2,
        flops=small_mm,
        moved=7 << 20,
    )(
        decay, bounds, queries, queries, made["intra", 0], made["intra", 4], out_grad, out_grad, gain, mine, other
    )
    others = [lax.ppermute(sums, "dp", [(i, i ^ k) for i in range(4)]) for k in (1, 2, 3)]
    sums_spec = whole(8, TOK)
    grown = whole(4 * HEAD + 8, HEAD)
    d0, d1, keep, send = call(
        mixed_kernel,
        [shape(TOK, width // 2, dtype=BF16)] * 2 + [shape(4 * HEAD + 8, HEAD)] * 2,
        grid=(4,),
        in_specs=[SMEM, SMEM] + [sums_spec] * 4 + [low, low, low, high, low, high] + [whole(HEADS_DEV, HEAD)],
        out_specs=[low, low, grown, grown],
        scratch=[pltpu.VMEM((TOK, HEAD), F32)] * 2,
        flops=small_mm,
        moved=7 << 20,
    )(decay, bounds, sums, *others, o0, o1, out_grad, out_grad, queries, queries, gain)

    grads = [shape(TOK, width, dtype=BF16), shape(TOK, width), shape(TOK, width)]
    mask, flipped = made["masks"]

    def make_grads(n):
        start = 2 * n

        def run(after):
            before = made.get("grads", [])
            made["grads"] = call(
                functools.partial(grads_kernel, start=start),
                grads,
                grid=(2,),
                in_specs=[SMEM, SMEM]
                + [part(start)] * 3
                + [part(start % 4)]
                + [whole(TOK, TOK)] * 2
                + [states] * 2
                + [ANY] * (1 + len(before)),
                out_specs=[part(start)] * 3,
                flops=6 * big_mm // 4,
                moved=9 << 18,
                aliases={11 + k: k for k in range(len(before))},
            )(
                decay,
                bounds,
                queries,
                keys,
                values,
                d0 if start < 4 else d1,
                mask,
                flipped,
                mine,
                other,
                after,
                *before,
            )
            return made["grads"][1]

        return run

    last_mine, last_other, gains = carried(
        keep, send, decay, bounds, True, True, [same] + [make_grads(n) for n in range(4)]
    )
    dq, dk, dv = made["grads"]
    dk, dv = call(
        last_kernel,
        [shape(TOK, width, dtype=BF16)] * 2,
        grid=(HEADS_DEV,),
        in_specs=[SMEM, SMEM, low, low, low, low, states, states],
        out_specs=[low, low],
        flops=2 * small_mm,
        moved=8 << 20,
    )(decay, bounds, keys, values, dk, dv, last_mine, last_other)
    return dq, dk, dv, gains


def solution(mesh):
    return jax.shard_map(
        shards,
        mesh=mesh,
        in_specs=(
            P("seq", "dp"),
            P("seq", "dp"),
            P("seq", "dp"),
            P("seq", "dp"),
            P("dp"),
            P("dp"),
            P(),
        ),
        out_specs=(P("seq", "dp"), P("seq", "dp"), P("seq", "dp"), P(("dp", "seq"))),
        check_vma=False,
    )
```

```python
import functools
import math

import jax
import jax.numpy as jnp
from jax import lax
from jax.experimental import pallas as pl
from jax.experimental.pallas import tpu as pltpu
from jax.sharding import PartitionSpec as P

F32, BF16 = jnp.float32, jnp.bfloat16
HEAD, TOK, HEADS_DEV, STREAM, FEATURES = 128, 512, 8, 32768, 4096
BLOCK_Z, BLOCK_Y = 8 * TOK, 2 * TOK
SMEM = pl.BlockSpec(memory_space=pltpu.SMEM)
VMEM = pl.BlockSpec(memory_space=pltpu.VMEM)
ANY = pl.BlockSpec(memory_space=pl.ANY)


def rate_of(level):
    row = jnp.full((1, HEAD), level.astype(F32), F32)
    slow = jnp.exp(row * (math.log(8.0) / 7.0)) * (-0.25 / STREAM)
    lowest = math.log(4.0 / STREAM)
    fast = -jnp.exp(lowest + (row - 8.0) * ((math.log(1.0 / 32.0) - lowest) / 7.0))
    return jnp.where(row < 8.0, slow, fast)


def starts_before(bounds, place):
    return sum((bounds[i] < place).astype(jnp.int32) for i in range(3))


def carry(rate, bounds, left, right):
    same = (starts_before(bounds, left) == starts_before(bounds, right)) & (left <= right)
    span = jnp.maximum(right - left, 0).astype(F32)
    return jnp.exp(rate * span) * jnp.where(same, 1.0, 0.0).astype(F32)


def place():
    at = lax.axis_index("seq")
    return at, at // 8, (at // 2) % 4, at % 2


def tokens_in(bounds, at):
    first = at * TOK
    entering, leaving = TOK, 0
    for i in range(3):
        local = bounds[i] - first
        entering = jnp.where((local >= 0) & (local < entering), local, entering)
        leaving = jnp.where((local < TOK) & (local > leaving), local, leaving)
    return entering, leaving


def powers(rate, first, up):
    t = lax.broadcasted_iota(jnp.int32, (8, HEAD), 0)
    t = (t if up else 7 - t).astype(F32)
    rows, size = jnp.exp(rate * (t + first)), 8
    while size < TOK:
        more = rows * jnp.exp(rate * float(size))
        rows = jnp.concatenate([rows, more] if up else [more, rows], axis=0)
        size *= 2
    return rows


def token_rows():
    return lax.broadcasted_iota(jnp.int32, (TOK, HEAD), 0)


def enter_decay(rate, entering):
    return jnp.where(token_rows() < entering, powers(rate, 1.0, True), 0.0)


def leave_decay(rate, leaving):
    return jnp.where(token_rows() >= leaving, powers(rate, 0.0, False), 0.0)


def masks_kernel(decay, bounds, mask, flipped):
    first = place()[0] * TOK
    for lo in range(0, TOK, HEAD):
        row = lax.broadcasted_iota(jnp.int32, (HEAD, TOK), 0) + lo
        column = lax.broadcasted_iota(jnp.int32, (HEAD, TOK), 1)
        since = jnp.zeros((HEAD, TOK), jnp.int32)
        until = jnp.full((HEAD, TOK), TOK, jnp.int32)
        for i in range(3):
            local = bounds[i] - first
            since = jnp.where(row >= local, jnp.maximum(since, local), since)
            until = jnp.where(row < local, jnp.minimum(until, local), until)
        rows = slice(lo, lo + HEAD)
        mask[rows, :] = jnp.where((column <= row) & (column >= since), 1.0, 0.0).astype(BF16)
        flipped[rows, :] = jnp.where((column >= row) & (column < until), 1.0, 0.0).astype(BF16)


def mm(a, b):
    return lax.dot_general(a, b, (((1,), (0,)), ((), ())), preferred_element_type=F32)


def mm_bt(a, b):
    return lax.dot_general(a, b, (((1,), (1,)), ((), ())), preferred_element_type=F32)


def mm_at(a, b):
    return lax.dot_general(a, b, (((0,), (0,)), ((), ())), preferred_element_type=F32)


def call(kernel, outs, grid=None, in_specs=None, out_specs=None, scratch=(), flops=0, moved=0, limit=24, aliases={}):
    extra = {} if grid is None else {"grid": grid}
    return pl.pallas_call(
        kernel,
        out_shape=outs,
        in_specs=in_specs,
        out_specs=out_specs,
        scratch_shapes=list(scratch),
        input_output_aliases=aliases,
        compiler_params=pltpu.CompilerParams(vmem_limit_bytes=limit << 20),
        cost_estimate=pl.CostEstimate(flops=flops, bytes_accessed=moved, transcendentals=0),
        **extra,
    )


def shape(*dims, dtype=F32):
    return jax.ShapeDtypeStruct(dims, dtype)


def columns(index):
    return pl.ds(pl.multiple_of(index * HEAD, HEAD), HEAD)


def first_head(own):
    c = place()[3]
    return 4 * c if own else 4 * (1 - c)


def sent_states_kernel(decay, bounds, k, v, out, k_in, v_in, sems):
    at, _, y, _ = place()
    _, leaving = tokens_in(bounds, at)
    heads = [first_head(False) + (y ^ i) for i in range(4)]
    copies = []
    for i, head in enumerate(heads):
        pair = (
            pltpu.make_async_copy(k.at[:, columns(head)], k_in.at[i], sems.at[0, i]),
            pltpu.make_async_copy(v.at[:, columns(head)], v_in.at[i], sems.at[1, i]),
        )
        for copy in pair:
            copy.start()
        copies.append(pair)
    for i, head in enumerate(heads):
        weights = leave_decay(rate_of(decay[head]), leaving)
        for copy in copies[i]:
            copy.wait()
        decayed = (weights * k_in[i].astype(F32)).astype(BF16)
        out[i * HEAD : (i + 1) * HEAD, :] = mm_at(decayed, v_in[i])


def kept_states_kernel(decay, bounds, k, v, after, out):
    at, _, y, _ = place()
    _, leaving = tokens_in(bounds, at)
    for i in range(4):
        head = first_head(True) + (y ^ i)
        weights = leave_decay(rate_of(decay[head]), leaving)
        decayed = (weights * k[:, columns(head)].astype(F32)).astype(BF16)
        out[i * HEAD : (i + 1) * HEAD, :] = mm_at(decayed, v[:, columns(head)])


def intra_kernel(decay, bounds, q, k, v, mask, after, out_ref, *, own):
    half = TOK // 2
    for j in range(4):
        head = first_head(own) + j
        rate, at = rate_of(decay[head]), columns(head)
        scaled = (powers(-rate, 0.0, True) * k[:, at].astype(F32)).astype(BF16)
        down = powers(rate, 0.0, True)
        for lo in (0, half):
            hi = lo + half
            mixing = mm_bt(q[lo:hi, at], scaled[0:hi, :]).astype(BF16) * mask[lo:hi, 0:hi]
            out_ref[lo:hi, j * HEAD : (j + 1) * HEAD] = down[lo:hi, :] * mm(mixing, v[0:hi, at])


def chip_kernel(decay, bounds, keep, got, send, after, *outs, reverse, gains):
    at, z, y, c = place()
    middle = (at - c + 1) * TOK
    for k in range(4):
        rate = rate_of(decay[4 * c + (y ^ k)])
        if reverse:
            far = carry(rate, bounds, middle - TOK, middle)
            own, other = jnp.where(c == 1, far, 1.0), jnp.where(c == 1, 1.0, far)
        else:
            far = carry(rate, bounds, middle, middle + TOK)
            own, other = jnp.where(c == 0, far, 1.0), jnp.where(c == 0, 1.0, far)
        rows = slice(k * HEAD, (k + 1) * HEAD)
        outs[k][0:HEAD, :] = own * keep[rows, :] + other * got[rows, :]
        if gains:
            tail = slice(4 * HEAD, 4 * HEAD + 8)
            outs[k][HEAD : HEAD + 8, :] = send[tail, :] + got[tail, :]


def row_kernel(decay, bounds, t0, t1, t2, t3, after, out, *, reverse, gains):
    at, z, y, c = place()
    rate = rate_of(decay[4 * c + y])
    total = 0.0
    for k, t in enumerate((t0, t1, t2, t3)):
        edge = z * BLOCK_Z + (y ^ k) * BLOCK_Y
        if reverse:
            weight = carry(rate, bounds, z * BLOCK_Z, edge)
        else:
            weight = carry(rate, bounds, edge + BLOCK_Y, (z + 1) * BLOCK_Z)
        total += weight * t[0:HEAD, :]
    out[0:HEAD, :] = total
    if gains:
        tail = slice(HEAD, HEAD + 8)
        out[tail, :] = t0[tail, :] + t1[tail, :] + t2[tail, :] + t3[tail, :]


def pair_kernel(decay, bounds, r0, r1, after, out, *, reverse, gains):
    at, z, y, c = place()
    rate = rate_of(decay[4 * c + y])
    first = (z - z % 2) * BLOCK_Z
    total = 0.0
    for k, r in enumerate((r0, r1)):
        edge = (z ^ k) * BLOCK_Z
        if reverse:
            weight = carry(rate, bounds, first, edge)
        else:
            weight = carry(rate, bounds, edge + BLOCK_Z, first + 2 * BLOCK_Z)
        total += weight * r[0:HEAD, :]
    out[0:HEAD, :] = total
    if gains:
        tail = slice(HEAD, HEAD + 8)
        out[tail, :] = r0[tail, :] + r1[tail, :]


PAIRS = (2, 5, 6)


def chips_in_kernel(decay, bounds, r1, p0, p1, p2, p3, t0, t1, t2, t3, after, *outs, reverse, gains):
    at, z, y, c = place()
    rate = rate_of(decay[4 * c + y])
    edge = (z + 1) * BLOCK_Z if reverse else z * BLOCK_Z
    other = (z ^ 1) * BLOCK_Z
    if reverse:
        total = carry(rate, bounds, edge, other) * r1[0:HEAD, :]
    else:
        total = carry(rate, bounds, other + BLOCK_Z, edge) * r1[0:HEAD, :]
    for k, p in zip(PAIRS, (p1, p2, p3)):
        there = z ^ k
        first = (there - there % 2) * BLOCK_Z
        if reverse:
            weight = carry(rate, bounds, edge, first)
        else:
            weight = carry(rate, bounds, first + 2 * BLOCK_Z, edge)
        total += weight * p[0:HEAD, :]
    for k in range(4):
        here = z * BLOCK_Z + (y ^ k) * BLOCK_Y
        if reverse:
            state = carry(rate, bounds, here + BLOCK_Y, edge) * total
        else:
            state = carry(rate, bounds, edge, here) * total
        for m, t in enumerate((t0, t1, t2, t3)):
            if m == k:
                continue
            there = z * BLOCK_Z + (y ^ m) * BLOCK_Y
            if reverse:
                weight = carry(rate, bounds, here + BLOCK_Y, there)
            else:
                weight = carry(rate, bounds, there + BLOCK_Y, here)
            state += weight * t[0:HEAD, :]
        outs[k][...] = state
    if gains:
        tail = slice(HEAD, HEAD + 8)
        outs[4][...] = p0[tail, :] + p1[tail, :] + p2[tail, :] + p3[tail, :]
        row = outs[4][pl.ds(z, 1), :]
        turned = pltpu.roll(row, (HEAD - 32 * y - 16 * c) % HEAD, axis=1)
        outs[5][...] = turned[0, 0:16]


def cores_in_kernel(decay, bounds, v0, v1, v2, v3, keep, got, after, mine, other, *, reverse):
    at, z, y, c = place()
    middle = (at - c + 1) * TOK
    for k, v in enumerate((v0, v1, v2, v3)):
        rate = rate_of(decay[4 * c + (y ^ k)])
        if reverse:
            step, deep = carry(rate, bounds, middle, middle + TOK), c == 0
        else:
            step, deep = carry(rate, bounds, middle - TOK, middle), c == 1
        rows = slice(k * HEAD, (k + 1) * HEAD)
        state = v[...]
        mine[rows, :] = jnp.where(deep, step * state + got[rows, :], state)
        other[rows, :] = jnp.where(deep, state, step * state + keep[rows, :])


def state_of(states, j):
    return states[columns(j ^ place()[2]), :].astype(BF16)


def attended_kernel(decay, bounds, q, intra, grad, gain, states, *refs, own):
    out_ref, sums = refs[-2:]
    entering, _ = tokens_in(bounds, place()[0])
    square, cross = 0.0, 0.0
    for j in range(4):
        head = first_head(own) + j
        at, local = columns(head), slice(j * HEAD, (j + 1) * HEAD)
        weights = enter_decay(rate_of(decay[head]), entering)
        out = intra[:, local] + weights * mm(q[:, at], state_of(states, j))
        out_ref[:, local] = out
        square += out * out
        cross += out * (grad[:, at].astype(F32) * gain[pl.ds(head, 1), :])
    square = jnp.sum(square.T, axis=0, keepdims=True)
    cross = jnp.sum(cross.T, axis=0, keepdims=True)
    if not own:
        square += refs[0][0:1, :]
        cross += refs[0][4:5, :]
    sums[0:4, :] = jnp.broadcast_to(square, (4, TOK))
    sums[4:8, :] = jnp.broadcast_to(cross, (4, TOK))


def mixed_kernel(decay, bounds, s0, s1, s2, s3, o, grad, q, gain, *refs, own):
    d, states = refs[-2:]
    at, _, y, _ = place()
    entering, _ = tokens_in(bounds, at)
    sums = s0[...] + s1[...] + s2[...] + s3[...]
    r = lax.rsqrt(sums[0:1, :] * (1.0 / FEATURES) + 1e-06)
    inverse = jnp.broadcast_to(r, (HEAD, TOK)).T
    mean = jnp.broadcast_to(sums[4:5, :] * r * (1.0 / FEATURES), (HEAD, TOK)).T
    tail = 4 * HEAD

    def term(head, wide, normed):
        if not own:
            states[pl.ds(tail + head, 1), :] = jnp.sum(wide * normed, axis=0, keepdims=True)

    for j in range(4):
        head = first_head(own) + j
        local = slice(j * HEAD, (j + 1) * HEAD)
        normed = inverse * o[:, local]
        wide = grad[:, columns(head)].astype(F32)
        low = (inverse * (wide * gain[pl.ds(head, 1), :] - normed * mean)).astype(BF16)
        d[:, local] = low
        term(head, wide, normed)
        weights = enter_decay(rate_of(decay[head]), entering)
        states[columns(j ^ y), :] = mm_at((weights * q[:, columns(head)].astype(F32)).astype(BF16), low)
    if not own:
        for j in range(4):
            head = first_head(True) + j
            term(head, grad[:, columns(head)].astype(F32), inverse * refs[0][:, j * HEAD : (j + 1) * HEAD])


def grads_kernel(decay, bounds, q, k, v, d, mask, flipped, states, after, dq, dk, dv, *, own, start):
    entering, _ = tokens_in(bounds, place()[0])
    half = TOK // 2
    for n in range(2):
        j = start + n
        head = first_head(own) + j
        rate, at = rate_of(decay[head]), columns(head)
        out, local = slice(n * HEAD, (n + 1) * HEAD), slice(j * HEAD, (j + 1) * HEAD)
        state = state_of(states, j)
        up, down = powers(-rate, 0.0, True), powers(rate, 0.0, True)
        inside = jnp.where(token_rows() < entering, jnp.exp(rate), 0.0)
        v_up = (up * v[:, at].astype(F32)).astype(BF16)
        d_down = (down * d[:, local].astype(F32)).astype(BF16)
        q_down = (down * q[:, at].astype(F32)).astype(BF16)
        for lo in (0, half):
            hi = lo + half
            mixing = mm_bt(d[lo:hi, local], v_up[0:hi, :]).astype(BF16) * mask[lo:hi, 0:hi]
            grad = mm(mixing, k[0:hi, at]) + inside[lo:hi, :] * mm_bt(d[lo:hi, local], state)
            dq[lo:hi, out] = (down[lo:hi, :] * grad).astype(BF16)
            mixing = mm_bt(v[lo:hi, at], d_down[lo:TOK, :]).astype(BF16) * flipped[lo:hi, lo:TOK]
            dk[lo:hi, out] = up[lo:hi, :] * mm(mixing, q[lo:TOK, at])
            mixing = mm_bt(k[lo:hi, at], q_down[lo:TOK, :]).astype(BF16) * flipped[lo:hi, lo:TOK]
            dv[lo:hi, out] = up[lo:hi, :] * mm(mixing, d[lo:TOK, local])


def last_kernel(decay, bounds, k, v, states, *refs, own):
    parts, buffers = refs[:4], refs[-3:]
    (dk, dv), sems = refs[-5:-3] if not own else refs[-6:-4], buffers[2]
    _, leaving = tokens_in(bounds, place()[0])
    copies = []
    if own:
        dq = refs[-4]
        for n, part in enumerate(refs[4:8]):
            spot = pl.ds(pl.multiple_of((first_head(n < 2) + 2 * (n % 2)) * HEAD, 2 * HEAD), 2 * HEAD)
            copies.append(pltpu.make_async_copy(part, dq.at[:, spot], sems.at[2, n]))
            copies[-1].start()
    for j in range(4):
        head = first_head(own) + j
        at, local = columns(head), slice(j * HEAD, (j + 1) * HEAD)
        inner = slice(j % 2 * HEAD, (j % 2 + 1) * HEAD)
        weights = leave_decay(rate_of(decay[head]), leaving)
        state = state_of(states, j)
        buffers[0][:, local] = (parts[j // 2][:, inner] + weights * mm_bt(v[:, at], state)).astype(BF16)
        copies.append(pltpu.make_async_copy(buffers[0].at[:, local], dk.at[:, at], sems.at[0, j]))
        copies[-1].start()
        buffers[1][:, local] = (parts[2 + j // 2][:, inner] + weights * mm(k[:, at], state)).astype(BF16)
        copies.append(pltpu.make_async_copy(buffers[1].at[:, local], dv.at[:, at], sems.at[1, j]))
        copies[-1].start()
    for copy in copies:
        copy.wait()


def index(z, y, c):
    return (z * 4 + y) * 2 + c


def exchange(array, dz=0, dy=0, dc=0):
    pairs = [
        (index(z, y, c), index(z ^ dz, y ^ dy, c ^ dc))
        for z in range(8)
        for y in range(4)
        for c in range(2)
    ]
    return lax.ppermute(array, "seq", pairs)


def carried(send, make_keep, decay, bounds, reverse, gains, work):
    extra = 8 if gains else 0
    small = shape(HEAD + extra, HEAD)

    def step(kernel, outs, *args, after, **more):
        return call(
            functools.partial(kernel, reverse=reverse, **more),
            outs,
            in_specs=[SMEM, SMEM] + [VMEM] * len(args) + [ANY],
            out_specs=jax.tree.map(lambda _: VMEM, outs),
            limit=8,
        )(decay, bounds, *args, after)

    got = exchange(send, dc=1)
    keep = make_keep(send)
    chips = step(chip_kernel, [small] * 4, keep, got, send, gains=gains, after=keep)
    done = work[0](chips[0])
    chips = [chips[0]] + [exchange(chips[k], dy=k) for k in (1, 2, 3)]
    row = step(row_kernel, small, *chips, gains=gains, after=done)
    done = work[1](row)
    near = exchange(row, dz=1)
    pair = step(pair_kernel, small, row, near, gains=gains, after=done)
    done = work[2](pair)
    pairs = [pair] + [exchange(pair, dz=k) for k in PAIRS]
    outs = [shape(HEAD, HEAD)] * 4 + ([shape(8, HEAD), shape(16)] if gains else [])
    outs = step(chips_in_kernel, outs, near, *pairs, *chips, gains=gains, after=done)
    done = work[3](outs[0])
    states = [outs[0]] + [exchange(outs[k], dy=k) for k in (1, 2, 3)]
    mine, other = step(cores_in_kernel, [shape(4 * HEAD, HEAD)] * 2, *states, keep, got, after=done)
    return mine, other, (outs[5] if gains else None)


def shards(queries, keys, values, out_grad, gain, decay, bounds):
    gain = gain.reshape(HEADS_DEV, HEAD)
    width = HEADS_DEV * HEAD
    half = width // 2
    small_mm = TOK * HEAD * HEAD * HEADS_DEV
    big_mm = 2 * TOK * TOK * HEAD * HEADS_DEV * 3 // 4
    state_shape = shape(4 * HEAD, HEAD)
    scalars = [SMEM, SMEM]

    def local(kernel, outs, args, order=(), flops=0, moved=0, **more):
        return call(
            functools.partial(kernel, **more),
            outs,
            in_specs=scalars + [VMEM] * len(args) + [ANY] * len(order),
            out_specs=jax.tree.map(lambda _: VMEM, outs),
            flops=flops,
            moved=moved,
        )(decay, bounds, *args, *order)

    send = call(
        sent_states_kernel,
        state_shape,
        in_specs=scalars + [ANY] * 2,
        out_specs=VMEM,
        scratch=[pltpu.VMEM((4, TOK, HEAD), BF16)] * 2 + [pltpu.SemaphoreType.DMA((2, 4))],
        flops=small_mm,
        moved=3 << 19,
    )(*[pltpu.with_memory_space_constraint(x, pltpu.HBM) for x in (decay, bounds, keys, values)])

    def keep_states(after):
        return local(kept_states_kernel, state_shape, [keys, values], [after], small_mm, 3 << 19)

    made = {}
    pairs = shape(TOK, TOK, dtype=BF16)

    def make_intra(own):
        def run(after):
            if own:
                made["masks"] = local(masks_kernel, [pairs] * 2, [], moved=1 << 20)
            made[own] = local(
                intra_kernel,
                shape(TOK, half),
                [queries, keys, values, made["masks"][0]],
                [after],
                big_mm,
                3 << 20,
                own=own,
            )
            return made[own]

        return run

    def same(after):
        return after

    mine, other, _ = carried(
        send, keep_states, decay, bounds, False, False, [make_intra(True), same, make_intra(False), same]
    )
    theirs = exchange(other, dc=1)
    sums = shape(8, TOK)
    outs = [shape(TOK, half), sums]
    o_mine, own_sums = local(
        attended_kernel, outs, [queries, made[True], out_grad, gain, mine], [other], small_mm, 3 << 20, own=True
    )
    o_other, sums = local(
        attended_kernel,
        outs,
        [queries, made[False], out_grad, gain, theirs, own_sums],
        [],
        small_mm,
        3 << 20,
        own=False,
    )
    totals = [sums] + [lax.ppermute(sums, "dp", [(i, i ^ k) for i in range(4)]) for k in (1, 2, 3)]
    outs = [shape(TOK, half, dtype=BF16), shape(4 * HEAD + 8, HEAD)]
    d_other, send = local(
        mixed_kernel,
        outs,
        [*totals, o_other, out_grad, queries, gain, o_mine],
        [],
        small_mm,
        3 << 20,
        own=False,
    )

    def keep_grads(after):
        outs = [shape(TOK, half, dtype=BF16), shape(4 * HEAD, HEAD)]
        made["d"], keep = local(
            mixed_kernel, outs, [*totals, o_mine, out_grad, queries, gain], [after], small_mm, 3 << 20, own=True
        )
        return keep

    mask, flipped = made["masks"]

    def make_grads(n):
        def run(after):
            own = n < 2
            made["grads", n] = local(
                grads_kernel,
                [shape(TOK, 2 * HEAD, dtype=BF16), shape(TOK, 2 * HEAD), shape(TOK, 2 * HEAD)],
                [queries, keys, values, made["d"] if own else d_other, mask, flipped, mine if own else theirs],
                [after],
                6 * big_mm // 4,
                2 << 20,
                own=own,
                start=2 * (n % 2),
            )
            return made["grads", n][1]

        return run

    last_mine, last_other, gains = carried(
        send, keep_grads, decay, bounds, True, True, [make_grads(n) for n in range(4)]
    )
    last_theirs = exchange(last_other, dc=1)
    dq, dk, dv = zip(*[made["grads", n] for n in range(4)])
    full = shape(TOK, width, dtype=BF16)
    scratch = [pltpu.VMEM((TOK, half), BF16)] * 2 + [pltpu.SemaphoreType.DMA((3, 4))]
    dk_out, dv_out, dq_out = call(
        functools.partial(last_kernel, own=True),
        [full] * 3,
        in_specs=scalars + [VMEM] * 11 + [ANY],
        out_specs=[ANY] * 3,
        scratch=scratch,
        flops=2 * small_mm,
        moved=6 << 20,
    )(decay, bounds, keys, values, last_mine, *dk[:2], *dv[:2], *dq, last_other)
    dk_out, dv_out = call(
        functools.partial(last_kernel, own=False),
        [full] * 2,
        in_specs=scalars + [VMEM] * 7 + [ANY] * 2,
        out_specs=[ANY] * 2,
        scratch=scratch,
        flops=2 * small_mm,
        moved=4 << 20,
        aliases={9: 0, 10: 1},
    )(decay, bounds, keys, values, last_theirs, *dk[2:], *dv[2:], dk_out, dv_out)
    return dq_out, dk_out, dv_out, gains


def solution(mesh):
    return jax.shard_map(
        shards,
        mesh=mesh,
        in_specs=(
            P("seq", "dp"),
            P("seq", "dp"),
            P("seq", "dp"),
            P("seq", "dp"),
            P("dp"),
            P("dp"),
            P(),
        ),
        out_specs=(P("seq", "dp"), P("seq", "dp"), P("seq", "dp"), P(("dp", "seq"))),
        check_vma=False,
    )
```

```python
import functools
import math

import jax
import jax.numpy as jnp
from jax import lax
from jax.experimental import pallas as pl
from jax.experimental.pallas import tpu as pltpu
from jax.sharding import PartitionSpec as P

F32, BF16 = jnp.float32, jnp.bfloat16
HEAD, TOK, HEADS_DEV, STREAM, FEATURES = 128, 512, 8, 32768, 4096
BLOCK_Z, BLOCK_Y = 8 * TOK, 2 * TOK
SMEM = pl.BlockSpec(memory_space=pltpu.SMEM)
VMEM = pl.BlockSpec(memory_space=pltpu.VMEM)
ANY = pl.BlockSpec(memory_space=pl.ANY)


def rate_of(level):
    row = jnp.full((1, HEAD), level.astype(F32), F32)
    slow = jnp.exp(row * (math.log(8.0) / 7.0)) * (-0.25 / STREAM)
    lowest = math.log(4.0 / STREAM)
    fast = -jnp.exp(lowest + (row - 8.0) * ((math.log(1.0 / 32.0) - lowest) / 7.0))
    return jnp.where(row < 8.0, slow, fast)


def starts_before(bounds, place):
    return sum((bounds[i] < place).astype(jnp.int32) for i in range(3))


def carry(rate, bounds, left, right):
    same = (starts_before(bounds, left) == starts_before(bounds, right)) & (left <= right)
    span = jnp.maximum(right - left, 0).astype(F32)
    return jnp.exp(rate * span) * jnp.where(same, 1.0, 0.0).astype(F32)


def place():
    at = lax.axis_index("seq")
    return at, at // 8, (at // 2) % 4, at % 2


def tokens_in(bounds, at):
    first = at * TOK
    entering, leaving = TOK, 0
    for i in range(3):
        local = bounds[i] - first
        entering = jnp.where((local >= 0) & (local < entering), local, entering)
        leaving = jnp.where((local < TOK) & (local > leaving), local, leaving)
    return entering, leaving


def powers(rate, first, up):
    t = lax.broadcasted_iota(jnp.int32, (8, HEAD), 0)
    t = (t if up else 7 - t).astype(F32)
    rows, size = jnp.exp(rate * (t + first)), 8
    while size < TOK:
        more = rows * jnp.exp(rate * float(size))
        rows = jnp.concatenate([rows, more] if up else [more, rows], axis=0)
        size *= 2
    return rows


RATES, ENTER, LEAVE, FORWARD, BACKWARD = 0, 8, 9, 16, 0
CHIP_OWN, CHIP_OTHER, ROW, HALF, FAR, NEAR, INTO, ACROSS, CORE = 0, 4, 8, 12, 16, 16, 20, 24, 40
CHAIN_ROWS = 48
FAR_Z = 6
SLOT = (0, 2, 1, 3)


def token_rows():
    return lax.broadcasted_iota(jnp.int32, (TOK, HEAD), 0).astype(F32)


def rate_row(table, head):
    return table[pl.ds(head, 1), :]


def enter_decay(table, head):
    return jnp.where(token_rows() < table[ENTER : ENTER + 1, :], powers(rate_row(table, head), 1.0, True), 0.0)


def leave_decay(table, head):
    return jnp.where(token_rows() >= table[LEAVE : LEAVE + 1, :], powers(rate_row(table, head), 0.0, False), 0.0)


def fill_chain(table, base, decay, bounds, reverse):
    at, z, y, c = place()
    one = jnp.ones((1, HEAD), F32)
    middle = (at - c + 1) * TOK
    row, row_end, centre = z * BLOCK_Z, (z + 1) * BLOCK_Z, 4 * BLOCK_Z

    def put(index, value):
        table[base + index : base + index + 1, :] = value

    def across(rate, earlier, later):
        return carry(rate, bounds, earlier, later)

    for k in range(4):
        rate = rate_of(decay[4 * c + (y ^ k)])
        first, second = across(rate, middle - TOK, middle), across(rate, middle, middle + TOK)
        if reverse:
            put(CHIP_OWN + k, jnp.where(c == 1, first, one))
            put(CHIP_OTHER + k, jnp.where(c == 1, one, first))
            put(CORE + k, second)
        else:
            put(CHIP_OWN + k, jnp.where(c == 0, second, one))
            put(CHIP_OTHER + k, jnp.where(c == 0, one, second))
            put(CORE + k, first)
    rate = rate_of(decay[4 * c + y])
    for k in range(4):
        here, line = row + (y ^ k) * BLOCK_Y, (z ^ k) * BLOCK_Z
        if reverse:
            put(ROW + k, across(rate, row, here))
            put(HALF + k, across(rate, centre, line))
            put(NEAR + k, across(rate, row_end, line if k else centre))
            put(INTO + k, across(rate, here + BLOCK_Y, row_end))
        else:
            put(ROW + k, across(rate, here + BLOCK_Y, row_end))
            put(HALF + k, across(rate, line + BLOCK_Z, centre))
            put(NEAR + k, across(rate, line + BLOCK_Z if k else centre, row))
            put(INTO + k, across(rate, row, here))
        for m in range(4):
            if m != k:
                there = row + (y ^ m) * BLOCK_Y
                if reverse:
                    put(ACROSS + 4 * k + m, across(rate, here + BLOCK_Y, there))
                else:
                    put(ACROSS + 4 * k + m, across(rate, there + BLOCK_Y, here))


def masks_kernel(decay, bounds, gain, after, mask, flipped, table, gain_out):
    gain_out[...] = gain[...]
    fill_chain(table, BACKWARD, decay, bounds, True)
    first = place()[0] * TOK
    for lo in range(0, TOK, HEAD):
        row = lax.broadcasted_iota(jnp.int32, (HEAD, TOK), 0) + lo
        column = lax.broadcasted_iota(jnp.int32, (HEAD, TOK), 1)
        since = jnp.zeros((HEAD, TOK), jnp.int32)
        until = jnp.full((HEAD, TOK), TOK, jnp.int32)
        for i in range(3):
            local = bounds[i] - first
            since = jnp.where(row >= local, jnp.maximum(since, local), since)
            until = jnp.where(row < local, jnp.minimum(until, local), until)
        rows = slice(lo, lo + HEAD)
        mask[rows, :] = jnp.where((column <= row) & (column >= since), 1.0, 0.0).astype(BF16)
        flipped[rows, :] = jnp.where((column >= row) & (column < until), 1.0, 0.0).astype(BF16)


def mm(a, b):
    return lax.dot_general(a, b, (((1,), (0,)), ((), ())), preferred_element_type=F32)


def mm_bt(a, b):
    return lax.dot_general(a, b, (((1,), (1,)), ((), ())), preferred_element_type=F32)


def mm_at(a, b):
    return lax.dot_general(a, b, (((0,), (0,)), ((), ())), preferred_element_type=F32)


def call(kernel, outs, grid=None, in_specs=None, out_specs=None, scratch=(), flops=0, moved=0, limit=24, aliases={}):
    extra = {} if grid is None else {"grid": grid}
    return pl.pallas_call(
        kernel,
        out_shape=outs,
        in_specs=in_specs,
        out_specs=out_specs,
        scratch_shapes=list(scratch),
        input_output_aliases=aliases,
        compiler_params=pltpu.CompilerParams(vmem_limit_bytes=limit << 20),
        cost_estimate=pl.CostEstimate(flops=flops, bytes_accessed=moved, transcendentals=0),
        **extra,
    )


def shape(*dims, dtype=F32):
    return jax.ShapeDtypeStruct(dims, dtype)


def columns(index):
    return pl.ds(pl.multiple_of(index * HEAD, HEAD), HEAD)


def first_head(own):
    c = place()[3]
    return 4 * c if own else 4 * (1 - c)


def sent_states_kernel(decay_in, bounds_in, k, v, out, table, k_in, v_in, decay, bounds, sems):
    at, _, y, _ = place()
    heads = [first_head(False) + (y ^ i) for i in range(4)]
    numbers = (
        pltpu.make_async_copy(decay_in, decay, sems.at[2, 0]),
        pltpu.make_async_copy(bounds_in, bounds, sems.at[2, 1]),
    )
    for copy in numbers:
        copy.start()
    copies = []
    for i, head in enumerate(heads):
        pair = (
            pltpu.make_async_copy(k.at[:, columns(head)], k_in.at[i], sems.at[0, i]),
            pltpu.make_async_copy(v.at[:, columns(head)], v_in.at[i], sems.at[1, i]),
        )
        for copy in pair:
            copy.start()
        copies.append(pair)
    for copy in numbers:
        copy.wait()
    for head in range(HEADS_DEV):
        table[RATES + head : RATES + head + 1, :] = rate_of(decay[head])
    entering, leaving = tokens_in(bounds, at)
    table[ENTER : ENTER + 1, :] = jnp.full((1, HEAD), entering.astype(F32), F32)
    table[LEAVE : LEAVE + 1, :] = jnp.full((1, HEAD), leaving.astype(F32), F32)
    fill_chain(table, FORWARD, decay, bounds, False)
    for i, head in enumerate(heads):
        weights = leave_decay(table, head)
        for copy in copies[i]:
            copy.wait()
        decayed = (weights * k_in[i].astype(F32)).astype(BF16)
        out[i * HEAD : (i + 1) * HEAD, :] = mm_at(decayed, v_in[i])


def kept_states_kernel(table, k, v, after, out):
    y = place()[2]
    for i in range(4):
        head = first_head(True) + (y ^ i)
        decayed = (leave_decay(table, head) * k[:, columns(head)].astype(F32)).astype(BF16)
        out[i * HEAD : (i + 1) * HEAD, :] = mm_at(decayed, v[:, columns(head)])


def intra_kernel(table, q, k, v, mask, after, out_ref, *, own):
    half = TOK // 2
    for j in range(4):
        head = first_head(own) + j
        rate, at = rate_row(table, head), columns(head)
        scaled = (powers(-rate, 0.0, True) * k[:, at].astype(F32)).astype(BF16)
        down = powers(rate, 0.0, True)
        for lo in (0, half):
            hi = lo + half
            mixing = mm_bt(q[lo:hi, at], scaled[0:hi, :]).astype(BF16) * mask[lo:hi, 0:hi]
            out_ref[lo:hi, j * HEAD : (j + 1) * HEAD] = down[lo:hi, :] * mm(mixing, v[0:hi, at])


def chip_kernel(table, keep, got, send, after, *outs, base, reverse, gains):
    for k in range(4):
        own, other = base + CHIP_OWN + k, base + CHIP_OTHER + k
        rows = slice(k * HEAD, (k + 1) * HEAD)
        outs[SLOT[k]][0:HEAD, :] = table[own : own + 1, :] * keep[rows, :] + table[other : other + 1, :] * got[rows, :]
        if gains:
            tail = slice(4 * HEAD, 4 * HEAD + 8)
            outs[SLOT[k]][HEAD : HEAD + 8, :] = send[tail, :] + got[tail, :]


def sum_kernel(table, p0, p1, p2, p3, after, out, *, base, reverse, gains):
    total = 0.0
    for k, p in enumerate((p0, p1, p2, p3)):
        total += table[base + k : base + k + 1, :] * p[0:HEAD, :]
    out[0:HEAD, :] = total
    if gains:
        tail = slice(HEAD, HEAD + 8)
        out[tail, :] = p0[tail, :] + p1[tail, :] + p2[tail, :] + p3[tail, :]


def chips_in_kernel(table, r1, r2, r3, far, sent, t0, t1, t2, t3, after, *outs, base, reverse, gains):
    total = table[base + FAR : base + FAR + 1, :] * far[0:HEAD, :]
    for k, r in enumerate((r1, r2, r3)):
        at = base + NEAR + 1 + k
        total += table[at : at + 1, :] * r[0:HEAD, :]
    for k in range(4):
        at = base + INTO + k
        state = table[at : at + 1, :] * total
        for m, t in enumerate((t0, t1, t2, t3)):
            if m != k:
                at = base + ACROSS + 4 * k + m
                state += table[at : at + 1, :] * t[0:HEAD, :]
        outs[SLOT[k]][...] = state
    if gains:
        _, z, y, c = place()
        tail = slice(HEAD, HEAD + 8)
        outs[4][...] = sent[tail, :] + far[tail, :]
        row = outs[4][pl.ds(z, 1), :]
        turned = pltpu.roll(row, (HEAD - 32 * y - 16 * c) % HEAD, axis=1)
        outs[5][...] = turned[0, 0:16]


def cores_in_kernel(table, v0, v1, v2, v3, keep, got, after, mine, other, *, base, reverse):
    c = place()[3]
    deep = c == 0 if reverse else c == 1
    for k, v in enumerate((v0, v1, v2, v3)):
        at = base + CORE + k
        rows = slice(k * HEAD, (k + 1) * HEAD)
        state = v[...]
        step = table[at : at + 1, :] * state
        mine[rows, :] = jnp.where(deep, step + got[rows, :], state)
        other[rows, :] = jnp.where(deep, state, step + keep[rows, :])


def state_of(states, j):
    return states[columns(j ^ place()[2]), :].astype(BF16)


def attended_kernel(table, q, intra, grad, gain, states, *refs, own):
    out_ref, sums = refs[-2:]
    square, cross = 0.0, 0.0
    for j in range(4):
        head = first_head(own) + j
        at, local = columns(head), slice(j * HEAD, (j + 1) * HEAD)
        weights = enter_decay(table, head)
        out = intra[:, local] + weights * mm(q[:, at], state_of(states, j))
        out_ref[:, local] = out
        square += out * out
        cross += out * (grad[:, at].astype(F32) * gain[pl.ds(head, 1), :])
    square = jnp.sum(square.T, axis=0, keepdims=True)
    cross = jnp.sum(cross.T, axis=0, keepdims=True)
    if not own:
        square += refs[0][0:1, :]
        cross += refs[0][4:5, :]
    sums[0:4, :] = jnp.broadcast_to(square, (4, TOK))
    sums[4:8, :] = jnp.broadcast_to(cross, (4, TOK))


def mixed_kernel(table, s0, s1, s2, s3, o, grad, q, gain, *refs, own):
    d, states = refs[-2:]
    y = place()[2]
    sums = s0[...] + s1[...] + s2[...] + s3[...]
    r = lax.rsqrt(sums[0:1, :] * (1.0 / FEATURES) + 1e-06)
    inverse = jnp.broadcast_to(r, (HEAD, TOK)).T
    mean = jnp.broadcast_to(sums[4:5, :] * r * (1.0 / FEATURES), (HEAD, TOK)).T
    tail = 4 * HEAD

    def term(head, wide, normed):
        if not own:
            states[pl.ds(tail + head, 1), :] = jnp.sum(wide * normed, axis=0, keepdims=True)

    for j in range(4):
        head = first_head(own) + j
        local = slice(j * HEAD, (j + 1) * HEAD)
        normed = inverse * o[:, local]
        wide = grad[:, columns(head)].astype(F32)
        low = (inverse * (wide * gain[pl.ds(head, 1), :] - normed * mean)).astype(BF16)
        d[:, local] = low
        term(head, wide, normed)
        weights = enter_decay(table, head)
        states[columns(j ^ y), :] = mm_at((weights * q[:, columns(head)].astype(F32)).astype(BF16), low)
    if not own:
        for j in range(4):
            head = first_head(True) + j
            term(head, grad[:, columns(head)].astype(F32), inverse * refs[0][:, j * HEAD : (j + 1) * HEAD])


def grads_kernel(table, q, k, v, d, mask, flipped, states, after, dq, dk, dv, *, own, start):
    half = TOK // 2
    for n in range(2):
        j = start + n
        head = first_head(own) + j
        rate, at = rate_row(table, head), columns(head)
        out, local = slice(n * HEAD, (n + 1) * HEAD), slice(j * HEAD, (j + 1) * HEAD)
        state = state_of(states, j)
        up, down = powers(-rate, 0.0, True), powers(rate, 0.0, True)
        inside = jnp.where(token_rows() < table[ENTER : ENTER + 1, :], jnp.exp(rate), 0.0)
        v_up = (up * v[:, at].astype(F32)).astype(BF16)
        d_down = (down * d[:, local].astype(F32)).astype(BF16)
        q_down = (down * q[:, at].astype(F32)).astype(BF16)
        for lo in (0, half):
            hi = lo + half
            mixing = mm_bt(d[lo:hi, local], v_up[0:hi, :]).astype(BF16) * mask[lo:hi, 0:hi]
            grad = mm(mixing, k[0:hi, at]) + inside[lo:hi, :] * mm_bt(d[lo:hi, local], state)
            dq[lo:hi, out] = (down[lo:hi, :] * grad).astype(BF16)
            mixing = mm_bt(v[lo:hi, at], d_down[lo:TOK, :]).astype(BF16) * flipped[lo:hi, lo:TOK]
            dk[lo:hi, out] = up[lo:hi, :] * mm(mixing, q[lo:TOK, at])
            mixing = mm_bt(k[lo:hi, at], q_down[lo:TOK, :]).astype(BF16) * flipped[lo:hi, lo:TOK]
            dv[lo:hi, out] = up[lo:hi, :] * mm(mixing, d[lo:TOK, local])


def last_kernel(table, k, v, states, *refs, own):
    parts, buffers = refs[:4], refs[-3:]
    (dk, dv), sems = refs[-5:-3] if not own else refs[-6:-4], buffers[2]
    copies = []
    if own:
        dq = refs[-4]
        for n, part in enumerate(refs[4:8]):
            spot = pl.ds(pl.multiple_of((first_head(n < 2) + 2 * (n % 2)) * HEAD, 2 * HEAD), 2 * HEAD)
            copies.append(pltpu.make_async_copy(part, dq.at[:, spot], sems.at[2, n]))
            copies[-1].start()
    for j in range(4):
        head = first_head(own) + j
        at, local = columns(head), slice(j * HEAD, (j + 1) * HEAD)
        inner = slice(j % 2 * HEAD, (j % 2 + 1) * HEAD)
        weights = leave_decay(table, head)
        state = state_of(states, j)
        buffers[0][:, local] = (parts[j // 2][:, inner] + weights * mm_bt(v[:, at], state)).astype(BF16)
        copies.append(pltpu.make_async_copy(buffers[0].at[:, local], dk.at[:, at], sems.at[0, j]))
        copies[-1].start()
        buffers[1][:, local] = (parts[2 + j // 2][:, inner] + weights * mm(k[:, at], state)).astype(BF16)
        copies.append(pltpu.make_async_copy(buffers[1].at[:, local], dv.at[:, at], sems.at[1, j]))
        copies[-1].start()
    for copy in copies:
        copy.wait()


def index(z, y, c):
    return (z * 4 + y) * 2 + c


def exchange(array, dz=0, dy=0, dc=0):
    pairs = [
        (index(z, y, c), index(z ^ dz, y ^ dy, c ^ dc))
        for z in range(8)
        for y in range(4)
        for c in range(2)
    ]
    return lax.ppermute(array, "seq", pairs)


def carried(send, make_keep, table, base, reverse, gains, work):
    extra = 8 if gains else 0
    small = shape(HEAD + extra, HEAD)

    def step(kernel, outs, *args, after, base=base, **more):
        return call(
            functools.partial(kernel, reverse=reverse, base=base, **more),
            outs,
            in_specs=[VMEM] * (1 + len(args)) + [ANY],
            out_specs=jax.tree.map(lambda _: VMEM, outs),
            limit=8,
        )(table, *args, after)

    def around(arrays, ks, **axis):
        moved = {k: exchange(arrays[k], **{name: k for name in axis}) for k in ks}
        return [arrays[0]] + [moved[k] for k in (1, 2, 3)]

    got = exchange(send, dc=1)
    keep = make_keep(send)
    chips = step(chip_kernel, [small] * 4, keep, got, send, gains=gains, after=keep)
    done = work[0](chips[0])
    chips = around([chips[n] for n in SLOT], (2, 1, 3), dy=1)
    row = step(sum_kernel, small, *chips, gains=gains, after=done, base=base + ROW)
    done = work[1](row)
    rows = around([row] * 4, (1, 2, 3), dz=1)
    sent = step(sum_kernel, small, *rows, gains=gains, after=done, base=base + HALF)
    done = work[2](sent)
    far = exchange(sent, dz=FAR_Z)
    outs = [shape(HEAD, HEAD)] * 4 + ([shape(8, HEAD), shape(16)] if gains else [])
    outs = step(chips_in_kernel, outs, *rows[1:], far, sent, *chips, gains=gains, after=done)
    done = work[3](outs[0])
    states = around([outs[n] for n in SLOT], (2, 1, 3), dy=1)
    mine, other = step(cores_in_kernel, [shape(4 * HEAD, HEAD)] * 2, *states, keep, got, after=done)
    return mine, other, (outs[5] if gains else None)


def shards(queries, keys, values, out_grad, gain, decay, bounds):
    gain = gain.reshape(HEADS_DEV, HEAD)
    width = HEADS_DEV * HEAD
    half = width // 2
    small_mm = TOK * HEAD * HEAD * HEADS_DEV
    big_mm = 2 * TOK * TOK * HEAD * HEADS_DEV * 3 // 4
    state_shape = shape(4 * HEAD, HEAD)

    def local(kernel, outs, args, order=(), flops=0, moved=0, **more):
        return call(
            functools.partial(kernel, **more),
            outs,
            in_specs=[VMEM] * (1 + len(args)) + [ANY] * len(order),
            out_specs=jax.tree.map(lambda _: VMEM, outs),
            flops=flops,
            moved=moved,
        )(table, *args, *order)

    send, table = call(
        sent_states_kernel,
        [state_shape, shape(FORWARD + CHAIN_ROWS, HEAD)],
        in_specs=[ANY] * 4,
        out_specs=[VMEM] * 2,
        scratch=[pltpu.VMEM((4, TOK, HEAD), BF16)] * 2
        + [pltpu.SMEM((HEADS_DEV,), jnp.int32), pltpu.SMEM((3,), jnp.int32), pltpu.SemaphoreType.DMA((3, 4))],
        flops=small_mm,
        moved=3 << 19,
    )(*[pltpu.with_memory_space_constraint(x, pltpu.HBM) for x in (decay, bounds, keys, values)])

    def keep_states(after):
        return local(kept_states_kernel, state_shape, [keys, values], [after], small_mm, 3 << 19)

    made = {}
    pairs = shape(TOK, TOK, dtype=BF16)

    def make_intra(own):
        def run(after):
            if own:
                outs = [pairs] * 2 + [shape(CHAIN_ROWS, HEAD), shape(HEADS_DEV, HEAD)]
                made["masks"] = call(
                    masks_kernel,
                    outs,
                    in_specs=[SMEM, SMEM, VMEM, ANY],
                    out_specs=[VMEM] * 4,
                    moved=1 << 20,
                )(*[pltpu.with_memory_space_constraint(x, pltpu.HBM) for x in (decay, bounds)], gain, after)
            made[own] = local(
                intra_kernel,
                shape(TOK, half),
                [queries, keys, values, made["masks"][0]],
                [after],
                big_mm,
                3 << 20,
                own=own,
            )
            return made[own]

        return run

    def same(after):
        return after

    mine, other, _ = carried(
        send, keep_states, table, FORWARD, False, False, [make_intra(True), make_intra(False), same, same]
    )
    theirs = exchange(other, dc=1)
    mask, flipped, back_table, gain = made["masks"]
    sums = shape(8, TOK)
    outs = [shape(TOK, half), sums]
    o_mine, own_sums = local(
        attended_kernel, outs, [queries, made[True], out_grad, gain, mine], [other], small_mm, 3 << 20, own=True
    )
    o_other, sums = local(
        attended_kernel,
        outs,
        [queries, made[False], out_grad, gain, theirs, own_sums],
        [],
        small_mm,
        3 << 20,
        own=False,
    )
    totals = [sums] + [lax.ppermute(sums, "dp", [(i, i ^ k) for i in range(4)]) for k in (1, 2, 3)]
    outs = [shape(TOK, half, dtype=BF16), shape(4 * HEAD + 8, HEAD)]
    d_other, send = local(
        mixed_kernel,
        outs,
        [*totals, o_other, out_grad, queries, gain, o_mine],
        [],
        small_mm,
        3 << 20,
        own=False,
    )

    def keep_grads(after):
        outs = [shape(TOK, half, dtype=BF16), shape(4 * HEAD, HEAD)]
        made["d"], keep = local(
            mixed_kernel, outs, [*totals, o_mine, out_grad, queries, gain], [after], small_mm, 3 << 20, own=True
        )
        return keep


    def make_grads(n):
        def run(after):
            own = n < 2
            made["grads", n] = local(
                grads_kernel,
                [shape(TOK, 2 * HEAD, dtype=BF16), shape(TOK, 2 * HEAD), shape(TOK, 2 * HEAD)],
                [queries, keys, values, made["d"] if own else d_other, mask, flipped, mine if own else theirs],
                [after],
                6 * big_mm // 4,
                2 << 20,
                own=own,
                start=2 * (n % 2),
            )
            return made["grads", n][1]

        return run

    last_mine, last_other, gains = carried(
        send, keep_grads, back_table, BACKWARD, True, True, [make_grads(n) for n in range(4)]
    )
    last_theirs = exchange(last_other, dc=1)
    dq, dk, dv = zip(*[made["grads", n] for n in range(4)])
    full = shape(TOK, width, dtype=BF16)
    scratch = [pltpu.VMEM((TOK, half), BF16)] * 2 + [pltpu.SemaphoreType.DMA((3, 4))]
    dk_out, dv_out, dq_out = call(
        functools.partial(last_kernel, own=True),
        [full] * 3,
        in_specs=[VMEM] * 12 + [ANY],
        out_specs=[ANY] * 3,
        scratch=scratch,
        flops=2 * small_mm,
        moved=6 << 20,
    )(table, keys, values, last_mine, *dk[:2], *dv[:2], *dq, last_other)
    dk_out, dv_out = call(
        functools.partial(last_kernel, own=False),
        [full] * 2,
        in_specs=[VMEM] * 8 + [ANY] * 2,
        out_specs=[ANY] * 2,
        scratch=scratch,
        flops=2 * small_mm,
        moved=4 << 20,
        aliases={8: 0, 9: 1},
    )(table, keys, values, last_theirs, *dk[2:], *dv[2:], dk_out, dv_out)
    return dq_out, dk_out, dv_out, gains


def solution(mesh):
    return jax.shard_map(
        shards,
        mesh=mesh,
        in_specs=(
            P("seq", "dp"),
            P("seq", "dp"),
            P("seq", "dp"),
            P("seq", "dp"),
            P("dp"),
            P("dp"),
            P(),
        ),
        out_specs=(P("seq", "dp"), P("seq", "dp"), P("seq", "dp"), P(("dp", "seq"))),
        check_vma=False,
    )
```

```python
import functools
import math

import jax
import jax.numpy as jnp
from jax import lax
from jax.experimental import pallas as pl
from jax.experimental.pallas import tpu as pltpu
from jax.sharding import PartitionSpec as P

F32, BF16 = jnp.float32, jnp.bfloat16
HEAD, TOK, HEADS_DEV, STREAM, FEATURES = 128, 512, 8, 32768, 4096
BLOCK_Z, BLOCK_Y = 8 * TOK, 2 * TOK
SMEM = pl.BlockSpec(memory_space=pltpu.SMEM)
VMEM = pl.BlockSpec(memory_space=pltpu.VMEM)
ANY = pl.BlockSpec(memory_space=pl.ANY)


def rate_of(level):
    row = jnp.full((1, HEAD), level.astype(F32), F32)
    slow = jnp.exp(row * (math.log(8.0) / 7.0)) * (-0.25 / STREAM)
    lowest = math.log(4.0 / STREAM)
    fast = -jnp.exp(lowest + (row - 8.0) * ((math.log(1.0 / 32.0) - lowest) / 7.0))
    return jnp.where(row < 8.0, slow, fast)


def starts_before(bounds, place):
    return sum((bounds[i] < place).astype(jnp.int32) for i in range(3))


def carry(rate, bounds, left, right):
    same = (starts_before(bounds, left) == starts_before(bounds, right)) & (left <= right)
    span = jnp.maximum(right - left, 0).astype(F32)
    return jnp.exp(rate * span) * jnp.where(same, 1.0, 0.0).astype(F32)


def place():
    at = lax.axis_index("seq")
    return at, at // 8, (at // 2) % 4, at % 2


def tokens_in(bounds, at):
    first = at * TOK
    entering, leaving = TOK, 0
    for i in range(3):
        local = bounds[i] - first
        entering = jnp.where((local >= 0) & (local < entering), local, entering)
        leaving = jnp.where((local < TOK) & (local > leaving), local, leaving)
    return entering, leaving


def powers(rate, first, up):
    t = lax.broadcasted_iota(jnp.int32, (8, HEAD), 0)
    t = (t if up else 7 - t).astype(F32)
    rows, size = jnp.exp(rate * (t + first)), 8
    while size < TOK:
        more = rows * jnp.exp(rate * float(size))
        rows = jnp.concatenate([rows, more] if up else [more, rows], axis=0)
        size *= 2
    return rows


RATES, ENTER, LEAVE, FORWARD, BACKWARD = 0, 8, 9, 16, 0
CHIP_OWN, CHIP_OTHER, ROW, HALF, FAR, NEAR, INTO, ACROSS, CORE = 0, 4, 8, 12, 16, 16, 20, 24, 40
CHAIN_ROWS = 48
FAR_Z = 6
SLOT = (0, 2, 1, 3)


def token_rows():
    return lax.broadcasted_iota(jnp.int32, (TOK, HEAD), 0).astype(F32)


def rate_row(table, head):
    return table[pl.ds(head, 1), :]


def enter_decay(table, head):
    return jnp.where(token_rows() < table[ENTER : ENTER + 1, :], powers(rate_row(table, head), 1.0, True), 0.0)


def leave_decay(table, head):
    return jnp.where(token_rows() >= table[LEAVE : LEAVE + 1, :], powers(rate_row(table, head), 0.0, False), 0.0)


def fill_chain(table, base, decay, bounds, reverse):
    at, z, y, c = place()
    one = jnp.ones((1, HEAD), F32)
    middle = (at - c + 1) * TOK
    row, row_end, centre = z * BLOCK_Z, (z + 1) * BLOCK_Z, 4 * BLOCK_Z

    def put(index, value):
        table[base + index : base + index + 1, :] = value

    def across(rate, earlier, later):
        return carry(rate, bounds, earlier, later)

    for k in range(4):
        rate = rate_of(decay[4 * c + (y ^ k)])
        first, second = across(rate, middle - TOK, middle), across(rate, middle, middle + TOK)
        if reverse:
            put(CHIP_OWN + k, jnp.where(c == 1, first, one))
            put(CHIP_OTHER + k, jnp.where(c == 1, one, first))
            put(CORE + k, second)
        else:
            put(CHIP_OWN + k, jnp.where(c == 0, second, one))
            put(CHIP_OTHER + k, jnp.where(c == 0, one, second))
            put(CORE + k, first)
    rate = rate_of(decay[4 * c + y])
    for k in range(4):
        here, line = row + (y ^ k) * BLOCK_Y, (z ^ k) * BLOCK_Z
        if reverse:
            put(ROW + k, across(rate, row, here))
            put(HALF + k, across(rate, centre, line))
            put(NEAR + k, across(rate, row_end, line if k else centre))
            put(INTO + k, across(rate, here + BLOCK_Y, row_end))
        else:
            put(ROW + k, across(rate, here + BLOCK_Y, row_end))
            put(HALF + k, across(rate, line + BLOCK_Z, centre))
            put(NEAR + k, across(rate, line + BLOCK_Z if k else centre, row))
            put(INTO + k, across(rate, row, here))
        for m in range(4):
            if m != k:
                there = row + (y ^ m) * BLOCK_Y
                if reverse:
                    put(ACROSS + 4 * k + m, across(rate, here + BLOCK_Y, there))
                else:
                    put(ACROSS + 4 * k + m, across(rate, there + BLOCK_Y, here))


def masks_kernel(decay, bounds, gain, after, mask, flipped, table, gain_out):
    gain_out[...] = gain[...]
    fill_chain(table, BACKWARD, decay, bounds, True)
    first = place()[0] * TOK
    for lo in range(0, TOK, HEAD):
        row = lax.broadcasted_iota(jnp.int32, (HEAD, TOK), 0) + lo
        column = lax.broadcasted_iota(jnp.int32, (HEAD, TOK), 1)
        since = jnp.zeros((HEAD, TOK), jnp.int32)
        until = jnp.full((HEAD, TOK), TOK, jnp.int32)
        for i in range(3):
            local = bounds[i] - first
            since = jnp.where(row >= local, jnp.maximum(since, local), since)
            until = jnp.where(row < local, jnp.minimum(until, local), until)
        rows = slice(lo, lo + HEAD)
        mask[rows, :] = jnp.where((column <= row) & (column >= since), 1.0, 0.0).astype(BF16)
        flipped[rows, :] = jnp.where((column >= row) & (column < until), 1.0, 0.0).astype(BF16)


def mm(a, b):
    return lax.dot_general(a, b, (((1,), (0,)), ((), ())), preferred_element_type=F32)


def mm_bt(a, b):
    return lax.dot_general(a, b, (((1,), (1,)), ((), ())), preferred_element_type=F32)


def mm_at(a, b):
    return lax.dot_general(a, b, (((0,), (0,)), ((), ())), preferred_element_type=F32)


def call(kernel, outs, grid=None, in_specs=None, out_specs=None, scratch=(), flops=0, moved=0, limit=24, aliases={}):
    extra = {} if grid is None else {"grid": grid}
    return pl.pallas_call(
        kernel,
        out_shape=outs,
        in_specs=in_specs,
        out_specs=out_specs,
        scratch_shapes=list(scratch),
        input_output_aliases=aliases,
        compiler_params=pltpu.CompilerParams(vmem_limit_bytes=limit << 20),
        cost_estimate=pl.CostEstimate(flops=flops, bytes_accessed=moved, transcendentals=0),
        **extra,
    )


def shape(*dims, dtype=F32):
    return jax.ShapeDtypeStruct(dims, dtype)


def columns(index):
    return pl.ds(pl.multiple_of(index * HEAD, HEAD), HEAD)


def first_head(own):
    c = place()[3]
    return 4 * c if own else 4 * (1 - c)


def sent_states_kernel(decay_in, bounds_in, k_in, v_in, out, table, k, v, decay, bounds, sems):
    at, _, y, _ = place()
    heads = [first_head(False) + (y ^ i) for i in range(4)]
    rest = pl.ds(pl.multiple_of(first_head(True) * HEAD, 4 * HEAD), 4 * HEAD)

    def start(source, target, sem):
        copy = pltpu.make_async_copy(source, target, sem)
        copy.start()
        return copy

    numbers = [start(decay_in, decay, sems.at[2, 0]), start(bounds_in, bounds, sems.at[2, 1])]
    copies = []
    for i, head in enumerate(heads):
        spot = columns(head)
        copies.append(start(k_in.at[:, spot], k.at[:, spot], sems.at[0, i]))
        copies.append(start(v_in.at[:, spot], v.at[:, spot], sems.at[1, i]))
    halves = [start(k_in.at[:, rest], k.at[:, rest], sems.at[2, 2]), start(v_in.at[:, rest], v.at[:, rest], sems.at[2, 3])]
    for copy in numbers:
        copy.wait()
    for head in range(HEADS_DEV):
        table[RATES + head : RATES + head + 1, :] = rate_of(decay[head])
    entering, leaving = tokens_in(bounds, at)
    table[ENTER : ENTER + 1, :] = jnp.full((1, HEAD), entering.astype(F32), F32)
    table[LEAVE : LEAVE + 1, :] = jnp.full((1, HEAD), leaving.astype(F32), F32)
    fill_chain(table, FORWARD, decay, bounds, False)
    for i, head in enumerate(heads):
        weights = leave_decay(table, head)
        copies[2 * i].wait()
        copies[2 * i + 1].wait()
        decayed = (weights * k[:, columns(head)].astype(F32)).astype(BF16)
        out[i * HEAD : (i + 1) * HEAD, :] = mm_at(decayed, v[:, columns(head)])
    for copy in halves:
        copy.wait()


def kept_states_kernel(table, k, v, after, out):
    y = place()[2]
    for i in range(4):
        head = first_head(True) + (y ^ i)
        decayed = (leave_decay(table, head) * k[:, columns(head)].astype(F32)).astype(BF16)
        out[i * HEAD : (i + 1) * HEAD, :] = mm_at(decayed, v[:, columns(head)])


def intra_kernel(table, q, k, v, mask, after, out_ref, *, own):
    half = TOK // 2
    for j in range(4):
        head = first_head(own) + j
        rate, at = rate_row(table, head), columns(head)
        scaled = (powers(-rate, 0.0, True) * k[:, at].astype(F32)).astype(BF16)
        down = powers(rate, 0.0, True)
        for lo in (0, half):
            hi = lo + half
            mixing = mm_bt(q[lo:hi, at], scaled[0:hi, :]).astype(BF16) * mask[lo:hi, 0:hi]
            out_ref[lo:hi, j * HEAD : (j + 1) * HEAD] = down[lo:hi, :] * mm(mixing, v[0:hi, at])


def chip_kernel(table, keep, got, send, after, *outs, base, reverse, gains):
    for k in range(4):
        own, other = base + CHIP_OWN + k, base + CHIP_OTHER + k
        rows = slice(k * HEAD, (k + 1) * HEAD)
        outs[SLOT[k]][0:HEAD, :] = table[own : own + 1, :] * keep[rows, :] + table[other : other + 1, :] * got[rows, :]
        if gains:
            tail = slice(4 * HEAD, 4 * HEAD + 8)
            outs[SLOT[k]][HEAD : HEAD + 8, :] = send[tail, :] + got[tail, :]


def sum_kernel(table, p0, p1, p2, p3, after, out, *, base, reverse, gains):
    total = 0.0
    for k, p in enumerate((p0, p1, p2, p3)):
        total += table[base + k : base + k + 1, :] * p[0:HEAD, :]
    out[0:HEAD, :] = total
    if gains:
        tail = slice(HEAD, HEAD + 8)
        out[tail, :] = p0[tail, :] + p1[tail, :] + p2[tail, :] + p3[tail, :]


def chips_in_kernel(table, r1, r2, r3, far, sent, t0, t1, t2, t3, after, *outs, base, reverse, gains):
    total = table[base + FAR : base + FAR + 1, :] * far[0:HEAD, :]
    for k, r in enumerate((r1, r2, r3)):
        at = base + NEAR + 1 + k
        total += table[at : at + 1, :] * r[0:HEAD, :]
    for k in range(4):
        at = base + INTO + k
        state = table[at : at + 1, :] * total
        for m, t in enumerate((t0, t1, t2, t3)):
            if m != k:
                at = base + ACROSS + 4 * k + m
                state += table[at : at + 1, :] * t[0:HEAD, :]
        outs[SLOT[k]][...] = state
    if gains:
        tail = slice(HEAD, HEAD + 8)
        outs[4][...] = sent[tail, :] + far[tail, :]


def gains_kernel(totals, out):
    _, z, y, c = place()
    turned = pltpu.roll(totals[pl.ds(z, 1), :], (HEAD - 32 * y - 16 * c) % HEAD, axis=1)
    out[...] = turned[0, 0:16]


def cores_in_kernel(table, v0, v1, v2, v3, keep, got, *refs, base, reverse):
    mine, other = refs[-2:]
    c = place()[3]
    deep = c == 0 if reverse else c == 1
    for k, v in enumerate((v0, v1, v2, v3)):
        at = base + CORE + k
        rows = slice(k * HEAD, (k + 1) * HEAD)
        state = v[...]
        step = table[at : at + 1, :] * state
        mine[rows, :] = jnp.where(deep, step + got[rows, :], state)
        other[rows, :] = jnp.where(deep, state, step + keep[rows, :])


def state_of(states, j):
    return states[columns(j ^ place()[2]), :].astype(BF16)


def attended_kernel(table, q, intra, grad, gain, states, *refs, own):
    out_ref, sums = refs[-2:]
    square, cross = 0.0, 0.0
    for j in range(4):
        head = first_head(own) + j
        at, local = columns(head), slice(j * HEAD, (j + 1) * HEAD)
        weights = enter_decay(table, head)
        out = intra[:, local] + weights * mm(q[:, at], state_of(states, j))
        out_ref[:, local] = out
        square += out * out
        cross += out * (grad[:, at].astype(F32) * gain[pl.ds(head, 1), :])
    square = jnp.sum(square.T, axis=0, keepdims=True)
    cross = jnp.sum(cross.T, axis=0, keepdims=True)
    if not own:
        square += refs[0][0:1, :]
        cross += refs[0][4:5, :]
    sums[0:4, :] = jnp.broadcast_to(square, (4, TOK))
    sums[4:8, :] = jnp.broadcast_to(cross, (4, TOK))


def mixed_kernel(table, s0, s1, s2, s3, o, grad, q, gain, *refs, own):
    d, states = refs[-2:]
    y = place()[2]
    sums = s0[...] + s1[...] + s2[...] + s3[...]
    r = lax.rsqrt(sums[0:1, :] * (1.0 / FEATURES) + 1e-06)
    inverse = jnp.broadcast_to(r, (HEAD, TOK)).T
    mean = jnp.broadcast_to(sums[4:5, :] * r * (1.0 / FEATURES), (HEAD, TOK)).T
    tail = 4 * HEAD

    def term(head, wide, normed):
        if not own:
            states[pl.ds(tail + head, 1), :] = jnp.sum(wide * normed, axis=0, keepdims=True)

    for j in range(4):
        head = first_head(own) + j
        local = slice(j * HEAD, (j + 1) * HEAD)
        normed = inverse * o[:, local]
        wide = grad[:, columns(head)].astype(F32)
        low = (inverse * (wide * gain[pl.ds(head, 1), :] - normed * mean)).astype(BF16)
        d[:, local] = low
        term(head, wide, normed)
        weights = enter_decay(table, head)
        states[columns(j ^ y), :] = mm_at((weights * q[:, columns(head)].astype(F32)).astype(BF16), low)
    if not own:
        for j in range(4):
            head = first_head(True) + j
            term(head, grad[:, columns(head)].astype(F32), inverse * refs[0][:, j * HEAD : (j + 1) * HEAD])


def grads_kernel(table, q, k, v, d, mask, flipped, states, after, dq, dk, dv, *, own, start):
    half = TOK // 2
    for n in range(2):
        j = start + n
        head = first_head(own) + j
        rate, at = rate_row(table, head), columns(head)
        out, local = slice(n * HEAD, (n + 1) * HEAD), slice(j * HEAD, (j + 1) * HEAD)
        state = state_of(states, j)
        up, down = powers(-rate, 0.0, True), powers(rate, 0.0, True)
        inside = jnp.where(token_rows() < table[ENTER : ENTER + 1, :], jnp.exp(rate), 0.0)
        v_up = (up * v[:, at].astype(F32)).astype(BF16)
        d_down = (down * d[:, local].astype(F32)).astype(BF16)
        q_down = (down * q[:, at].astype(F32)).astype(BF16)
        for lo in (0, half):
            hi = lo + half
            mixing = mm_bt(d[lo:hi, local], v_up[0:hi, :]).astype(BF16) * mask[lo:hi, 0:hi]
            grad = mm(mixing, k[0:hi, at]) + inside[lo:hi, :] * mm_bt(d[lo:hi, local], state)
            dq[lo:hi, out] = (down[lo:hi, :] * grad).astype(BF16)
            mixing = mm_bt(v[lo:hi, at], d_down[lo:TOK, :]).astype(BF16) * flipped[lo:hi, lo:TOK]
            dk[lo:hi, out] = up[lo:hi, :] * mm(mixing, q[lo:TOK, at])
            mixing = mm_bt(k[lo:hi, at], q_down[lo:TOK, :]).astype(BF16) * flipped[lo:hi, lo:TOK]
            dv[lo:hi, out] = up[lo:hi, :] * mm(mixing, d[lo:TOK, local])


def last_kernel(table, k, v, states, *refs, own):
    parts, buffers = refs[:4], refs[-3:]
    (dk, dv), sems = refs[-5:-3] if not own else refs[-6:-4], buffers[2]
    copies = []
    if own:
        dq = refs[-4]
        for n, part in enumerate(refs[4:8]):
            spot = pl.ds(pl.multiple_of((first_head(n < 2) + 2 * (n % 2)) * HEAD, 2 * HEAD), 2 * HEAD)
            copies.append(pltpu.make_async_copy(part, dq.at[:, spot], sems.at[2, n]))
            copies[-1].start()
    for j in range(4):
        head = first_head(own) + j
        at, local = columns(head), slice(j * HEAD, (j + 1) * HEAD)
        inner = slice(j % 2 * HEAD, (j % 2 + 1) * HEAD)
        weights = leave_decay(table, head)
        state = state_of(states, j)
        buffers[0][:, local] = (parts[j // 2][:, inner] + weights * mm_bt(v[:, at], state)).astype(BF16)
        copies.append(pltpu.make_async_copy(buffers[0].at[:, local], dk.at[:, at], sems.at[0, j]))
        copies[-1].start()
        buffers[1][:, local] = (parts[2 + j // 2][:, inner] + weights * mm(k[:, at], state)).astype(BF16)
        copies.append(pltpu.make_async_copy(buffers[1].at[:, local], dv.at[:, at], sems.at[1, j]))
        copies[-1].start()
    for copy in copies:
        copy.wait()


def index(z, y, c):
    return (z * 4 + y) * 2 + c


def exchange(array, dz=0, dy=0, dc=0):
    pairs = [
        (index(z, y, c), index(z ^ dz, y ^ dy, c ^ dc))
        for z in range(8)
        for y in range(4)
        for c in range(2)
    ]
    return lax.ppermute(array, "seq", pairs)


def carried(send, make_keep, table, base, reverse, gains, work):
    extra = 8 if gains else 0
    small = shape(HEAD + extra, HEAD)

    def step(kernel, outs, *args, after, base=base, **more):
        return call(
            functools.partial(kernel, reverse=reverse, base=base, **more),
            outs,
            in_specs=[VMEM] * (1 + len(args)) + [ANY] * len(after),
            out_specs=jax.tree.map(lambda _: VMEM, outs),
            limit=8,
        )(table, *args, *after)

    def around(arrays, ks, **axis):
        moved = {k: exchange(arrays[k], **{name: k for name in axis}) for k in ks}
        return [arrays[0]] + [moved[k] for k in (1, 2, 3)]

    got = exchange(send, dc=1)
    keep = make_keep(send)
    chips = step(chip_kernel, [small] * 4, keep, got, send, gains=gains, after=[keep])
    done = work[0](chips[0])
    chips = around([chips[n] for n in SLOT], (2, 1, 3), dy=1)
    row = step(sum_kernel, small, *chips, gains=gains, after=[done], base=base + ROW)
    done = work[1](row)
    rows = around([row] * 4, (1, 2, 3), dz=1)
    sent = step(sum_kernel, small, *rows, gains=gains, after=[done], base=base + HALF)
    done = work[2](sent)
    far = exchange(sent, dz=FAR_Z)
    outs = [shape(HEAD, HEAD)] * 4 + ([shape(8, HEAD)] if gains else [])
    outs = step(chips_in_kernel, outs, *rows[1:], far, sent, *chips, gains=gains, after=[done])
    done = work[3](outs[0])
    states = around([outs[n] for n in SLOT], (2, 1, 3), dy=1)
    total = call(gains_kernel, shape(16), in_specs=[VMEM], out_specs=VMEM)(outs[4]) if gains else None
    mine, other = step(cores_in_kernel, [shape(4 * HEAD, HEAD)] * 2, *states, keep, got, after=[done] + [total] * gains)
    return mine, other, total


def shards(queries, keys, values, out_grad, gain, decay, bounds):
    gain = gain.reshape(HEADS_DEV, HEAD)
    width = HEADS_DEV * HEAD
    half = width // 2
    small_mm = TOK * HEAD * HEAD * HEADS_DEV
    big_mm = 2 * TOK * TOK * HEAD * HEADS_DEV * 3 // 4
    state_shape = shape(4 * HEAD, HEAD)

    def local(kernel, outs, args, order=(), flops=0, moved=0, **more):
        return call(
            functools.partial(kernel, **more),
            outs,
            in_specs=[VMEM] * (1 + len(args)) + [ANY] * len(order),
            out_specs=jax.tree.map(lambda _: VMEM, outs),
            flops=flops,
            moved=moved,
        )(table, *args, *order)

    wide = shape(TOK, width, dtype=BF16)
    send, table, keys, values = call(
        sent_states_kernel,
        [state_shape, shape(FORWARD + CHAIN_ROWS, HEAD), wide, wide],
        in_specs=[ANY] * 4,
        out_specs=[VMEM] * 4,
        scratch=[pltpu.SMEM((HEADS_DEV,), jnp.int32), pltpu.SMEM((3,), jnp.int32), pltpu.SemaphoreType.DMA((3, 4))],
        flops=small_mm,
        moved=3 << 19,
    )(*[pltpu.with_memory_space_constraint(x, pltpu.HBM) for x in (decay, bounds, keys, values)])

    def keep_states(after):
        return local(kept_states_kernel, state_shape, [keys, values], [after], small_mm, 3 << 19)

    made = {}
    pairs = shape(TOK, TOK, dtype=BF16)

    def make_intra(own):
        def run(after):
            if own:
                outs = [pairs] * 2 + [shape(CHAIN_ROWS, HEAD), shape(HEADS_DEV, HEAD)]
                made["masks"] = call(
                    masks_kernel,
                    outs,
                    in_specs=[SMEM, SMEM, VMEM, ANY],
                    out_specs=[VMEM] * 4,
                    moved=1 << 20,
                )(*[pltpu.with_memory_space_constraint(x, pltpu.HBM) for x in (decay, bounds)], gain, after)
            made[own] = local(
                intra_kernel,
                shape(TOK, half),
                [queries, keys, values, made["masks"][0]],
                [after],
                big_mm,
                3 << 20,
                own=own,
            )
            return made[own]

        return run

    def same(after):
        return after

    mine, other, _ = carried(
        send, keep_states, table, FORWARD, False, False, [make_intra(True), make_intra(False), same, same]
    )
    theirs = exchange(other, dc=1)
    mask, flipped, back_table, gain = made["masks"]
    sums = shape(8, TOK)
    outs = [shape(TOK, half), sums]
    o_mine, own_sums = local(
        attended_kernel, outs, [queries, made[True], out_grad, gain, mine], [other], small_mm, 3 << 20, own=True
    )
    o_other, sums = local(
        attended_kernel,
        outs,
        [queries, made[False], out_grad, gain, theirs, own_sums],
        [],
        small_mm,
        3 << 20,
        own=False,
    )
    totals = [sums] + [lax.ppermute(sums, "dp", [(i, i ^ k) for i in range(4)]) for k in (1, 2, 3)]
    outs = [shape(TOK, half, dtype=BF16), shape(4 * HEAD + 8, HEAD)]
    d_other, send = local(
        mixed_kernel,
        outs,
        [*totals, o_other, out_grad, queries, gain, o_mine],
        [],
        small_mm,
        3 << 20,
        own=False,
    )

    def keep_grads(after):
        outs = [shape(TOK, half, dtype=BF16), shape(4 * HEAD, HEAD)]
        made["d"], keep = local(
            mixed_kernel, outs, [*totals, o_mine, out_grad, queries, gain], [after], small_mm, 3 << 20, own=True
        )
        return keep


    def make_grads(n):
        def run(after):
            own = n < 2
            made["grads", n] = local(
                grads_kernel,
                [shape(TOK, 2 * HEAD, dtype=BF16), shape(TOK, 2 * HEAD), shape(TOK, 2 * HEAD)],
                [queries, keys, values, made["d"] if own else d_other, mask, flipped, mine if own else theirs],
                [after],
                6 * big_mm // 4,
                2 << 20,
                own=own,
                start=2 * (n % 2),
            )
            return made["grads", n][1]

        return run

    last_mine, last_other, gains = carried(
        send, keep_grads, back_table, BACKWARD, True, True, [make_grads(n) for n in range(4)]
    )
    last_theirs = exchange(last_other, dc=1)
    dq, dk, dv = zip(*[made["grads", n] for n in range(4)])
    full = shape(TOK, width, dtype=BF16)
    scratch = [pltpu.VMEM((TOK, half), BF16)] * 2 + [pltpu.SemaphoreType.DMA((3, 4))]
    dk_out, dv_out, dq_out = call(
        functools.partial(last_kernel, own=True),
        [full] * 3,
        in_specs=[VMEM] * 12 + [ANY],
        out_specs=[ANY] * 3,
        scratch=scratch,
        flops=2 * small_mm,
        moved=6 << 20,
    )(table, keys, values, last_mine, *dk[:2], *dv[:2], *dq, last_other)
    dk_out, dv_out = call(
        functools.partial(last_kernel, own=False),
        [full] * 2,
        in_specs=[VMEM] * 8 + [ANY] * 2,
        out_specs=[ANY] * 2,
        scratch=scratch,
        flops=2 * small_mm,
        moved=4 << 20,
        aliases={8: 0, 9: 1},
    )(table, keys, values, last_theirs, *dk[2:], *dv[2:], dk_out, dv_out)
    return dq_out, dk_out, dv_out, gains


def solution(mesh):
    return jax.shard_map(
        shards,
        mesh=mesh,
        in_specs=(
            P("seq", "dp"),
            P("seq", "dp"),
            P("seq", "dp"),
            P("seq", "dp"),
            P("dp"),
            P("dp"),
            P(),
        ),
        out_specs=(P("seq", "dp"), P("seq", "dp"), P("seq", "dp"), P(("dp", "seq"))),
        check_vma=False,
    )
```

```python
import functools
import math

import jax
import jax.numpy as jnp
from jax import lax
from jax.experimental import pallas as pl
from jax.experimental.pallas import tpu as pltpu
from jax.sharding import PartitionSpec as P

F32, BF16 = jnp.float32, jnp.bfloat16
HEAD, TOK, HEADS_DEV, STREAM, FEATURES = 128, 512, 8, 32768, 4096
BLOCK_Z, BLOCK_Y = 8 * TOK, 2 * TOK
SMEM = pl.BlockSpec(memory_space=pltpu.SMEM)
VMEM = pl.BlockSpec(memory_space=pltpu.VMEM)
ANY = pl.BlockSpec(memory_space=pl.ANY)


def rate_of(level):
    row = jnp.full((1, HEAD), level.astype(F32), F32)
    slow = jnp.exp(row * (math.log(8.0) / 7.0)) * (-0.25 / STREAM)
    lowest = math.log(4.0 / STREAM)
    fast = -jnp.exp(lowest + (row - 8.0) * ((math.log(1.0 / 32.0) - lowest) / 7.0))
    return jnp.where(row < 8.0, slow, fast)


def starts_before(edges, place):
    return sum(jnp.where(edge < place, 1.0, 0.0) for edge in edges)


def carry(rate, edges, left, right):
    left, right = left.astype(F32), right.astype(F32)
    same = (starts_before(edges, left) == starts_before(edges, right)) & (left <= right)
    return jnp.where(same, jnp.exp(rate * jnp.maximum(right - left, 0.0)), 0.0)


def place():
    at = lax.axis_index("seq")
    return at, at // 8, (at // 2) % 4, at % 2


def tokens_in(bounds, at):
    first = at * TOK
    entering, leaving = TOK, 0
    for i in range(3):
        local = bounds[i] - first
        entering = jnp.where((local >= 0) & (local < entering), local, entering)
        leaving = jnp.where((local < TOK) & (local > leaving), local, leaving)
    return entering, leaving


def powers(rate, first, up):
    t = lax.broadcasted_iota(jnp.int32, (8, HEAD), 0)
    t = (t if up else 7 - t).astype(F32)
    rows, size = jnp.exp(rate * (t + first)), 8
    while size < TOK:
        more = rows * jnp.exp(rate * float(size))
        rows = jnp.concatenate([rows, more] if up else [more, rows], axis=0)
        size *= 2
    return rows


RATES, ENTER, LEAVE, EDGES = 0, 8, 9, 10
CHIP_OWN, CHIP_OTHER, ROW, HALF, FAR, NEAR, INTO, ACROSS, CORE = 0, 4, 8, 12, 16, 16, 20, 24, 40
CHAIN_ROWS = 48
FAR_Z = 7
SLOT = (0, 2, 1, 3)


def token_rows():
    return lax.broadcasted_iota(jnp.int32, (TOK, HEAD), 0).astype(F32)


def rate_row(table, head):
    return table[pl.ds(head, 1), :]


def enter_decay(table, head):
    return jnp.where(token_rows() < table[ENTER : ENTER + 1, :], powers(rate_row(table, head), 1.0, True), 0.0)


def leave_decay(table, head):
    return jnp.where(token_rows() >= table[LEAVE : LEAVE + 1, :], powers(rate_row(table, head), 0.0, False), 0.0)


def fill_chain(out, table, reverse):
    at, z, y, c = place()
    one = jnp.ones((1, HEAD), F32)
    edges = [table[EDGES + i : EDGES + i + 1, :] for i in range(3)]
    middle = (at - c + 1) * TOK
    row, row_end, centre = z * BLOCK_Z, (z + 1) * BLOCK_Z, jnp.int32(4 * BLOCK_Z)

    def put(index, value):
        out[index : index + 1, :] = value

    def across(rate, earlier, later):
        return carry(rate, edges, earlier, later)

    for k in range(4):
        rate = rate_row(table, 4 * c + (y ^ k))
        first, second = across(rate, middle - TOK, middle), across(rate, middle, middle + TOK)
        if reverse:
            put(CHIP_OWN + k, jnp.where(c == 1, first, one))
            put(CHIP_OTHER + k, jnp.where(c == 1, one, first))
            put(CORE + k, second)
        else:
            put(CHIP_OWN + k, jnp.where(c == 0, second, one))
            put(CHIP_OTHER + k, jnp.where(c == 0, one, second))
            put(CORE + k, first)
    rate = rate_row(table, 4 * c + y)
    for k in range(4):
        here, line = row + (y ^ k) * BLOCK_Y, (z ^ k) * BLOCK_Z
        if reverse:
            put(ROW + k, across(rate, row, here))
            put(HALF + k, across(rate, centre, line))
            put(NEAR + k, across(rate, row_end, line if k else centre))
            put(INTO + k, across(rate, here + BLOCK_Y, row_end))
        else:
            put(ROW + k, across(rate, here + BLOCK_Y, row_end))
            put(HALF + k, across(rate, line + BLOCK_Z, centre))
            put(NEAR + k, across(rate, line + BLOCK_Z if k else centre, row))
            put(INTO + k, across(rate, row, here))
        for m in range(4):
            if m != k:
                there = row + (y ^ m) * BLOCK_Y
                if reverse:
                    put(ACROSS + 4 * k + m, across(rate, here + BLOCK_Y, there))
                else:
                    put(ACROSS + 4 * k + m, across(rate, there + BLOCK_Y, here))


def masks_kernel(bounds, table, gain, after, mask, flipped, chain, gain_out):
    gain_out[...] = gain[...]
    fill_chain(chain, table, True)
    first = place()[0] * TOK
    for lo in range(0, TOK, HEAD):
        row = lax.broadcasted_iota(jnp.int32, (HEAD, TOK), 0) + lo
        column = lax.broadcasted_iota(jnp.int32, (HEAD, TOK), 1)
        since = jnp.zeros((HEAD, TOK), jnp.int32)
        until = jnp.full((HEAD, TOK), TOK, jnp.int32)
        for i in range(3):
            local = bounds[i] - first
            since = jnp.where(row >= local, jnp.maximum(since, local), since)
            until = jnp.where(row < local, jnp.minimum(until, local), until)
        rows = slice(lo, lo + HEAD)
        mask[rows, :] = jnp.where((column <= row) & (column >= since), 1.0, 0.0).astype(BF16)
        flipped[rows, :] = jnp.where((column >= row) & (column < until), 1.0, 0.0).astype(BF16)


def mm(a, b):
    return lax.dot_general(a, b, (((1,), (0,)), ((), ())), preferred_element_type=F32)


def mm_bt(a, b):
    return lax.dot_general(a, b, (((1,), (1,)), ((), ())), preferred_element_type=F32)


def mm_at(a, b):
    return lax.dot_general(a, b, (((0,), (0,)), ((), ())), preferred_element_type=F32)


def call(kernel, outs, grid=None, in_specs=None, out_specs=None, scratch=(), flops=0, moved=0, limit=24, aliases={}):
    extra = {} if grid is None else {"grid": grid}
    return pl.pallas_call(
        kernel,
        out_shape=outs,
        in_specs=in_specs,
        out_specs=out_specs,
        scratch_shapes=list(scratch),
        input_output_aliases=aliases,
        compiler_params=pltpu.CompilerParams(vmem_limit_bytes=limit << 20),
        cost_estimate=pl.CostEstimate(flops=flops, bytes_accessed=moved, transcendentals=0),
        **extra,
    )


def shape(*dims, dtype=F32):
    return jax.ShapeDtypeStruct(dims, dtype)


def columns(index):
    return pl.ds(pl.multiple_of(index * HEAD, HEAD), HEAD)


def first_head(own):
    c = place()[3]
    return 4 * c if own else 4 * (1 - c)


def sent_states_kernel(decay_in, bounds_in, k_in, v_in, out, table, k, v, decay, bounds, sems):
    at, _, y, _ = place()
    heads = [first_head(False) + (y ^ i) for i in range(4)]
    rest = pl.ds(pl.multiple_of(first_head(True) * HEAD, 4 * HEAD), 4 * HEAD)

    def start(source, target, sem):
        copy = pltpu.make_async_copy(source, target, sem)
        copy.start()
        return copy

    numbers = [start(decay_in, decay, sems.at[2, 0]), start(bounds_in, bounds, sems.at[2, 1])]
    copies = []
    for i, head in enumerate(heads):
        spot = columns(head)
        copies.append(start(k_in.at[:, spot], k.at[:, spot], sems.at[0, i]))
        copies.append(start(v_in.at[:, spot], v.at[:, spot], sems.at[1, i]))
    halves = [start(k_in.at[:, rest], k.at[:, rest], sems.at[2, 2]), start(v_in.at[:, rest], v.at[:, rest], sems.at[2, 3])]
    for copy in numbers:
        copy.wait()
    for head in range(HEADS_DEV):
        table[RATES + head : RATES + head + 1, :] = rate_of(decay[head])
    entering, leaving = tokens_in(bounds, at)
    table[ENTER : ENTER + 1, :] = jnp.full((1, HEAD), entering.astype(F32), F32)
    table[LEAVE : LEAVE + 1, :] = jnp.full((1, HEAD), leaving.astype(F32), F32)
    for i in range(3):
        table[EDGES + i : EDGES + i + 1, :] = jnp.full((1, HEAD), bounds[i].astype(F32), F32)
    for i, head in enumerate(heads):
        weights = leave_decay(table, head)
        copies[2 * i].wait()
        copies[2 * i + 1].wait()
        decayed = (weights * k[:, columns(head)].astype(F32)).astype(BF16)
        out[i * HEAD : (i + 1) * HEAD, :] = mm_at(decayed, v[:, columns(head)])
    for copy in halves:
        copy.wait()


def kept_states_kernel(table, k, v, after, out, chain):
    fill_chain(chain, table, False)
    y = place()[2]
    for i in range(4):
        head = first_head(True) + (y ^ i)
        decayed = (leave_decay(table, head) * k[:, columns(head)].astype(F32)).astype(BF16)
        out[i * HEAD : (i + 1) * HEAD, :] = mm_at(decayed, v[:, columns(head)])


def intra_kernel(table, q, k, v, mask, after, out_ref, *, own):
    half = TOK // 2
    for j in range(4):
        head = first_head(own) + j
        rate, at = rate_row(table, head), columns(head)
        scaled = (powers(-rate, 0.0, True) * k[:, at].astype(F32)).astype(BF16)
        down = powers(rate, 0.0, True)
        for lo in (0, half):
            hi = lo + half
            mixing = mm_bt(q[lo:hi, at], scaled[0:hi, :]).astype(BF16) * mask[lo:hi, 0:hi]
            out_ref[lo:hi, j * HEAD : (j + 1) * HEAD] = down[lo:hi, :] * mm(mixing, v[0:hi, at])


def chip_kernel(table, keep, got, send, after, *outs, base, reverse, gains):
    for k in range(4):
        own, other = base + CHIP_OWN + k, base + CHIP_OTHER + k
        rows = slice(k * HEAD, (k + 1) * HEAD)
        outs[SLOT[k]][0:HEAD, :] = table[own : own + 1, :] * keep[rows, :] + table[other : other + 1, :] * got[rows, :]
        if gains:
            tail = slice(4 * HEAD, 4 * HEAD + 8)
            outs[SLOT[k]][HEAD : HEAD + 8, :] = send[tail, :] + got[tail, :]


def sum_kernel(table, p0, p1, p2, p3, after, out, *tails, base, reverse, gains):
    total = 0.0
    for k, p in enumerate((p0, p1, p2, p3)):
        total += table[base + k : base + k + 1, :] * p[0:HEAD, :]
    out[0:HEAD, :] = total
    if gains:
        tail = slice(HEAD, HEAD + 8)
        out[tail, :] = p0[tail, :] + p1[tail, :] + p2[tail, :] + p3[tail, :]
        for copy in tails:
            copy[...] = out[tail, :]


def chips_in_kernel(table, r1, r2, r3, far, t0, t1, t2, t3, after, *outs, base, reverse):
    total = table[base + FAR : base + FAR + 1, :] * far[0:HEAD, :]
    for k, r in enumerate((r1, r2, r3)):
        at = base + NEAR + 1 + k
        total += table[at : at + 1, :] * r[0:HEAD, :]
    for k in range(4):
        at = base + INTO + k
        state = table[at : at + 1, :] * total
        for m, t in enumerate((t0, t1, t2, t3)):
            if m != k:
                at = base + ACROSS + 4 * k + m
                state += table[at : at + 1, :] * t[0:HEAD, :]
        outs[SLOT[k]][...] = state


def gains_kernel(own, far, back, after, out, totals):
    _, z, y, c = place()
    totals[...] = own[...] + far[HEAD : HEAD + 8, :] + back[...]
    turned = pltpu.roll(totals[pl.ds(z, 1), :], (HEAD - 32 * y - 16 * c) % HEAD, axis=1)
    out[...] = turned[0, 0:16]


def cores_in_kernel(table, v0, v1, v2, v3, keep, got, *refs, base, reverse):
    mine, other = refs[-2:]
    c = place()[3]
    deep = c == 0 if reverse else c == 1
    for k, v in enumerate((v0, v1, v2, v3)):
        at = base + CORE + k
        rows = slice(k * HEAD, (k + 1) * HEAD)
        state = v[...]
        step = table[at : at + 1, :] * state
        mine[rows, :] = jnp.where(deep, step + got[rows, :], state)
        other[rows, :] = jnp.where(deep, state, step + keep[rows, :])


def state_of(states, j):
    return states[columns(j ^ place()[2]), :].astype(BF16)


def attended_kernel(table, q, intra, grad, gain, states, *refs, own):
    out_ref, sums = refs[-2:]
    square, cross = 0.0, 0.0
    for j in range(4):
        head = first_head(own) + j
        at, local = columns(head), slice(j * HEAD, (j + 1) * HEAD)
        weights = enter_decay(table, head)
        out = intra[:, local] + weights * mm(q[:, at], state_of(states, j))
        out_ref[:, local] = out
        square += out * out
        cross += out * (grad[:, at].astype(F32) * gain[pl.ds(head, 1), :])
    square = jnp.sum(square.T, axis=0, keepdims=True)
    cross = jnp.sum(cross.T, axis=0, keepdims=True)
    if not own:
        square += refs[0][0:1, :]
        cross += refs[0][4:5, :]
    sums[0:4, :] = jnp.broadcast_to(square, (4, TOK))
    sums[4:8, :] = jnp.broadcast_to(cross, (4, TOK))


def mixed_kernel(table, s0, s1, s2, s3, o, grad, q, gain, *refs, own):
    d, states = refs[-2:]
    y = place()[2]
    sums = s0[...] + s1[...] + s2[...] + s3[...]
    r = lax.rsqrt(sums[0:1, :] * (1.0 / FEATURES) + 1e-06)
    inverse = jnp.broadcast_to(r, (HEAD, TOK)).T
    mean = jnp.broadcast_to(sums[4:5, :] * r * (1.0 / FEATURES), (HEAD, TOK)).T
    tail = 4 * HEAD

    def term(head, wide, normed):
        if not own:
            states[pl.ds(tail + head, 1), :] = jnp.sum(wide * normed, axis=0, keepdims=True)

    for j in range(4):
        head = first_head(own) + j
        local = slice(j * HEAD, (j + 1) * HEAD)
        normed = inverse * o[:, local]
        wide = grad[:, columns(head)].astype(F32)
        low = (inverse * (wide * gain[pl.ds(head, 1), :] - normed * mean)).astype(BF16)
        d[:, local] = low
        term(head, wide, normed)
        weights = enter_decay(table, head)
        states[columns(j ^ y), :] = mm_at((weights * q[:, columns(head)].astype(F32)).astype(BF16), low)
    if not own:
        for j in range(4):
            head = first_head(True) + j
            term(head, grad[:, columns(head)].astype(F32), inverse * refs[0][:, j * HEAD : (j + 1) * HEAD])


def grads_kernel(table, q, k, v, d, mask, flipped, states, after, dq, dk, dv, *, own, start):
    half = TOK // 2
    for n in range(2):
        j = start + n
        head = first_head(own) + j
        rate, at = rate_row(table, head), columns(head)
        out, local = slice(n * HEAD, (n + 1) * HEAD), slice(j * HEAD, (j + 1) * HEAD)
        state = state_of(states, j)
        up, down = powers(-rate, 0.0, True), powers(rate, 0.0, True)
        inside = jnp.where(token_rows() < table[ENTER : ENTER + 1, :], jnp.exp(rate), 0.0)
        v_up = (up * v[:, at].astype(F32)).astype(BF16)
        d_down = (down * d[:, local].astype(F32)).astype(BF16)
        q_down = (down * q[:, at].astype(F32)).astype(BF16)
        for lo in (0, half):
            hi = lo + half
            mixing = mm_bt(d[lo:hi, local], v_up[0:hi, :]).astype(BF16) * mask[lo:hi, 0:hi]
            grad = mm(mixing, k[0:hi, at]) + inside[lo:hi, :] * mm_bt(d[lo:hi, local], state)
            dq[lo:hi, out] = (down[lo:hi, :] * grad).astype(BF16)
            mixing = mm_bt(v[lo:hi, at], d_down[lo:TOK, :]).astype(BF16) * flipped[lo:hi, lo:TOK]
            dk[lo:hi, out] = up[lo:hi, :] * mm(mixing, q[lo:TOK, at])
            mixing = mm_bt(k[lo:hi, at], q_down[lo:TOK, :]).astype(BF16) * flipped[lo:hi, lo:TOK]
            dv[lo:hi, out] = up[lo:hi, :] * mm(mixing, d[lo:TOK, local])


def last_kernel(table, k, v, states, *refs, own):
    parts, buffers = refs[:4], refs[-3:]
    (dk, dv), sems = refs[-5:-3] if not own else refs[-6:-4], buffers[2]
    copies = []
    if own:
        dq = refs[-4]
        for n, part in enumerate(refs[4:8]):
            spot = pl.ds(pl.multiple_of((first_head(n < 2) + 2 * (n % 2)) * HEAD, 2 * HEAD), 2 * HEAD)
            copies.append(pltpu.make_async_copy(part, dq.at[:, spot], sems.at[2, n]))
            copies[-1].start()
    for j in range(4):
        head = first_head(own) + j
        at, local = columns(head), slice(j * HEAD, (j + 1) * HEAD)
        inner = slice(j % 2 * HEAD, (j % 2 + 1) * HEAD)
        weights = leave_decay(table, head)
        state = state_of(states, j)
        buffers[0][:, local] = (parts[j // 2][:, inner] + weights * mm_bt(v[:, at], state)).astype(BF16)
        copies.append(pltpu.make_async_copy(buffers[0].at[:, local], dk.at[:, at], sems.at[0, j]))
        copies[-1].start()
        buffers[1][:, local] = (parts[2 + j // 2][:, inner] + weights * mm(k[:, at], state)).astype(BF16)
        copies.append(pltpu.make_async_copy(buffers[1].at[:, local], dv.at[:, at], sems.at[1, j]))
        copies[-1].start()
    for copy in copies:
        copy.wait()


def index(z, y, c):
    return (z * 4 + y) * 2 + c


def exchange(array, dz=0, dy=0, dc=0):
    pairs = [
        (index(z, y, c), index(z ^ dz, y ^ dy, c ^ dc))
        for z in range(8)
        for y in range(4)
        for c in range(2)
    ]
    return lax.ppermute(array, "seq", pairs)


def one_way(array, dz, up):
    pairs = [
        (index(z, y, c), index(z ^ dz, y, c))
        for z in range(8)
        for y in range(4)
        for c in range(2)
        if ((z ^ dz) > z) == up
    ]
    return lax.ppermute(array, "seq", pairs)


def carried(send, make_keep, reverse, gains, work):
    extra = 8 if gains else 0
    small = shape(HEAD + extra, HEAD)

    def step(kernel, outs, *args, after, base=0, **more):
        return call(
            functools.partial(kernel, reverse=reverse, base=base, **more),
            outs,
            in_specs=[VMEM] * (1 + len(args)) + [ANY] * len(after),
            out_specs=jax.tree.map(lambda _: VMEM, outs),
            limit=8,
        )(table, *args, *after)

    def around(arrays, ks, **axis):
        moved = {k: exchange(arrays[k], **{name: k for name in axis}) for k in ks}
        return [arrays[0]] + [moved[k] for k in (1, 2, 3)]

    got = exchange(send, dc=1)
    keep, table = make_keep(send)
    chips = step(chip_kernel, [small] * 4, keep, got, send, gains=gains, after=[keep])
    done = work[0](chips[0])
    chips = around([chips[n] for n in SLOT], (2, 1, 3), dy=1)
    row = step(sum_kernel, [small], *chips, gains=gains, after=[done], base=ROW)[0]
    done = work[1](row)
    rows = around([row] * 4, (1, 2, 3), dz=1)
    outs = [small] + ([shape(8, HEAD)] if gains else [])
    sent = step(sum_kernel, outs, *rows, gains=gains, after=[done], base=HALF)
    done = work[2](sent[0])
    far = [one_way(sent[0], FAR_Z, not reverse)] + [one_way(tail, FAR_Z, reverse) for tail in sent[1:]]
    outs = [shape(HEAD, HEAD)] * 4
    outs = step(chips_in_kernel, outs, *rows[1:], far[0], *chips, after=[done])
    done = work[3](outs[0])
    states = around([outs[n] for n in SLOT], (2, 1, 3), dy=1)
    total = None
    if gains:
        total = call(
            gains_kernel,
            shape(16),
            in_specs=[VMEM] * 3 + [ANY],
            out_specs=VMEM,
            scratch=[pltpu.VMEM((8, HEAD), F32)],
        )(sent[1], *far, done)
    mine, other = step(cores_in_kernel, [shape(4 * HEAD, HEAD)] * 2, *states, keep, got, after=[done] + [total] * gains)
    return mine, other, total


def shards(queries, keys, values, out_grad, gain, decay, bounds):
    gain = gain.reshape(HEADS_DEV, HEAD)
    width = HEADS_DEV * HEAD
    half = width // 2
    small_mm = TOK * HEAD * HEAD * HEADS_DEV
    big_mm = 2 * TOK * TOK * HEAD * HEADS_DEV * 3 // 4
    state_shape = shape(4 * HEAD, HEAD)

    def local(kernel, outs, args, order=(), flops=0, moved=0, **more):
        return call(
            functools.partial(kernel, **more),
            outs,
            in_specs=[VMEM] * (1 + len(args)) + [ANY] * len(order),
            out_specs=jax.tree.map(lambda _: VMEM, outs),
            flops=flops,
            moved=moved,
        )(table, *args, *order)

    wide = shape(TOK, width, dtype=BF16)
    send, table, keys, values = call(
        sent_states_kernel,
        [state_shape, shape(16, HEAD), wide, wide],
        in_specs=[ANY] * 4,
        out_specs=[VMEM] * 4,
        scratch=[pltpu.SMEM((HEADS_DEV,), jnp.int32), pltpu.SMEM((3,), jnp.int32), pltpu.SemaphoreType.DMA((3, 4))],
        flops=small_mm,
        moved=3 << 19,
    )(*[pltpu.with_memory_space_constraint(x, pltpu.HBM) for x in (decay, bounds, keys, values)])

    def keep_states(after):
        outs = [state_shape, shape(CHAIN_ROWS, HEAD)]
        return local(kept_states_kernel, outs, [keys, values], [after], small_mm, 3 << 19)

    made = {}
    pairs = shape(TOK, TOK, dtype=BF16)

    def make_intra(own):
        def run(after):
            if own:
                outs = [pairs] * 2 + [shape(CHAIN_ROWS, HEAD), shape(HEADS_DEV, HEAD)]
                made["masks"] = call(
                    masks_kernel,
                    outs,
                    in_specs=[SMEM, VMEM, VMEM, ANY],
                    out_specs=[VMEM] * 4,
                    moved=1 << 20,
                )(pltpu.with_memory_space_constraint(bounds, pltpu.HBM), table, gain, after)
            made[own] = local(
                intra_kernel,
                shape(TOK, half),
                [queries, keys, values, made["masks"][0]],
                [after],
                big_mm,
                3 << 20,
                own=own,
            )
            return made[own]

        return run

    def same(after):
        return after

    mine, other, _ = carried(
        send, keep_states, False, False, [make_intra(True), make_intra(False), same, same]
    )
    theirs = exchange(other, dc=1)
    mask, flipped, back_table, gain = made["masks"]
    sums = shape(8, TOK)
    outs = [shape(TOK, half), sums]
    o_mine, own_sums = local(
        attended_kernel, outs, [queries, made[True], out_grad, gain, mine], [other], small_mm, 3 << 20, own=True
    )
    o_other, sums = local(
        attended_kernel,
        outs,
        [queries, made[False], out_grad, gain, theirs, own_sums],
        [],
        small_mm,
        3 << 20,
        own=False,
    )
    totals = [sums] + [lax.ppermute(sums, "dp", [(i, i ^ k) for i in range(4)]) for k in (1, 2, 3)]
    outs = [shape(TOK, half, dtype=BF16), shape(4 * HEAD + 8, HEAD)]
    d_other, send = local(
        mixed_kernel,
        outs,
        [*totals, o_other, out_grad, queries, gain, o_mine],
        [],
        small_mm,
        3 << 20,
        own=False,
    )

    def keep_grads(after):
        outs = [shape(TOK, half, dtype=BF16), shape(4 * HEAD, HEAD)]
        made["d"], keep = local(
            mixed_kernel, outs, [*totals, o_mine, out_grad, queries, gain], [after], small_mm, 3 << 20, own=True
        )
        return keep, back_table


    def make_grads(n):
        def run(after):
            own = n < 2
            made["grads", n] = local(
                grads_kernel,
                [shape(TOK, 2 * HEAD, dtype=BF16), shape(TOK, 2 * HEAD), shape(TOK, 2 * HEAD)],
                [queries, keys, values, made["d"] if own else d_other, mask, flipped, mine if own else theirs],
                [after],
                6 * big_mm // 4,
                2 << 20,
                own=own,
                start=2 * (n % 2),
            )
            return made["grads", n][1]

        return run

    last_mine, last_other, gains = carried(
        send, keep_grads, True, True, [make_grads(n) for n in range(4)]
    )
    last_theirs = exchange(last_other, dc=1)
    dq, dk, dv = zip(*[made["grads", n] for n in range(4)])
    full = shape(TOK, width, dtype=BF16)
    scratch = [pltpu.VMEM((TOK, half), BF16)] * 2 + [pltpu.SemaphoreType.DMA((3, 4))]
    dk_out, dv_out, dq_out = call(
        functools.partial(last_kernel, own=True),
        [full] * 3,
        in_specs=[VMEM] * 12 + [ANY],
        out_specs=[ANY] * 3,
        scratch=scratch,
        flops=2 * small_mm,
        moved=6 << 20,
    )(table, keys, values, last_mine, *dk[:2], *dv[:2], *dq, last_other)
    dk_out, dv_out = call(
        functools.partial(last_kernel, own=False),
        [full] * 2,
        in_specs=[VMEM] * 8 + [ANY] * 2,
        out_specs=[ANY] * 2,
        scratch=scratch,
        flops=2 * small_mm,
        moved=4 << 20,
        aliases={8: 0, 9: 1},
    )(table, keys, values, last_theirs, *dk[2:], *dv[2:], dk_out, dv_out)
    return dq_out, dk_out, dv_out, gains


def solution(mesh):
    return jax.shard_map(
        shards,
        mesh=mesh,
        in_specs=(
            P("seq", "dp"),
            P("seq", "dp"),
            P("seq", "dp"),
            P("seq", "dp"),
            P("dp"),
            P("dp"),
            P(),
        ),
        out_specs=(P("seq", "dp"), P("seq", "dp"), P("seq", "dp"), P(("dp", "seq"))),
        check_vma=False,
    )
```

```python
import functools
import math

import jax
import jax.numpy as jnp
from jax import lax
from jax.experimental import pallas as pl
from jax.experimental.pallas import tpu as pltpu
from jax.sharding import PartitionSpec as P

F32, BF16 = jnp.float32, jnp.bfloat16
HEAD, TOK, HEADS_DEV, STREAM, FEATURES = 128, 512, 8, 32768, 4096
BLOCK_Z, BLOCK_Y = 8 * TOK, 2 * TOK
SMEM = pl.BlockSpec(memory_space=pltpu.SMEM)
VMEM = pl.BlockSpec(memory_space=pltpu.VMEM)
ANY = pl.BlockSpec(memory_space=pl.ANY)


def rate_of(level):
    row = jnp.full((1, HEAD), level.astype(F32), F32)
    slow = jnp.exp(row * (math.log(8.0) / 7.0)) * (-0.25 / STREAM)
    lowest = math.log(4.0 / STREAM)
    fast = -jnp.exp(lowest + (row - 8.0) * ((math.log(1.0 / 32.0) - lowest) / 7.0))
    return jnp.where(row < 8.0, slow, fast)


def starts_before(bounds, place):
    return sum((bounds[i] < place).astype(jnp.int32) for i in range(3))


def carry(rate, bounds, left, right):
    same = (starts_before(bounds, left) == starts_before(bounds, right)) & (left <= right)
    span = jnp.maximum(right - left, 0).astype(F32)
    return jnp.exp(rate * span) * jnp.where(same, 1.0, 0.0).astype(F32)


def place():
    at = lax.axis_index("seq")
    return at, at // 8, (at // 2) % 4, at % 2


def tokens_in(bounds, at):
    first = at * TOK
    entering, leaving = TOK, 0
    for i in range(3):
        local = bounds[i] - first
        entering = jnp.where((local >= 0) & (local < entering), local, entering)
        leaving = jnp.where((local < TOK) & (local > leaving), local, leaving)
    return entering, leaving


def powers(rate, first, up):
    t = lax.broadcasted_iota(jnp.int32, (8, HEAD), 0)
    t = (t if up else 7 - t).astype(F32)
    rows, size = jnp.exp(rate * (t + first)), 8
    while size < TOK:
        more = rows * jnp.exp(rate * float(size))
        rows = jnp.concatenate([rows, more] if up else [more, rows], axis=0)
        size *= 2
    return rows


RATES, ENTER, LEAVE, FORWARD, BACKWARD = 0, 8, 9, 16, 0
CHIP_OWN, CHIP_OTHER, ROW, HALF, FAR, NEAR, INTO, ACROSS, CORE = 0, 4, 8, 12, 16, 16, 20, 24, 40
CHAIN_ROWS = 48
FAR_Z = 6
SLOT = (0, 2, 1, 3)


def token_rows():
    return lax.broadcasted_iota(jnp.int32, (TOK, HEAD), 0).astype(F32)


def rate_row(table, head):
    return table[pl.ds(head, 1), :]


def enter_decay(table, head):
    return jnp.where(token_rows() < table[ENTER : ENTER + 1, :], powers(rate_row(table, head), 1.0, True), 0.0)


def leave_decay(table, head):
    return jnp.where(token_rows() >= table[LEAVE : LEAVE + 1, :], powers(rate_row(table, head), 0.0, False), 0.0)


def fill_chain(table, base, decay, bounds, reverse):
    at, z, y, c = place()
    one = jnp.ones((1, HEAD), F32)
    middle = (at - c + 1) * TOK
    row, row_end, centre = z * BLOCK_Z, (z + 1) * BLOCK_Z, 4 * BLOCK_Z

    def put(index, value):
        table[base + index : base + index + 1, :] = value

    def across(rate, earlier, later):
        return carry(rate, bounds, earlier, later)

    for k in range(4):
        rate = rate_of(decay[4 * c + (y ^ k)])
        first, second = across(rate, middle - TOK, middle), across(rate, middle, middle + TOK)
        if reverse:
            put(CHIP_OWN + k, jnp.where(c == 1, first, one))
            put(CHIP_OTHER + k, jnp.where(c == 1, one, first))
            put(CORE + k, second)
        else:
            put(CHIP_OWN + k, jnp.where(c == 0, second, one))
            put(CHIP_OTHER + k, jnp.where(c == 0, one, second))
            put(CORE + k, first)
    rate = rate_of(decay[4 * c + y])
    for k in range(4):
        here, line = row + (y ^ k) * BLOCK_Y, (z ^ k) * BLOCK_Z
        if reverse:
            put(ROW + k, across(rate, row, here))
            put(HALF + k, across(rate, centre, line))
            put(NEAR + k, across(rate, row_end, line if k else centre))
            put(INTO + k, across(rate, here + BLOCK_Y, row_end))
        else:
            put(ROW + k, across(rate, here + BLOCK_Y, row_end))
            put(HALF + k, across(rate, line + BLOCK_Z, centre))
            put(NEAR + k, across(rate, line + BLOCK_Z if k else centre, row))
            put(INTO + k, across(rate, row, here))
        for m in range(4):
            if m != k:
                there = row + (y ^ m) * BLOCK_Y
                if reverse:
                    put(ACROSS + 4 * k + m, across(rate, here + BLOCK_Y, there))
                else:
                    put(ACROSS + 4 * k + m, across(rate, there + BLOCK_Y, here))


def masks_kernel(decay, bounds, gain, after, mask, flipped, table, gain_out):
    gain_out[...] = gain[...]
    fill_chain(table, BACKWARD, decay, bounds, True)
    first = place()[0] * TOK
    for lo in range(0, TOK, HEAD):
        row = lax.broadcasted_iota(jnp.int32, (HEAD, TOK), 0) + lo
        column = lax.broadcasted_iota(jnp.int32, (HEAD, TOK), 1)
        since = jnp.zeros((HEAD, TOK), jnp.int32)
        until = jnp.full((HEAD, TOK), TOK, jnp.int32)
        for i in range(3):
            local = bounds[i] - first
            since = jnp.where(row >= local, jnp.maximum(since, local), since)
            until = jnp.where(row < local, jnp.minimum(until, local), until)
        rows = slice(lo, lo + HEAD)
        mask[rows, :] = jnp.where((column <= row) & (column >= since), 1.0, 0.0).astype(BF16)
        flipped[rows, :] = jnp.where((column >= row) & (column < until), 1.0, 0.0).astype(BF16)


def mm(a, b):
    return lax.dot_general(a, b, (((1,), (0,)), ((), ())), preferred_element_type=F32)


def mm_bt(a, b):
    return lax.dot_general(a, b, (((1,), (1,)), ((), ())), preferred_element_type=F32)


def mm_at(a, b):
    return lax.dot_general(a, b, (((0,), (0,)), ((), ())), preferred_element_type=F32)


def call(kernel, outs, grid=None, in_specs=None, out_specs=None, scratch=(), flops=0, moved=0, limit=24, aliases={}):
    extra = {} if grid is None else {"grid": grid}
    return pl.pallas_call(
        kernel,
        out_shape=outs,
        in_specs=in_specs,
        out_specs=out_specs,
        scratch_shapes=list(scratch),
        input_output_aliases=aliases,
        compiler_params=pltpu.CompilerParams(vmem_limit_bytes=limit << 20),
        cost_estimate=pl.CostEstimate(flops=flops, bytes_accessed=moved, transcendentals=0),
        **extra,
    )


def shape(*dims, dtype=F32):
    return jax.ShapeDtypeStruct(dims, dtype)


def columns(index):
    return pl.ds(pl.multiple_of(index * HEAD, HEAD), HEAD)


def first_head(own):
    c = place()[3]
    return 4 * c if own else 4 * (1 - c)


def sent_states_kernel(decay_in, bounds_in, k_in, v_in, out, table, k, v, decay, bounds, sems):
    at, _, y, _ = place()
    heads = [first_head(False) + (y ^ i) for i in range(4)]
    rest = pl.ds(pl.multiple_of(first_head(True) * HEAD, 4 * HEAD), 4 * HEAD)

    def start(source, target, sem):
        copy = pltpu.make_async_copy(source, target, sem)
        copy.start()
        return copy

    numbers = [start(decay_in, decay, sems.at[2, 0]), start(bounds_in, bounds, sems.at[2, 1])]
    sent = pl.ds(pl.multiple_of(first_head(False) * HEAD, 4 * HEAD), 4 * HEAD)
    copies = [start(k_in.at[:, sent], k.at[:, sent], sems.at[0, 0]), start(v_in.at[:, sent], v.at[:, sent], sems.at[1, 0])]
    halves = [start(k_in.at[:, rest], k.at[:, rest], sems.at[2, 2]), start(v_in.at[:, rest], v.at[:, rest], sems.at[2, 3])]
    for copy in numbers:
        copy.wait()
    for head in range(HEADS_DEV):
        table[RATES + head : RATES + head + 1, :] = rate_of(decay[head])
    entering, leaving = tokens_in(bounds, at)
    table[ENTER : ENTER + 1, :] = jnp.full((1, HEAD), entering.astype(F32), F32)
    table[LEAVE : LEAVE + 1, :] = jnp.full((1, HEAD), leaving.astype(F32), F32)
    fill_chain(table, FORWARD, decay, bounds, False)
    for copy in copies:
        copy.wait()
    for i, head in enumerate(heads):
        weights = leave_decay(table, head)
        decayed = (weights * k[:, columns(head)].astype(F32)).astype(BF16)
        out[i * HEAD : (i + 1) * HEAD, :] = mm_at(decayed, v[:, columns(head)])
    for copy in halves:
        copy.wait()


def kept_states_kernel(table, k, v, after, out):
    y = place()[2]
    for i in range(4):
        head = first_head(True) + (y ^ i)
        decayed = (leave_decay(table, head) * k[:, columns(head)].astype(F32)).astype(BF16)
        out[i * HEAD : (i + 1) * HEAD, :] = mm_at(decayed, v[:, columns(head)])


def intra_kernel(table, q, k, v, mask, after, out_ref, *, own):
    half = TOK // 2
    for j in range(4):
        head = first_head(own) + j
        rate, at = rate_row(table, head), columns(head)
        scaled = (powers(-rate, 0.0, True) * k[:, at].astype(F32)).astype(BF16)
        down = powers(rate, 0.0, True)
        for lo in (0, half):
            hi = lo + half
            mixing = mm_bt(q[lo:hi, at], scaled[0:hi, :]).astype(BF16) * mask[lo:hi, 0:hi]
            out_ref[lo:hi, j * HEAD : (j + 1) * HEAD] = down[lo:hi, :] * mm(mixing, v[0:hi, at])


def chip_kernel(table, keep, got, send, after, *outs, base, reverse, gains):
    for k in range(4):
        own, other = base + CHIP_OWN + k, base + CHIP_OTHER + k
        rows = slice(k * HEAD, (k + 1) * HEAD)
        outs[SLOT[k]][0:HEAD, :] = table[own : own + 1, :] * keep[rows, :] + table[other : other + 1, :] * got[rows, :]
        if gains:
            tail = slice(4 * HEAD, 4 * HEAD + 8)
            outs[SLOT[k]][HEAD : HEAD + 8, :] = send[tail, :] + got[tail, :]


def sum_kernel(table, p0, p1, p2, p3, after, out, *, base, reverse, gains):
    total = 0.0
    for k, p in enumerate((p0, p1, p2, p3)):
        total += table[base + k : base + k + 1, :] * p[0:HEAD, :]
    out[0:HEAD, :] = total
    if gains:
        tail = slice(HEAD, HEAD + 8)
        out[tail, :] = p0[tail, :] + p1[tail, :] + p2[tail, :] + p3[tail, :]


def chips_in_kernel(table, r1, r2, r3, far, sent, t0, t1, t2, t3, after, *outs, base, reverse, gains):
    total = table[base + FAR : base + FAR + 1, :] * far[0:HEAD, :]
    for k, r in enumerate((r1, r2, r3)):
        at = base + NEAR + 1 + k
        total += table[at : at + 1, :] * r[0:HEAD, :]
    for k in range(4):
        at = base + INTO + k
        state = table[at : at + 1, :] * total
        for m, t in enumerate((t0, t1, t2, t3)):
            if m != k:
                at = base + ACROSS + 4 * k + m
                state += table[at : at + 1, :] * t[0:HEAD, :]
        outs[SLOT[k]][...] = state
    if gains:
        tail = slice(HEAD, HEAD + 8)
        outs[4][...] = sent[tail, :] + far[tail, :]


def gains_kernel(totals, out):
    _, z, y, c = place()
    turned = pltpu.roll(totals[pl.ds(z, 1), :], (HEAD - 32 * y - 16 * c) % HEAD, axis=1)
    out[...] = turned[0, 0:16]


def cores_in_kernel(table, v0, v1, v2, v3, keep, got, *refs, base, reverse):
    mine, other = refs[-2:]
    c = place()[3]
    deep = c == 0 if reverse else c == 1
    for k, v in enumerate((v0, v1, v2, v3)):
        at = base + CORE + k
        rows = slice(k * HEAD, (k + 1) * HEAD)
        state = v[...]
        step = table[at : at + 1, :] * state
        mine[rows, :] = jnp.where(deep, step + got[rows, :], state)
        other[rows, :] = jnp.where(deep, state, step + keep[rows, :])


def state_of(states, j):
    return states[columns(j ^ place()[2]), :].astype(BF16)


def attended_kernel(table, q, intra, grad, gain, states, *refs, own):
    out_ref, sums = refs[-2:]
    square, cross = 0.0, 0.0
    for j in range(4):
        head = first_head(own) + j
        at, local = columns(head), slice(j * HEAD, (j + 1) * HEAD)
        weights = enter_decay(table, head)
        out = intra[:, local] + weights * mm(q[:, at], state_of(states, j))
        out_ref[:, local] = out
        square += out * out
        cross += out * (grad[:, at].astype(F32) * gain[pl.ds(head, 1), :])
    square = jnp.sum(square.T, axis=0, keepdims=True)
    cross = jnp.sum(cross.T, axis=0, keepdims=True)
    if not own:
        square += refs[0][0:1, :]
        cross += refs[0][4:5, :]
    sums[0:4, :] = jnp.broadcast_to(square, (4, TOK))
    sums[4:8, :] = jnp.broadcast_to(cross, (4, TOK))


def mixed_kernel(table, s0, s1, s2, s3, o, grad, q, gain, *refs, own):
    d, states = refs[-2:]
    y = place()[2]
    sums = s0[...] + s1[...] + s2[...] + s3[...]
    r = lax.rsqrt(sums[0:1, :] * (1.0 / FEATURES) + 1e-06)
    inverse = jnp.broadcast_to(r, (HEAD, TOK)).T
    mean = jnp.broadcast_to(sums[4:5, :] * r * (1.0 / FEATURES), (HEAD, TOK)).T
    tail = 4 * HEAD

    def term(head, wide, normed):
        if not own:
            states[pl.ds(tail + head, 1), :] = jnp.sum(wide * normed, axis=0, keepdims=True)

    for j in range(4):
        head = first_head(own) + j
        local = slice(j * HEAD, (j + 1) * HEAD)
        normed = inverse * o[:, local]
        wide = grad[:, columns(head)].astype(F32)
        low = (inverse * (wide * gain[pl.ds(head, 1), :] - normed * mean)).astype(BF16)
        d[:, local] = low
        term(head, wide, normed)
        weights = enter_decay(table, head)
        states[columns(j ^ y), :] = mm_at((weights * q[:, columns(head)].astype(F32)).astype(BF16), low)
    if not own:
        for j in range(4):
            head = first_head(True) + j
            term(head, grad[:, columns(head)].astype(F32), inverse * refs[0][:, j * HEAD : (j + 1) * HEAD])


def grads_kernel(table, q, k, v, d, mask, flipped, states, after, dq, dk, dv, *, own, start):
    half = TOK // 2
    for n in range(2):
        j = start + n
        head = first_head(own) + j
        rate, at = rate_row(table, head), columns(head)
        out, local = slice(n * HEAD, (n + 1) * HEAD), slice(j * HEAD, (j + 1) * HEAD)
        state = state_of(states, j)
        up, down = powers(-rate, 0.0, True), powers(rate, 0.0, True)
        inside = jnp.where(token_rows() < table[ENTER : ENTER + 1, :], jnp.exp(rate), 0.0)
        v_up = (up * v[:, at].astype(F32)).astype(BF16)
        d_down = (down * d[:, local].astype(F32)).astype(BF16)
        q_down = (down * q[:, at].astype(F32)).astype(BF16)
        for lo in (0, half):
            hi = lo + half
            mixing = mm_bt(d[lo:hi, local], v_up[0:hi, :]).astype(BF16) * mask[lo:hi, 0:hi]
            grad = mm(mixing, k[0:hi, at]) + inside[lo:hi, :] * mm_bt(d[lo:hi, local], state)
            dq[lo:hi, out] = (down[lo:hi, :] * grad).astype(BF16)
            mixing = mm_bt(v[lo:hi, at], d_down[lo:TOK, :]).astype(BF16) * flipped[lo:hi, lo:TOK]
            dk[lo:hi, out] = up[lo:hi, :] * mm(mixing, q[lo:TOK, at])
            mixing = mm_bt(k[lo:hi, at], q_down[lo:TOK, :]).astype(BF16) * flipped[lo:hi, lo:TOK]
            dv[lo:hi, out] = up[lo:hi, :] * mm(mixing, d[lo:TOK, local])


def last_kernel(table, k, v, states, *refs, own):
    parts, buffers = refs[:4], refs[-3:]
    (dk, dv), sems = refs[-5:-3] if not own else refs[-6:-4], buffers[2]
    copies = []
    if own:
        dq = refs[-4]
        for n, part in enumerate(refs[4:8]):
            spot = pl.ds(pl.multiple_of((first_head(n < 2) + 2 * (n % 2)) * HEAD, 2 * HEAD), 2 * HEAD)
            copies.append(pltpu.make_async_copy(part, dq.at[:, spot], sems.at[2, n]))
            copies[-1].start()
    for j in range(4):
        head = first_head(own) + j
        at, local = columns(head), slice(j * HEAD, (j + 1) * HEAD)
        inner = slice(j % 2 * HEAD, (j % 2 + 1) * HEAD)
        weights = leave_decay(table, head)
        state = state_of(states, j)
        buffers[0][:, local] = (parts[j // 2][:, inner] + weights * mm_bt(v[:, at], state)).astype(BF16)
        copies.append(pltpu.make_async_copy(buffers[0].at[:, local], dk.at[:, at], sems.at[0, j]))
        copies[-1].start()
        buffers[1][:, local] = (parts[2 + j // 2][:, inner] + weights * mm(k[:, at], state)).astype(BF16)
        copies.append(pltpu.make_async_copy(buffers[1].at[:, local], dv.at[:, at], sems.at[1, j]))
        copies[-1].start()
    for copy in copies:
        copy.wait()


def index(z, y, c):
    return (z * 4 + y) * 2 + c


def exchange(array, dz=0, dy=0, dc=0):
    pairs = [
        (index(z, y, c), index(z ^ dz, y ^ dy, c ^ dc))
        for z in range(8)
        for y in range(4)
        for c in range(2)
    ]
    return lax.ppermute(array, "seq", pairs)


def carried(send, make_keep, table, base, reverse, gains, work):
    extra = 8 if gains else 0
    small = shape(HEAD + extra, HEAD)

    def step(kernel, outs, *args, after, base=base, **more):
        return call(
            functools.partial(kernel, reverse=reverse, base=base, **more),
            outs,
            in_specs=[VMEM] * (1 + len(args)) + [ANY] * len(after),
            out_specs=jax.tree.map(lambda _: VMEM, outs),
            limit=8,
        )(table, *args, *after)

    def around(arrays, ks, **axis):
        moved = {k: exchange(arrays[k], **{name: k for name in axis}) for k in ks}
        return [arrays[0]] + [moved[k] for k in (1, 2, 3)]

    got = exchange(send, dc=1)
    keep = make_keep(send)
    chips = step(chip_kernel, [small] * 4, keep, got, send, gains=gains, after=[keep])
    done = work[0](chips[0])
    chips = around([chips[n] for n in SLOT], (2, 1, 3), dy=1)
    row = step(sum_kernel, small, *chips, gains=gains, after=[done], base=base + ROW)
    done = work[1](row)
    rows = around([row] * 4, (1, 2, 3), dz=1)
    sent = step(sum_kernel, small, *rows, gains=gains, after=[done], base=base + HALF)
    done = work[2](sent)
    far = exchange(sent, dz=FAR_Z)
    outs = [shape(HEAD, HEAD)] * 4 + ([shape(8, HEAD)] if gains else [])
    outs = step(chips_in_kernel, outs, *rows[1:], far, sent, *chips, gains=gains, after=[done])
    done = work[3](outs[0])
    states = around([outs[n] for n in SLOT], (2, 1, 3), dy=1)
    total = call(gains_kernel, shape(16), in_specs=[VMEM], out_specs=VMEM)(outs[4]) if gains else None
    mine, other = step(cores_in_kernel, [shape(4 * HEAD, HEAD)] * 2, *states, keep, got, after=[done] + [total] * gains)
    return mine, other, total


def shards(queries, keys, values, out_grad, gain, decay, bounds):
    gain = gain.reshape(HEADS_DEV, HEAD)
    width = HEADS_DEV * HEAD
    half = width // 2
    small_mm = TOK * HEAD * HEAD * HEADS_DEV
    big_mm = 2 * TOK * TOK * HEAD * HEADS_DEV * 3 // 4
    state_shape = shape(4 * HEAD, HEAD)

    def local(kernel, outs, args, order=(), flops=0, moved=0, **more):
        return call(
            functools.partial(kernel, **more),
            outs,
            in_specs=[VMEM] * (1 + len(args)) + [ANY] * len(order),
            out_specs=jax.tree.map(lambda _: VMEM, outs),
            flops=flops,
            moved=moved,
        )(table, *args, *order)

    wide = shape(TOK, width, dtype=BF16)
    send, table, keys, values = call(
        sent_states_kernel,
        [state_shape, shape(FORWARD + CHAIN_ROWS, HEAD), wide, wide],
        in_specs=[ANY] * 4,
        out_specs=[VMEM] * 4,
        scratch=[pltpu.SMEM((HEADS_DEV,), jnp.int32), pltpu.SMEM((3,), jnp.int32), pltpu.SemaphoreType.DMA((3, 4))],
        flops=small_mm,
        moved=3 << 19,
    )(*[pltpu.with_memory_space_constraint(x, pltpu.HBM) for x in (decay, bounds, keys, values)])

    def keep_states(after):
        return local(kept_states_kernel, state_shape, [keys, values], [after], small_mm, 3 << 19)

    made = {}
    pairs = shape(TOK, TOK, dtype=BF16)

    def make_intra(own):
        def run(after):
            if own:
                outs = [pairs] * 2 + [shape(CHAIN_ROWS, HEAD), shape(HEADS_DEV, HEAD)]
                made["masks"] = call(
                    masks_kernel,
                    outs,
                    in_specs=[SMEM, SMEM, VMEM, ANY],
                    out_specs=[VMEM] * 4,
                    moved=1 << 20,
                )(*[pltpu.with_memory_space_constraint(x, pltpu.HBM) for x in (decay, bounds)], gain, after)
            made[own] = local(
                intra_kernel,
                shape(TOK, half),
                [queries, keys, values, made["masks"][0]],
                [after],
                big_mm,
                3 << 20,
                own=own,
            )
            return made[own]

        return run

    def same(after):
        return after

    mine, other, _ = carried(
        send, keep_states, table, FORWARD, False, False, [make_intra(True), make_intra(False), same, same]
    )
    theirs = exchange(other, dc=1)
    mask, flipped, back_table, gain = made["masks"]
    sums = shape(8, TOK)
    outs = [shape(TOK, half), sums]
    o_mine, own_sums = local(
        attended_kernel, outs, [queries, made[True], out_grad, gain, mine], [other], small_mm, 3 << 20, own=True
    )
    o_other, sums = local(
        attended_kernel,
        outs,
        [queries, made[False], out_grad, gain, theirs, own_sums],
        [],
        small_mm,
        3 << 20,
        own=False,
    )
    totals = [sums] + [lax.ppermute(sums, "dp", [(i, i ^ k) for i in range(4)]) for k in (1, 2, 3)]
    outs = [shape(TOK, half, dtype=BF16), shape(4 * HEAD + 8, HEAD)]
    d_other, send = local(
        mixed_kernel,
        outs,
        [*totals, o_other, out_grad, queries, gain, o_mine],
        [],
        small_mm,
        3 << 20,
        own=False,
    )

    def keep_grads(after):
        outs = [shape(TOK, half, dtype=BF16), shape(4 * HEAD, HEAD)]
        made["d"], keep = local(
            mixed_kernel, outs, [*totals, o_mine, out_grad, queries, gain], [after], small_mm, 3 << 20, own=True
        )
        return keep


    def make_grads(n):
        def run(after):
            own = n < 2
            made["grads", n] = local(
                grads_kernel,
                [shape(TOK, 2 * HEAD, dtype=BF16), shape(TOK, 2 * HEAD), shape(TOK, 2 * HEAD)],
                [queries, keys, values, made["d"] if own else d_other, mask, flipped, mine if own else theirs],
                [after],
                6 * big_mm // 4,
                2 << 20,
                own=own,
                start=2 * (n % 2),
            )
            return made["grads", n][1]

        return run

    last_mine, last_other, gains = carried(
        send, keep_grads, back_table, BACKWARD, True, True, [make_grads(n) for n in range(4)]
    )
    last_theirs = exchange(last_other, dc=1)
    dq, dk, dv = zip(*[made["grads", n] for n in range(4)])
    full = shape(TOK, width, dtype=BF16)
    scratch = [pltpu.VMEM((TOK, half), BF16)] * 2 + [pltpu.SemaphoreType.DMA((3, 4))]
    dk_out, dv_out, dq_out = call(
        functools.partial(last_kernel, own=True),
        [full] * 3,
        in_specs=[VMEM] * 12 + [ANY],
        out_specs=[ANY] * 3,
        scratch=scratch,
        flops=2 * small_mm,
        moved=6 << 20,
    )(table, keys, values, last_mine, *dk[:2], *dv[:2], *dq, last_other)
    dk_out, dv_out = call(
        functools.partial(last_kernel, own=False),
        [full] * 2,
        in_specs=[VMEM] * 8 + [ANY] * 2,
        out_specs=[ANY] * 2,
        scratch=scratch,
        flops=2 * small_mm,
        moved=4 << 20,
        aliases={8: 0, 9: 1},
    )(table, keys, values, last_theirs, *dk[2:], *dv[2:], dk_out, dv_out)
    return dq_out, dk_out, dv_out, gains


def solution(mesh):
    return jax.shard_map(
        shards,
        mesh=mesh,
        in_specs=(
            P("seq", "dp"),
            P("seq", "dp"),
            P("seq", "dp"),
            P("seq", "dp"),
            P("dp"),
            P("dp"),
            P(),
        ),
        out_specs=(P("seq", "dp"), P("seq", "dp"), P("seq", "dp"), P(("dp", "seq"))),
        check_vma=False,
    )
```

```python
import functools
import math

import jax
import jax.numpy as jnp
from jax import lax
from jax.experimental import pallas as pl
from jax.experimental.pallas import tpu as pltpu
from jax.sharding import PartitionSpec as P

F32, BF16 = jnp.float32, jnp.bfloat16
HEAD, TOK, HEADS_DEV, STREAM, FEATURES = 128, 512, 8, 32768, 4096
BLOCK_Z, BLOCK_Y = 8 * TOK, 2 * TOK
SMEM = pl.BlockSpec(memory_space=pltpu.SMEM)
VMEM = pl.BlockSpec(memory_space=pltpu.VMEM)
ANY = pl.BlockSpec(memory_space=pl.ANY)


def rate_of(level):
    row = jnp.full((1, HEAD), level.astype(F32), F32)
    slow = jnp.exp(row * (math.log(8.0) / 7.0)) * (-0.25 / STREAM)
    lowest = math.log(4.0 / STREAM)
    fast = -jnp.exp(lowest + (row - 8.0) * ((math.log(1.0 / 32.0) - lowest) / 7.0))
    return jnp.where(row < 8.0, slow, fast)


def starts_before(bounds, place):
    return sum((bounds[i] < place).astype(jnp.int32) for i in range(3))


def carry(rate, bounds, left, right):
    same = (starts_before(bounds, left) == starts_before(bounds, right)) & (left <= right)
    span = jnp.maximum(right - left, 0).astype(F32)
    return jnp.exp(rate * span) * jnp.where(same, 1.0, 0.0).astype(F32)


def place():
    at = lax.axis_index("seq")
    return at, at // 8, (at // 2) % 4, at % 2


def tokens_in(bounds, at):
    first = at * TOK
    entering, leaving = TOK, 0
    for i in range(3):
        local = bounds[i] - first
        entering = jnp.where((local >= 0) & (local < entering), local, entering)
        leaving = jnp.where((local < TOK) & (local > leaving), local, leaving)
    return entering, leaving


def powers(rate, first, up):
    t = lax.broadcasted_iota(jnp.int32, (8, HEAD), 0)
    t = (t if up else 7 - t).astype(F32)
    rows, size = jnp.exp(rate * (t + first)), 8
    while size < TOK:
        more = rows * jnp.exp(rate * float(size))
        rows = jnp.concatenate([rows, more] if up else [more, rows], axis=0)
        size *= 2
    return rows


RATES, ENTER, LEAVE, FORWARD, BACKWARD = 0, 8, 9, 16, 0
CHIP_OWN, CHIP_OTHER, ROW, HALF, FAR, NEAR, INTO, ACROSS, CORE = 0, 4, 8, 12, 16, 16, 20, 24, 40
CHAIN_ROWS = 48
FAR_Z = 6
SLOT = (0, 2, 1, 3)


def token_rows():
    return lax.broadcasted_iota(jnp.int32, (TOK, HEAD), 0).astype(F32)


def rate_row(table, head):
    return table[pl.ds(head, 1), :]


def enter_decay(table, head):
    return jnp.where(token_rows() < table[ENTER : ENTER + 1, :], powers(rate_row(table, head), 1.0, True), 0.0)


def leave_decay(table, head):
    return jnp.where(token_rows() >= table[LEAVE : LEAVE + 1, :], powers(rate_row(table, head), 0.0, False), 0.0)


def fill_chain(table, base, decay, bounds, reverse):
    at, z, y, c = place()
    one = jnp.ones((1, HEAD), F32)
    middle = (at - c + 1) * TOK
    row, row_end, centre = z * BLOCK_Z, (z + 1) * BLOCK_Z, 4 * BLOCK_Z

    def put(index, value):
        table[base + index : base + index + 1, :] = value

    def across(rate, earlier, later):
        return carry(rate, bounds, earlier, later)

    for k in range(4):
        rate = rate_of(decay[4 * c + (y ^ k)])
        first, second = across(rate, middle - TOK, middle), across(rate, middle, middle + TOK)
        if reverse:
            put(CHIP_OWN + k, jnp.where(c == 1, first, one))
            put(CHIP_OTHER + k, jnp.where(c == 1, one, first))
            put(CORE + k, second)
        else:
            put(CHIP_OWN + k, jnp.where(c == 0, second, one))
            put(CHIP_OTHER + k, jnp.where(c == 0, one, second))
            put(CORE + k, first)
    rate = rate_of(decay[4 * c + y])
    for k in range(4):
        here, line = row + (y ^ k) * BLOCK_Y, (z ^ k) * BLOCK_Z
        if reverse:
            put(ROW + k, across(rate, row, here))
            put(HALF + k, across(rate, centre, line))
            put(NEAR + k, across(rate, row_end, line if k else centre))
            put(INTO + k, across(rate, here + BLOCK_Y, row_end))
        else:
            put(ROW + k, across(rate, here + BLOCK_Y, row_end))
            put(HALF + k, across(rate, line + BLOCK_Z, centre))
            put(NEAR + k, across(rate, line + BLOCK_Z if k else centre, row))
            put(INTO + k, across(rate, row, here))
        for m in range(4):
            if m != k:
                there = row + (y ^ m) * BLOCK_Y
                if reverse:
                    put(ACROSS + 4 * k + m, across(rate, here + BLOCK_Y, there))
                else:
                    put(ACROSS + 4 * k + m, across(rate, there + BLOCK_Y, here))


def masks_kernel(decay, bounds, gain, after, mask, flipped, table, gain_out):
    gain_out[...] = gain[...]
    fill_chain(table, BACKWARD, decay, bounds, True)
    first = place()[0] * TOK
    for lo in range(0, TOK, HEAD):
        row = lax.broadcasted_iota(jnp.int32, (HEAD, TOK), 0) + lo
        column = lax.broadcasted_iota(jnp.int32, (HEAD, TOK), 1)
        since = jnp.zeros((HEAD, TOK), jnp.int32)
        until = jnp.full((HEAD, TOK), TOK, jnp.int32)
        for i in range(3):
            local = bounds[i] - first
            since = jnp.where(row >= local, jnp.maximum(since, local), since)
            until = jnp.where(row < local, jnp.minimum(until, local), until)
        rows = slice(lo, lo + HEAD)
        mask[rows, :] = jnp.where((column <= row) & (column >= since), 1.0, 0.0).astype(BF16)
        flipped[rows, :] = jnp.where((column >= row) & (column < until), 1.0, 0.0).astype(BF16)


def mm(a, b):
    return lax.dot_general(a, b, (((1,), (0,)), ((), ())), preferred_element_type=F32)


def mm_bt(a, b):
    return lax.dot_general(a, b, (((1,), (1,)), ((), ())), preferred_element_type=F32)


def mm_at(a, b):
    return lax.dot_general(a, b, (((0,), (0,)), ((), ())), preferred_element_type=F32)


def call(kernel, outs, grid=None, in_specs=None, out_specs=None, scratch=(), flops=0, moved=0, limit=24, aliases={}):
    extra = {} if grid is None else {"grid": grid}
    return pl.pallas_call(
        kernel,
        out_shape=outs,
        in_specs=in_specs,
        out_specs=out_specs,
        scratch_shapes=list(scratch),
        input_output_aliases=aliases,
        compiler_params=pltpu.CompilerParams(vmem_limit_bytes=limit << 20),
        cost_estimate=pl.CostEstimate(flops=flops, bytes_accessed=moved, transcendentals=0),
        **extra,
    )


def shape(*dims, dtype=F32):
    return jax.ShapeDtypeStruct(dims, dtype)


def columns(index):
    return pl.ds(pl.multiple_of(index * HEAD, HEAD), HEAD)


def first_head(own):
    c = place()[3]
    return 4 * c if own else 4 * (1 - c)


def sent_states_kernel(decay_in, bounds_in, k_in, v_in, out, table, k, v, decay, bounds, sems):
    at, _, y, _ = place()
    heads = [first_head(False) + (y ^ i) for i in range(4)]
    rest = pl.ds(pl.multiple_of(first_head(True) * HEAD, 4 * HEAD), 4 * HEAD)

    def start(source, target, sem):
        copy = pltpu.make_async_copy(source, target, sem)
        copy.start()
        return copy

    numbers = [start(decay_in, decay, sems.at[2, 0]), start(bounds_in, bounds, sems.at[2, 1])]
    sent = pl.ds(pl.multiple_of(first_head(False) * HEAD, 4 * HEAD), 4 * HEAD)
    copies = [start(k_in.at[:, sent], k.at[:, sent], sems.at[0, 0]), start(v_in.at[:, sent], v.at[:, sent], sems.at[1, 0])]
    halves = [start(k_in.at[:, rest], k.at[:, rest], sems.at[2, 2]), start(v_in.at[:, rest], v.at[:, rest], sems.at[2, 3])]
    for copy in numbers:
        copy.wait()
    for head in range(HEADS_DEV):
        table[RATES + head : RATES + head + 1, :] = rate_of(decay[head])
    entering, leaving = tokens_in(bounds, at)
    table[ENTER : ENTER + 1, :] = jnp.full((1, HEAD), entering.astype(F32), F32)
    table[LEAVE : LEAVE + 1, :] = jnp.full((1, HEAD), leaving.astype(F32), F32)
    fill_chain(table, FORWARD, decay, bounds, False)
    for copy in copies:
        copy.wait()
    for i, head in enumerate(heads):
        weights = leave_decay(table, head)
        decayed = (weights * k[:, columns(head)].astype(F32)).astype(BF16)
        out[i * HEAD : (i + 1) * HEAD, :] = mm_at(decayed, v[:, columns(head)])
    for copy in halves:
        copy.wait()


def kept_states_kernel(table, k, v, after, out):
    y = place()[2]
    for i in range(4):
        head = first_head(True) + (y ^ i)
        decayed = (leave_decay(table, head) * k[:, columns(head)].astype(F32)).astype(BF16)
        out[i * HEAD : (i + 1) * HEAD, :] = mm_at(decayed, v[:, columns(head)])


def intra_kernel(table, q, k, v, mask, after, out_ref, *, own):
    half = TOK // 2
    for j in range(4):
        head = first_head(own) + j
        rate, at = rate_row(table, head), columns(head)
        scaled = (powers(-rate, 0.0, True) * k[:, at].astype(F32)).astype(BF16)
        down = powers(rate, 0.0, True)
        for lo in (0, half):
            hi = lo + half
            mixing = mm_bt(q[lo:hi, at], scaled[0:hi, :]).astype(BF16) * mask[lo:hi, 0:hi]
            out_ref[lo:hi, j * HEAD : (j + 1) * HEAD] = down[lo:hi, :] * mm(mixing, v[0:hi, at])


def chip_kernel(table, keep, got, send, after, *outs, base, reverse, gains):
    for k in range(4):
        own, other = base + CHIP_OWN + k, base + CHIP_OTHER + k
        rows = slice(k * HEAD, (k + 1) * HEAD)
        outs[SLOT[k]][0:HEAD, :] = table[own : own + 1, :] * keep[rows, :] + table[other : other + 1, :] * got[rows, :]
        if gains:
            tail = slice(4 * HEAD, 4 * HEAD + 8)
            outs[SLOT[k]][HEAD : HEAD + 8, :] = send[tail, :] + got[tail, :]


def sum_kernel(table, p0, p1, p2, p3, after, out, *, base, reverse, gains):
    total = 0.0
    for k, p in enumerate((p0, p1, p2, p3)):
        total += table[base + k : base + k + 1, :] * p[0:HEAD, :]
    out[0:HEAD, :] = total
    if gains:
        tail = slice(HEAD, HEAD + 8)
        out[tail, :] = p0[tail, :] + p1[tail, :] + p2[tail, :] + p3[tail, :]


def chips_in_kernel(table, r1, r2, r3, far, sent, t0, t1, t2, t3, after, *outs, base, reverse, gains):
    total = table[base + FAR : base + FAR + 1, :] * far[0:HEAD, :]
    for k, r in enumerate((r1, r2, r3)):
        at = base + NEAR + 1 + k
        total += table[at : at + 1, :] * r[0:HEAD, :]
    for k in range(4):
        at = base + INTO + k
        state = table[at : at + 1, :] * total
        for m, t in enumerate((t0, t1, t2, t3)):
            if m != k:
                at = base + ACROSS + 4 * k + m
                state += table[at : at + 1, :] * t[0:HEAD, :]
        outs[SLOT[k]][...] = state
    if gains:
        tail = slice(HEAD, HEAD + 8)
        outs[4][...] = sent[tail, :] + far[tail, :]


def gains_kernel(totals, out):
    _, z, y, c = place()
    turned = pltpu.roll(totals[pl.ds(z, 1), :], (HEAD - 32 * y - 16 * c) % HEAD, axis=1)
    out[...] = turned[0, 0:16]


def cores_in_kernel(table, v0, v1, v2, v3, keep, got, *refs, base, reverse):
    mine, other = refs[-2:]
    c = place()[3]
    deep = c == 0 if reverse else c == 1
    for k, v in enumerate((v0, v1, v2, v3)):
        at = base + CORE + k
        rows = slice(k * HEAD, (k + 1) * HEAD)
        state = v[...]
        step = table[at : at + 1, :] * state
        mine[rows, :] = jnp.where(deep, step + got[rows, :], state)
        other[rows, :] = jnp.where(deep, state, step + keep[rows, :])


def state_of(states, j):
    return states[columns(j ^ place()[2]), :].astype(BF16)


def attended_kernel(table, q, intra, grad, gain, states, *refs, own):
    out_ref, sums = refs[-2:]
    square, cross = 0.0, 0.0
    for j in range(4):
        head = first_head(own) + j
        at, local = columns(head), slice(j * HEAD, (j + 1) * HEAD)
        weights = enter_decay(table, head)
        out = intra[:, local] + weights * mm(q[:, at], state_of(states, j))
        out_ref[:, local] = out
        square += out * out
        cross += out * (grad[:, at].astype(F32) * gain[pl.ds(head, 1), :])
    square = jnp.sum(square.T, axis=0, keepdims=True)
    cross = jnp.sum(cross.T, axis=0, keepdims=True)
    if not own:
        square += refs[0][0:1, :]
        cross += refs[0][1:2, :]
    sums[0:1, :] = square
    sums[1:2, :] = cross


def mixed_kernel(table, s0, s1, s2, s3, o, grad, q, gain, *refs, own):
    d, states = refs[-2:]
    y = place()[2]
    sums = s0[...] + s1[...] + s2[...] + s3[...]
    r = lax.rsqrt(sums[0:1, :] * (1.0 / FEATURES) + 1e-06)
    inverse = jnp.broadcast_to(r, (HEAD, TOK)).T
    mean = jnp.broadcast_to(sums[1:2, :] * r * (1.0 / FEATURES), (HEAD, TOK)).T
    tail = 4 * HEAD

    def term(head, wide, normed):
        if not own:
            states[pl.ds(tail + head, 1), :] = jnp.sum(wide * normed, axis=0, keepdims=True)

    for j in range(4):
        head = first_head(own) + j
        local = slice(j * HEAD, (j + 1) * HEAD)
        normed = inverse * o[:, local]
        wide = grad[:, columns(head)].astype(F32)
        low = (inverse * (wide * gain[pl.ds(head, 1), :] - normed * mean)).astype(BF16)
        d[:, local] = low
        term(head, wide, normed)
        weights = enter_decay(table, head)
        states[columns(j ^ y), :] = mm_at((weights * q[:, columns(head)].astype(F32)).astype(BF16), low)
    if not own:
        for j in range(4):
            head = first_head(True) + j
            term(head, grad[:, columns(head)].astype(F32), inverse * refs[0][:, j * HEAD : (j + 1) * HEAD])


def grads_kernel(table, q, k, v, d, mask, flipped, states, after, dq, dk, dv, *, own, start):
    half = TOK // 2
    for n in range(2):
        j = start + n
        head = first_head(own) + j
        rate, at = rate_row(table, head), columns(head)
        out, local = slice(n * HEAD, (n + 1) * HEAD), slice(j * HEAD, (j + 1) * HEAD)
        state = state_of(states, j)
        up, down = powers(-rate, 0.0, True), powers(rate, 0.0, True)
        inside = jnp.where(token_rows() < table[ENTER : ENTER + 1, :], jnp.exp(rate), 0.0)
        v_up = (up * v[:, at].astype(F32)).astype(BF16)
        d_down = (down * d[:, local].astype(F32)).astype(BF16)
        q_down = (down * q[:, at].astype(F32)).astype(BF16)
        for lo in (0, half):
            hi = lo + half
            mixing = mm_bt(d[lo:hi, local], v_up[0:hi, :]).astype(BF16) * mask[lo:hi, 0:hi]
            grad = mm(mixing, k[0:hi, at]) + inside[lo:hi, :] * mm_bt(d[lo:hi, local], state)
            dq[lo:hi, out] = (down[lo:hi, :] * grad).astype(BF16)
            mixing = mm_bt(v[lo:hi, at], d_down[lo:TOK, :]).astype(BF16) * flipped[lo:hi, lo:TOK]
            dk[lo:hi, out] = up[lo:hi, :] * mm(mixing, q[lo:TOK, at])
            mixing = mm_bt(k[lo:hi, at], q_down[lo:TOK, :]).astype(BF16) * flipped[lo:hi, lo:TOK]
            dv[lo:hi, out] = up[lo:hi, :] * mm(mixing, d[lo:TOK, local])


def last_kernel(table, k, v, states, *refs, own):
    parts, buffers = refs[:4], refs[-3:]
    (dk, dv), sems = refs[-5:-3] if not own else refs[-6:-4], buffers[2]
    copies = []
    if own:
        dq = refs[-4]
        for n, part in enumerate(refs[4:8]):
            spot = pl.ds(pl.multiple_of((first_head(n < 2) + 2 * (n % 2)) * HEAD, 2 * HEAD), 2 * HEAD)
            copies.append(pltpu.make_async_copy(part, dq.at[:, spot], sems.at[2, n]))
            copies[-1].start()
    for j in range(4):
        head = first_head(own) + j
        at, local = columns(head), slice(j * HEAD, (j + 1) * HEAD)
        inner = slice(j % 2 * HEAD, (j % 2 + 1) * HEAD)
        weights = leave_decay(table, head)
        state = state_of(states, j)
        buffers[0][:, local] = (parts[j // 2][:, inner] + weights * mm_bt(v[:, at], state)).astype(BF16)
        copies.append(pltpu.make_async_copy(buffers[0].at[:, local], dk.at[:, at], sems.at[0, j]))
        copies[-1].start()
        buffers[1][:, local] = (parts[2 + j // 2][:, inner] + weights * mm(k[:, at], state)).astype(BF16)
        copies.append(pltpu.make_async_copy(buffers[1].at[:, local], dv.at[:, at], sems.at[1, j]))
        copies[-1].start()
    for copy in copies:
        copy.wait()


def index(z, y, c):
    return (z * 4 + y) * 2 + c


def exchange(array, dz=0, dy=0, dc=0):
    pairs = [
        (index(z, y, c), index(z ^ dz, y ^ dy, c ^ dc))
        for z in range(8)
        for y in range(4)
        for c in range(2)
    ]
    return lax.ppermute(array, "seq", pairs)


def carried(send, make_keep, table, base, reverse, gains, work):
    extra = 8 if gains else 0
    small = shape(HEAD + extra, HEAD)

    def step(kernel, outs, *args, after, base=base, **more):
        return call(
            functools.partial(kernel, reverse=reverse, base=base, **more),
            outs,
            in_specs=[VMEM] * (1 + len(args)) + [ANY] * len(after),
            out_specs=jax.tree.map(lambda _: VMEM, outs),
            limit=8,
        )(table, *args, *after)

    def around(arrays, ks, **axis):
        moved = {k: exchange(arrays[k], **{name: k for name in axis}) for k in ks}
        return [arrays[0]] + [moved[k] for k in (1, 2, 3)]

    got = exchange(send, dc=1)
    keep = make_keep(send)
    chips = step(chip_kernel, [small] * 4, keep, got, send, gains=gains, after=[keep])
    done = work[0](chips[0])
    chips = around([chips[n] for n in SLOT], (2, 1, 3), dy=1)
    row = step(sum_kernel, small, *chips, gains=gains, after=[done], base=base + ROW)
    done = work[1](row)
    rows = around([row] * 4, (1, 2, 3), dz=1)
    sent = step(sum_kernel, small, *rows, gains=gains, after=[done], base=base + HALF)
    done = work[2](sent)
    far = exchange(sent, dz=FAR_Z)
    outs = [shape(HEAD, HEAD)] * 4 + ([shape(8, HEAD)] if gains else [])
    outs = step(chips_in_kernel, outs, *rows[1:], far, sent, *chips, gains=gains, after=[done])
    done = work[3](outs[0])
    states = around([outs[n] for n in SLOT], (2, 1, 3), dy=1)
    total = call(gains_kernel, shape(16), in_specs=[VMEM], out_specs=VMEM)(outs[4]) if gains else None
    mine, other = step(cores_in_kernel, [shape(4 * HEAD, HEAD)] * 2, *states, keep, got, after=[done] + [total] * gains)
    return mine, other, total


def shards(queries, keys, values, out_grad, gain, decay, bounds):
    gain = gain.reshape(HEADS_DEV, HEAD)
    width = HEADS_DEV * HEAD
    half = width // 2
    small_mm = TOK * HEAD * HEAD * HEADS_DEV
    big_mm = 2 * TOK * TOK * HEAD * HEADS_DEV * 3 // 4
    state_shape = shape(4 * HEAD, HEAD)

    def local(kernel, outs, args, order=(), flops=0, moved=0, **more):
        return call(
            functools.partial(kernel, **more),
            outs,
            in_specs=[VMEM] * (1 + len(args)) + [ANY] * len(order),
            out_specs=jax.tree.map(lambda _: VMEM, outs),
            flops=flops,
            moved=moved,
        )(table, *args, *order)

    wide = shape(TOK, width, dtype=BF16)
    send, table, keys, values = call(
        sent_states_kernel,
        [state_shape, shape(FORWARD + CHAIN_ROWS, HEAD), wide, wide],
        in_specs=[ANY] * 4,
        out_specs=[VMEM] * 4,
        scratch=[pltpu.SMEM((HEADS_DEV,), jnp.int32), pltpu.SMEM((3,), jnp.int32), pltpu.SemaphoreType.DMA((3, 4))],
        flops=small_mm,
        moved=3 << 19,
    )(*[pltpu.with_memory_space_constraint(x, pltpu.HBM) for x in (decay, bounds, keys, values)])

    def keep_states(after):
        return local(kept_states_kernel, state_shape, [keys, values], [after], small_mm, 3 << 19)

    made = {}
    pairs = shape(TOK, TOK, dtype=BF16)

    def make_intra(own):
        def run(after):
            if own:
                outs = [pairs] * 2 + [shape(CHAIN_ROWS, HEAD), shape(HEADS_DEV, HEAD)]
                made["masks"] = call(
                    masks_kernel,
                    outs,
                    in_specs=[SMEM, SMEM, VMEM, ANY],
                    out_specs=[VMEM] * 4,
                    moved=1 << 20,
                )(*[pltpu.with_memory_space_constraint(x, pltpu.HBM) for x in (decay, bounds)], gain, after)
            made[own] = local(
                intra_kernel,
                shape(TOK, half),
                [queries, keys, values, made["masks"][0]],
                [after],
                big_mm,
                3 << 20,
                own=own,
            )
            return made[own]

        return run

    def same(after):
        return after

    mine, other, _ = carried(
        send, keep_states, table, FORWARD, False, False, [make_intra(True), make_intra(False), same, same]
    )
    theirs = exchange(other, dc=1)
    mask, flipped, back_table, gain = made["masks"]
    sums = shape(2, TOK)
    outs = [shape(TOK, half), sums]
    o_mine, own_sums = local(
        attended_kernel, outs, [queries, made[True], out_grad, gain, mine], [other], small_mm, 3 << 20, own=True
    )
    o_other, sums = local(
        attended_kernel,
        outs,
        [queries, made[False], out_grad, gain, theirs, own_sums],
        [],
        small_mm,
        3 << 20,
        own=False,
    )
    totals = [sums] + [lax.ppermute(sums, "dp", [(i, i ^ k) for i in range(4)]) for k in (1, 2, 3)]
    outs = [shape(TOK, half, dtype=BF16), shape(4 * HEAD + 8, HEAD)]
    d_other, send = local(
        mixed_kernel,
        outs,
        [*totals, o_other, out_grad, queries, gain, o_mine],
        [],
        small_mm,
        3 << 20,
        own=False,
    )

    def keep_grads(after):
        outs = [shape(TOK, half, dtype=BF16), shape(4 * HEAD, HEAD)]
        made["d"], keep = local(
            mixed_kernel, outs, [*totals, o_mine, out_grad, queries, gain], [after], small_mm, 3 << 20, own=True
        )
        return keep


    def make_grads(n):
        def run(after):
            own = n < 2
            made["grads", n] = local(
                grads_kernel,
                [shape(TOK, 2 * HEAD, dtype=BF16), shape(TOK, 2 * HEAD), shape(TOK, 2 * HEAD)],
                [queries, keys, values, made["d"] if own else d_other, mask, flipped, mine if own else theirs],
                [after],
                6 * big_mm // 4,
                2 << 20,
                own=own,
                start=2 * (n % 2),
            )
            return made["grads", n][1]

        return run

    last_mine, last_other, gains = carried(
        send, keep_grads, back_table, BACKWARD, True, True, [make_grads(n) for n in range(4)]
    )
    last_theirs = exchange(last_other, dc=1)
    dq, dk, dv = zip(*[made["grads", n] for n in range(4)])
    full = shape(TOK, width, dtype=BF16)
    scratch = [pltpu.VMEM((TOK, half), BF16)] * 2 + [pltpu.SemaphoreType.DMA((3, 4))]
    dk_out, dv_out, dq_out = call(
        functools.partial(last_kernel, own=True),
        [full] * 3,
        in_specs=[VMEM] * 12 + [ANY],
        out_specs=[ANY] * 3,
        scratch=scratch,
        flops=2 * small_mm,
        moved=6 << 20,
    )(table, keys, values, last_mine, *dk[:2], *dv[:2], *dq, last_other)
    dk_out, dv_out = call(
        functools.partial(last_kernel, own=False),
        [full] * 2,
        in_specs=[VMEM] * 8 + [ANY] * 2,
        out_specs=[ANY] * 2,
        scratch=scratch,
        flops=2 * small_mm,
        moved=4 << 20,
        aliases={8: 0, 9: 1},
    )(table, keys, values, last_theirs, *dk[2:], *dv[2:], dk_out, dv_out)
    return dq_out, dk_out, dv_out, gains


def solution(mesh):
    return jax.shard_map(
        shards,
        mesh=mesh,
        in_specs=(
            P("seq", "dp"),
            P("seq", "dp"),
            P("seq", "dp"),
            P("seq", "dp"),
            P("dp"),
            P("dp"),
            P(),
        ),
        out_specs=(P("seq", "dp"), P("seq", "dp"), P("seq", "dp"), P(("dp", "seq"))),
        check_vma=False,
    )
```
